32 devices in a mesh: space: 16 (over z, y, core), traj: 2 (over x).
Axes of the slice: x: 2, y: 2, z: 4, core: 2. Of those that a mesh axis runs over, the one named last changes fastest.
Arguments:
- field: float32 [2, 39, 128, 256], P('traj', None, 'space'), may hold values from -6 to 6
- solid: int32 [2, 128, 256], P('traj', 'space'), may hold values 0 or 1
- cotangent: float32 [2, 39, 128, 256], P('traj', None, 'space'), may hold values from -6 to 6
- w_in: bfloat16 [20, 512], replicated, may hold values from -1.25 to 1.25
- b_in: float32 [512], replicated, may hold values from -3 to 3
- w_out: bfloat16 [512, 39], replicated, may hold values from -0.25 to 0.25
- b_out: float32 [39], replicated, may hold values from -3 to 3
Outputs:
- d_field: float32 [2, 39, 128, 256], P('traj', None, 'space')
- g_w_in: float32 [20, 512], replicated
- g_b_in: float32 [512], replicated
- g_w_out: float32 [512, 39], replicated
- g_b_out: float32 [39], replicated
The draws below stay inside these ranges and needn't reach their ends.
All inputs are finite; a program needn't handle non-finite values. No bound on the sum of `solid` on one device may be relied on, other than what follows from the above.
Results may differ from the reference program's by a relative error of at most 0.0089.
Values sent between devices are 32-bit elements; how exact they have to be, the bound alone decides.
No kernel may reach another device: no remote copies, remote signals or barrier semaphores. Data moves between devices by JAX's collectives and lax.ppermute only.
A program may use at most 64 MiB of HBM per device.

```python
import math
import jax
import jax.numpy as jnp
from jax import lax

Q = 39
MOM = 20
HID = 512
STEPS = 3
NX = 16
NY = 16
CZ = 8
PLANE = 256
NZ = 128
TRAJ = 2


def with_ends(drawn, rng, least, top_value):
    longest = drawn.shape.index(max(drawn.shape))
    spots = []
    for shift in (0, 1):
        where = [jax.random.randint(jax.random.fold_in(rng, axis), (), 0, length) for axis, length in enumerate(drawn.shape)]
        where[longest] = (where[longest] + shift) % drawn.shape[longest]
        spots.append(tuple(where))
    return drawn.at[spots[0]].set(least).at[spots[1]].set(top_value)


def levels(rng, dims, split, low, high):
    factor_of = 1.0
    for position, parts in split:
        heights = jax.random.uniform(jax.random.fold_in(jax.random.fold_in(rng, 6), position), (parts,), jnp.float32, low / len(split), high / len(split))
        factor_of = factor_of * jnp.repeat(jnp.exp(heights), dims[position] // parts).reshape((-1,) + (1,) * (len(dims) - 1 - position))
    return factor_of


def noise(key, shape, deviation, most, shards=(), kind=jnp.bfloat16):
    array = jax.random.normal(key, shape, jnp.float32) * deviation
    if len(shards) > 0:
        array = levels(key, shape, shards, -0.22, 0.18) * array
    return jnp.clip(array, min=-most, max=most).astype(kind)


def setup_inputs(seed: int = 0) -> dict:
    seeds = jax.random.split(jax.random.key(seed), 8)
    field = noise(seeds[0], (TRAJ, Q, NZ, PLANE), 1.0, 6.0, ((0, 2), (2, 16)), jnp.float32)
    solid = with_ends((jax.random.randint(seeds[1], (TRAJ, NZ, PLANE), 0, 8) < 1).astype(jnp.int32), jax.random.fold_in(seeds[1], 1), 0, 1)
    cotangent = noise(seeds[2], (TRAJ, Q, NZ, PLANE), 1.0, 6.0, ((0, 2), (2, 16)), jnp.float32)
    w_in = noise(seeds[3], (MOM, HID), MOM ** -0.5, 1.25)
    b_in = noise(seeds[4], (HID,), 0.5, 3.0, (), jnp.float32)
    w_out = noise(seeds[5], (HID, Q), HID ** -0.5, 0.25)
    b_out = noise(seeds[6], (Q,), 0.5, 3.0, (), jnp.float32)
    return {"field": field, "solid": solid, "cotangent": cotangent, "w_in": w_in, "b_in": b_in, "w_out": w_out, "b_out": b_out}


def velocity_table():
    rows = [(0, 0, 0)]
    for axis_one in range(3):
        for sign in (1, -1):
            entry = [0, 0, 0]
            entry[axis_one] = sign
            rows.append(tuple(entry))
    for along_x in (1, -1):
        for along_y in (1, -1):
            for along_z in (1, -1):
                rows.append((along_x, along_y, along_z))
    for axis_one in range(3):
        for sign in (1, -1):
            entry = [0, 0, 0]
            entry[axis_one] = 2 * sign
            rows.append(tuple(entry))
    for first, second in ((0, 1), (0, 2), (1, 2)):
        for sign_one in (2, -2):
            for sign_two in (2, -2):
                entry = [0, 0, 0]
                entry[first] = sign_one
                entry[second] = sign_two
                rows.append(tuple(entry))
    for axis_one in range(3):
        for sign in (1, -1):
            entry = [0, 0, 0]
            entry[axis_one] = 3 * sign
            rows.append(tuple(entry))
    return rows

def opposite_index(velocity):
    result = []
    for row in velocity:
        flipped = (-row[0], -row[1], -row[2])
        result.append(velocity.index(flipped))
    return result

def hermite_table(velocity):
    sound = 2.0 / 3.0
    ident = [[1.0 if a == b else 0.0 for b in range(3)] for a in range(3)]
    speed = [[float(v) for v in row] for row in velocity]
    rows = [[1.0 for row in speed]]
    for first in range(3):
        rows.append([row[first] for row in speed])
    for first in range(3):
        for second in range(first, 3):
            rows.append([row[first] * row[second] - sound * ident[first][second] for row in speed])
    for first in range(3):
        for second in range(first, 3):
            for third in range(second, 3):
                rows.append([row[first] * row[second] * row[third] - sound * (row[first] * ident[second][third] + row[second] * ident[first][third] + row[third] * ident[first][second]) for row in speed])
    normed = []
    for values in rows:
        length = math.sqrt(sum((v * v for v in values)))
        normed.append([v / length for v in values])
    return jnp.asarray(normed, jnp.float32)

def collide_block(block, weights, hermite):
    w_in, b_in, w_out, b_out = weights
    moments = jnp.dot(hermite, block, precision=lax.Precision.HIGHEST, preferred_element_type=jnp.float32)
    rounded = moments.astype(jnp.bfloat16)
    hidden = jnp.tanh(jnp.dot(w_in.T, rounded, preferred_element_type=jnp.float32) + b_in[:, None]).astype(jnp.bfloat16)
    change = jnp.dot(w_out.T, hidden, preferred_element_type=jnp.float32) + b_out[:, None]
    return (block + change, rounded, hidden)

def adjoint_block(block, incoming, weights, hermite):
    w_in, b_in, w_out, b_out = weights
    unused, rounded, hidden = collide_block(block, weights, hermite)
    grad_rounded = incoming.astype(jnp.bfloat16)
    d_hidden = jnp.dot(w_out, grad_rounded, preferred_element_type=jnp.float32)
    hidden_wide = hidden.astype(jnp.float32)
    d_act = (d_hidden * (1.0 - hidden_wide * hidden_wide)).astype(jnp.bfloat16)
    d_moments = jnp.dot(w_in, d_act, preferred_element_type=jnp.float32)
    d_block = incoming + jnp.dot(hermite.T, d_moments, precision=lax.Precision.HIGHEST, preferred_element_type=jnp.float32)
    grads = (jnp.dot(rounded, d_act.T, preferred_element_type=jnp.float32), lax.optimization_barrier(jnp.sum(d_act.astype(jnp.float32), axis=1)), jnp.dot(hidden, grad_rounded.T, preferred_element_type=jnp.float32), lax.optimization_barrier(jnp.sum(incoming, axis=1)))
    return (d_block, grads)

def split_blocks(values):
    count = values.shape[1] // CZ
    return jnp.moveaxis(values.reshape(values.shape[0], count, CZ * values.shape[2]), 1, 0)

def join_blocks(blocks, shape):
    return jnp.moveaxis(blocks, 0, 1).reshape(shape)

def collide_field(state, weights, hermite):
    blocks = lax.map(lambda block: collide_block(block, weights, hermite)[0], split_blocks(state))
    return join_blocks(blocks, state.shape)

def adjoint_field(state, incoming, weights, hermite):
    zeros = tuple((jnp.zeros(w.shape, jnp.float32) for w in weights))

    def advance(totals, pair):
        d_block, grads = adjoint_block(pair[0], pair[1], weights, hermite)
        return (tuple((a + b for a, b in zip(totals, grads))), d_block)
    totals, blocks = lax.scan(advance, zeros, (split_blocks(state), split_blocks(incoming)))
    return (join_blocks(blocks, state.shape), totals)

def roll_plane(rows, along_x, along_y):
    depth = rows.shape[0]
    grid = rows.reshape(depth, NX, NY)
    return jnp.roll(grid, (along_x, along_y), (1, 2)).reshape(depth, NX * NY)

def stream_whole(state, velocity, sign):
    moved = []
    for index in range(len(velocity)):
        along_x = sign * velocity[index][0]
        along_y = sign * velocity[index][1]
        along_z = sign * velocity[index][2]
        part = jnp.roll(state[index], along_z, 0)
        moved.append(roll_plane(part, along_x, along_y))
    return jnp.stack(moved)

def reference(field, solid, cotangent, w_in, b_in, w_out, b_out):
    velocity = velocity_table()
    opposite = opposite_index(velocity)
    hermite = hermite_table(velocity)
    weights = (w_in, b_in, w_out, b_out)
    totals = tuple((jnp.zeros(w.shape, jnp.float32) for w in weights))
    results = []
    for trajectory in range(TRAJ):
        wall = solid[trajectory].astype(jnp.float32)[None]
        fluid = 1.0 - wall
        current = field[trajectory]
        states = []
        for step in range(STEPS):
            states.append(current)
            post = collide_field(current, weights, hermite)
            current = fluid * stream_whole(post, velocity, 1) + wall * post[jnp.asarray(opposite, jnp.int32)]
        back = cotangent[trajectory]
        for step in range(STEPS - 1, -1, -1):
            incoming = stream_whole(fluid * back, velocity, -1) + (wall * back)[jnp.asarray(opposite, jnp.int32)]
            back, grads = adjoint_field(states[step], incoming, weights, hermite)
            totals = tuple((a + b for a, b in zip(totals, grads)))
        results.append(back)
    scale = 1.0 / math.sqrt(float(TRAJ * NZ * PLANE * STEPS))
    return (jnp.stack(results), totals[0] * scale, totals[1] * scale, totals[2] * scale, totals[3] * scale)
```

```python
import math

import jax
import jax.numpy as jnp
import numpy as np
from jax import lax
from jax.experimental import pallas as pl
from jax.experimental.pallas import tpu as pltpu
from jax.sharding import PartitionSpec as P

STEPS = 3
NX = 16
NY = 16
Q = 39
QP = 48
MOM = 20
MP = 32
REACH = 3
BLOCK = 40
CHUNK = 128
BF = jnp.bfloat16
F32 = jnp.float32


def velocity_table():
    rows = [(0, 0, 0)]
    for axis_one in range(3):
        for sign in (1, -1):
            entry = [0, 0, 0]
            entry[axis_one] = sign
            rows.append(tuple(entry))
    for along_x in (1, -1):
        for along_y in (1, -1):
            for along_z in (1, -1):
                rows.append((along_x, along_y, along_z))
    for axis_one in range(3):
        for sign in (1, -1):
            entry = [0, 0, 0]
            entry[axis_one] = 2 * sign
            rows.append(tuple(entry))
    for first, second in ((0, 1), (0, 2), (1, 2)):
        for sign_one in (2, -2):
            for sign_two in (2, -2):
                entry = [0, 0, 0]
                entry[first] = sign_one
                entry[second] = sign_two
                rows.append(tuple(entry))
    for axis_one in range(3):
        for sign in (1, -1):
            entry = [0, 0, 0]
            entry[axis_one] = 3 * sign
            rows.append(tuple(entry))
    return rows


def opposite_index(velocity):
    return [velocity.index((-row[0], -row[1], -row[2])) for row in velocity]


def hermite_table(velocity):
    sound = 2.0 / 3.0
    ident = [[1.0 if a == b else 0.0 for b in range(3)] for a in range(3)]
    speed = [[float(v) for v in row] for row in velocity]
    rows = [[1.0 for row in speed]]
    for first in range(3):
        rows.append([row[first] for row in speed])
    for first in range(3):
        for second in range(first, 3):
            rows.append([row[first] * row[second] - sound * ident[first][second] for row in speed])
    for first in range(3):
        for second in range(first, 3):
            for third in range(second, 3):
                rows.append(
                    [
                        row[first] * row[second] * row[third]
                        - sound
                        * (
                            row[first] * ident[second][third]
                            + row[second] * ident[first][third]
                            + row[third] * ident[first][second]
                        )
                        for row in speed
                    ]
                )
    normed = []
    for values in rows:
        length = math.sqrt(sum((v * v for v in values)))
        normed.append([v / length for v in values])
    return np.asarray(normed, np.float32)


VEL = velocity_table()
OPP = opposite_index(VEL)
HERM = hermite_table(VEL)


def reaching(sign):
    return [(k, q) for k in range(1, REACH + 1) for q in range(Q) if sign * VEL[q][2] >= k]


N_REACH = len(reaching(1))
SEND_ONE = REACH * BLOCK + 2 * N_REACH + REACH + 1
SEND_TWO = REACH * BLOCK + N_REACH + 6


def split_hi_lo(table):
    hi = table.astype(BF)
    lo = (table - np.asarray(hi, np.float32)).astype(BF)
    return hi, lo


def hermite_operands():
    wide = np.zeros((MP, QP), np.float32)
    wide[:MOM, :Q] = HERM
    hi, lo = split_hi_lo(wide)
    forward = np.concatenate([hi, hi, lo], axis=1)
    hi, lo = split_hi_lo(np.ascontiguousarray(wide.T))
    backward = np.concatenate([hi, hi, lo], axis=1)
    return jnp.asarray(forward), jnp.asarray(backward)


def dot(a, b):
    return jnp.dot(a, b, preferred_element_type=F32)


def dot_nt(a, b, precision=None):
    return lax.dot_general(
        a, b, (((1,), (1,)), ((), ())), preferred_element_type=F32, precision=precision
    )


def halves(value):
    lanes = value.shape[1] // 2
    return value[:, :lanes], value[:, lanes:]


def get_layer(buf, layer, stride, count=QP):
    return jnp.concatenate([buf[half, pl.ds(layer, count, stride=stride), :] for half in (0, 1)], axis=1)


def put_layer(buf, layer, stride, value):
    count = value.shape[0]
    for half, part in enumerate(halves(value)):
        buf[half, pl.ds(layer, count, stride=stride), :] = part


def get_rows(buf, q, stride, first, count):
    start = q * stride + first
    return jnp.concatenate([buf[half, start : start + count, :] for half in (0, 1)], axis=1)


def put_rows(buf, q, stride, first, value):
    start = q * stride + first
    for half, part in enumerate(halves(value)):
        buf[half, start : start + value.shape[0], :] = part


def clear_pad(buf, stride):
    lanes = buf.shape[2]
    for half in (0, 1):
        buf[half, Q * stride : QP * stride, :] = jnp.zeros(((QP - Q) * stride, lanes), F32)


def roll_plane(value, along_x, along_y):
    lanes = value.shape[1]
    shift = NY * along_x + along_y

    def turned(by):
        by = by % lanes
        return value if by == 0 else pltpu.roll(value, by, 1)

    if along_y == 0:
        return turned(shift)
    column = lax.broadcasted_iota(jnp.int32, value.shape, 1) % NY
    if along_y > 0:
        return jnp.where(column < along_y, turned(shift - NY), turned(shift))
    return jnp.where(column >= NY + along_y, turned(shift + NY), turned(shift))


def split_concat(value):
    hi = value.astype(BF)
    lo = (value - hi.astype(F32)).astype(BF)
    return jnp.concatenate([hi, lo, hi], axis=0)


def moments_of(x, herm):
    moments = dot(herm, split_concat(x))
    row = lax.broadcasted_iota(jnp.int32, moments.shape, 0)
    ones = jnp.where((row >= MOM) & (row < MOM + 3), 1.0, 0.0)
    return (moments + ones).astype(BF)


def hidden_into(h_ref, lanes, w1, mb):
    for start in range(0, w1.shape[0], CHUNK):
        act = dot(w1[start : start + CHUNK, :], mb)
        h_ref[start : start + CHUNK, lanes] = jnp.tanh(act).astype(BF)


def adjoint_layer(gp, gb, h_ref, h_lanes, da_ref, da_lanes, w_out, w_in, herm_t):
    for start in range(0, w_out.shape[0], CHUNK):
        d_hidden = dot(w_out[start : start + CHUNK, :], gb)
        hidden = h_ref[start : start + CHUNK, h_lanes].astype(F32)
        da_ref[start : start + CHUNK, da_lanes] = (d_hidden * (1.0 - hidden * hidden)).astype(BF)
    d_moments = dot(w_in[...], da_ref[:, da_lanes])
    return gp + dot(herm_t, split_concat(d_moments))


def first_kernel(
    field, cot, solid, w_in, b_in, w_out, b_out, herm,
    send_up, send_dn, post, h0, mb0, w1_o, w_in_o, w2_o, w_out_o, b_col_o,
    state, wide, tall,
):
    depth, plane = solid.shape
    hid = w_in.shape[1]
    wide[...] = jnp.zeros(wide.shape, F32)
    wide[:MOM, :] = w_in[...].astype(F32)
    w_in_o[...] = wide[...].astype(BF)
    rest = b_in[...]
    for part in range(3):
        piece = rest.astype(BF).astype(F32)
        wide[MOM + part : MOM + part + 1, :] = piece
        rest = rest - piece
    w1_o[...] = wide[...].T.astype(BF)
    tall[...] = jnp.zeros(tall.shape, F32)
    tall[:Q, :] = w_out[...].astype(F32).T
    w2_o[...] = tall[...].astype(BF)
    w_out_o[...] = tall[...].T.astype(BF)
    tall[0:8, :] = jnp.zeros((8, hid), F32)
    tall[0:1, 0:Q] = b_out[...]
    column = tall[0:8, 0:128].T
    b_col_o[...] = jnp.broadcast_to(column[:QP, 0:1], (QP, plane))

    for q in range(Q):
        put_rows(state, q, depth, 0, field[q * depth : (q + 1) * depth, :])
    clear_pad(state, depth)
    for z in range(depth):
        lanes = slice(z * plane, (z + 1) * plane)
        x = get_layer(state, z, depth)
        mb = moments_of(x, herm[...])
        mb0[:, lanes] = mb
        hidden_into(h0, lanes, w1_o, mb)
        out = x + dot(w2_o[...], h0[:, lanes]) + b_col_o[...]
        put_layer(post, z, depth, out[:Q])
        if z < REACH:
            send_dn[z * BLOCK : z * BLOCK + Q, :] = out[:Q]
        if depth - 1 - z < REACH:
            d = depth - 1 - z
            send_up[d * BLOCK : d * BLOCK + Q, :] = out[:Q]

    wall = solid[...].astype(F32)
    for sign, send in ((1, send_up), (-1, send_dn)):
        layer = (lambda d: depth - d) if sign > 0 else (lambda d: d - 1)
        row = REACH * BLOCK
        for k, q in reaching(sign):
            send[row : row + 1, :] = get_rows(post, q, depth, layer(REACH + k), 1)
            row += 1
        for k, q in reaching(-sign):
            z = layer(k)
            at = q * depth + z
            send[row : row + 1, :] = cot[at : at + 1, :] * (1.0 - wall[z : z + 1, :])
            row += 1
        for d in range(1, REACH + 1):
            send[row : row + 1, :] = wall[layer(d) : layer(d) + 1, :]
            row += 1


def second_kernel(
    post, below, above, cot, solid, w1, w_in, w2, w_out, b_col, herm, herm_t,
    send_up, send_dn, g2, wall_o, h1, mb1, h2, mb2, da2, gb2, gsum,
    p0, s1, p1, s2, gx, gp2,
):
    depth, plane = solid.shape
    edge = REACH + 1
    mid = depth + 2 * edge
    ext = depth + 16
    wall_o[...] = jnp.zeros(wall_o.shape, F32)
    wall_o[edge : edge + depth, :] = solid[...].astype(F32)
    row = REACH * BLOCK + 2 * N_REACH
    for d in range(1, REACH + 1):
        wall_o[edge - d : edge - d + 1, :] = below[row + d - 1 : row + d, :]
        wall_o[edge + depth + d - 1 : edge + depth + d, :] = above[row + d - 1 : row + d, :]
    wall_ext = wall_o[...]
    wall = wall_o[edge : edge + depth, :]

    for q in range(Q):
        put_rows(p0, q, ext, 8, get_rows(post, q, depth, 0, depth))
    for d in range(1, REACH + 1):
        put_layer(p0, 8 - d, ext, below[(d - 1) * BLOCK : (d - 1) * BLOCK + Q, :])
        put_layer(p0, 7 + depth + d, ext, above[(d - 1) * BLOCK : (d - 1) * BLOCK + Q, :])
    row = REACH * BLOCK
    for n, (k, q) in enumerate(reaching(1)):
        put_rows(p0, q, ext, 8 - REACH - k, below[row + n : row + n + 1, :])
    for n, (k, q) in enumerate(reaching(-1)):
        put_rows(p0, q, ext, 7 + depth + REACH + k, above[row + n : row + n + 1, :])

    for q in range(Q):
        ex, ey, ez = VEL[q]
        moved = roll_plane(get_rows(p0, q, ext, 8 - edge - ez, mid), ex, ey)
        bounced = get_rows(p0, OPP[q], ext, 8 - edge, mid)
        put_rows(s1, q, mid, 0, jnp.where(wall_ext > 0.5, bounced, moved))
    clear_pad(s1, mid)
    for i in range(1, mid - 1):
        lanes = slice((i - 1) * plane, i * plane)
        x = get_layer(s1, i, mid)
        mb = moments_of(x, herm[...])
        mb1[:, lanes] = mb
        hidden_into(h1, lanes, w1, mb)
        out = x + dot(w2[...], h1[:, lanes]) + b_col[...]
        put_layer(p1, i, mid, out[:Q])

    for q in range(Q):
        ex, ey, ez = VEL[q]
        moved = roll_plane(get_rows(p1, q, mid, edge - ez, depth), ex, ey)
        bounced = get_rows(p1, OPP[q], mid, edge, depth)
        put_rows(s2, q, depth, 0, jnp.where(wall > 0.5, bounced, moved))
    clear_pad(s2, depth)
    for q in range(Q):
        put_rows(gx, q, mid, edge, cot[q * depth : (q + 1) * depth, :] * (1.0 - wall))
    row = REACH * BLOCK + N_REACH
    for n, (k, q) in enumerate(reaching(-1)):
        put_rows(gx, q, mid, edge - k, below[row + n : row + n + 1, :])
    for n, (k, q) in enumerate(reaching(1)):
        put_rows(gx, q, mid, edge + depth - 1 + k, above[row + n : row + n + 1, :])
    for q in range(Q):
        ex, ey, ez = VEL[q]
        moved = roll_plane(get_rows(gx, q, mid, edge + ez, depth), -ex, -ey)
        at = OPP[q] * depth
        put_rows(gp2, q, depth, 0, moved + wall * cot[at : at + depth, :])
    clear_pad(gp2, depth)

    total = jnp.zeros((QP, plane), F32)
    for z in range(depth):
        lanes = slice(z * plane, (z + 1) * plane)
        mb = moments_of(get_layer(s2, z, depth), herm[...])
        mb2[:, lanes] = mb
        hidden_into(h2, lanes, w1, mb)
        gp = get_layer(gp2, z, depth)
        gb = gp.astype(BF)
        gb2[:, lanes] = gb
        total = total + gp
        g = adjoint_layer(gp, gb, h2, lanes, da2, lanes, w_out, w_in, herm_t[...])[:Q]
        put_layer(g2, z, depth, g)
        if z < REACH:
            send_dn[z * BLOCK : z * BLOCK + Q, :] = g
        if depth - 1 - z < REACH:
            d = depth - 1 - z
            send_up[d * BLOCK : d * BLOCK + Q, :] = g
    gsum[...] = total

    for sign, send in ((1, send_up), (-1, send_dn)):
        row = REACH * BLOCK
        for k, q in reaching(-sign):
            z = depth - REACH - k if sign > 0 else REACH + k - 1
            open_cells = 1.0 - wall_o[edge + z : edge + z + 1, :]
            send[row : row + 1, :] = get_rows(g2, q, depth, z, 1) * open_cells
            row += 1


def sums_kernel(mb2, da2, gb2, h2, acc):
    acc[0:MP, :] = dot_nt(mb2[...], da2[...])
    acc[MP : MP + QP, :] = dot_nt(gb2[...], h2[...])


def third_kernel(
    g2, below, above, wall_i, h1, mb1, h0, mb0, acc, gsum, w_in, w_out, herm_t,
    d_field, sums,
    gx, raw, gp1, g1, raw1, gp0, da1, da0, gb1, gb0, out0,
):
    mid, plane = wall_i.shape
    edge = REACH + 1
    depth = mid - 2 * edge
    ext = depth + 16
    wall_ext = wall_i[...]
    open_ext = 1.0 - wall_ext
    wall = wall_i[edge : edge + depth, :]

    for q in range(Q):
        put_rows(raw, q, mid, edge, get_rows(g2, q, depth, 0, depth))
    for d in range(1, REACH + 1):
        put_layer(raw, edge - d, mid, below[(d - 1) * BLOCK : (d - 1) * BLOCK + Q, :])
        put_layer(raw, edge + depth - 1 + d, mid, above[(d - 1) * BLOCK : (d - 1) * BLOCK + Q, :])
    for q in range(Q):
        put_rows(gx, q, ext, 8 - edge, get_rows(raw, q, mid, 0, mid) * open_ext)
    row = REACH * BLOCK
    for n, (k, q) in enumerate(reaching(-1)):
        put_rows(gx, q, ext, 8 - REACH - k, below[row + n : row + n + 1, :])
    for n, (k, q) in enumerate(reaching(1)):
        put_rows(gx, q, ext, 7 + depth + REACH + k, above[row + n : row + n + 1, :])
    for q in range(Q):
        ex, ey, ez = VEL[q]
        moved = roll_plane(get_rows(gx, q, ext, 8 - edge + ez, mid), -ex, -ey)
        put_rows(gp1, q, mid, 0, moved + wall_ext * get_rows(raw, OPP[q], mid, 0, mid))
    clear_pad(gp1, mid)

    total = gsum[...]
    for i in range(1, mid - 1):
        lanes = slice((i - 1) * plane, i * plane)
        gp = get_layer(gp1, i, mid)
        gb = gp.astype(BF)
        if edge <= i < edge + depth:
            gb1[:, (i - edge) * plane : (i - edge + 1) * plane] = gb
            total = total + gp
        g = adjoint_layer(gp, gb, h1, lanes, da1, lanes, w_out, w_in, herm_t[...])[:Q]
        put_layer(raw1, i, mid, g)
        put_layer(g1, i, mid, g * open_ext[i : i + 1, :])

    for q in range(Q):
        ex, ey, ez = VEL[q]
        moved = roll_plane(get_rows(g1, q, mid, edge + ez, depth), -ex, -ey)
        put_rows(gp0, q, depth, 0, moved + wall * get_rows(raw1, OPP[q], mid, edge, depth))
    clear_pad(gp0, depth)
    for z in range(depth):
        lanes = slice(z * plane, (z + 1) * plane)
        gp = get_layer(gp0, z, depth)
        gb = gp.astype(BF)
        gb0[:, lanes] = gb
        total = total + gp
        g = adjoint_layer(gp, gb, h0, lanes, da0, lanes, w_out, w_in, herm_t[...])[:Q]
        put_layer(out0, z, depth, g)
    for q in range(Q):
        d_field[q * depth : (q + 1) * depth, :] = get_rows(out0, q, depth, 0, depth)

    own = slice(REACH * plane, (REACH + depth) * plane)
    part = acc[0:MP, :] + dot_nt(mb1[:, own], da1[:, own]) + dot_nt(mb0[...], da0[...])
    sums[0:24, :] = part[0:24, :]
    part = acc[MP : MP + QP, :] + dot_nt(gb1[...], h1[:, own]) + dot_nt(gb0[...], h0[...])
    sums[24 : 24 + Q + 1, :] = part[0 : Q + 1, :]
    line = dot_nt(jnp.ones((8, plane), F32), total, lax.Precision.HIGHEST)
    sums[MOM + 1 : MOM + 2, 0:QP] = line[0:1, :]


def last_kernel(scale, core, mine, other, g_w_in, g_b_in, g_w_out, g_b_out):
    first = core[0] == 0
    low = jnp.where(first, mine[...], other[...]) * scale
    high = jnp.where(first, other[...], mine[...]) * scale
    g_w_in[...] = low[:MOM, :]
    g_b_in[...] = low[MOM : MOM + 1, :]
    g_b_out[...] = low[MOM + 1 : MOM + 2, :Q]
    turned = jnp.concatenate([low[24:, :], high], axis=0).T
    g_w_out[...] = turned[:, :Q]


def call(kernel, outs, scratch, args, flops, smem=()):
    vmem = pl.BlockSpec(memory_space=pltpu.VMEM)
    scalars = pl.BlockSpec(memory_space=pltpu.SMEM)
    return pl.pallas_call(
        kernel,
        out_shape=[jax.ShapeDtypeStruct(shape, kind) for shape, kind in outs],
        in_specs=[scalars if n in smem else vmem for n in range(len(args))],
        out_specs=[vmem] * len(outs),
        scratch_shapes=[pltpu.VMEM(shape, kind) for shape, kind in scratch],
        compiler_params=pltpu.CompilerParams(vmem_limit_bytes=28 * 1024 * 1024),
        cost_estimate=pl.CostEstimate(flops=flops, bytes_accessed=2000000, transcendentals=0),
    )(*args)


def factor_stages(space, traj):
    core = 2 if space % 2 == 0 else 1
    rest = space // core
    stride = traj * core
    stages = []
    first = [(1, traj)] if traj > 1 else []
    if rest % 2 == 0 and traj <= 2:
        first.append((stride, 2))
        stride, rest = stride * 2, rest // 2
    if first:
        stages.append(first)
    while rest > 1:
        size = next((f for f in (4, 3, 2) if rest % f == 0), rest)
        stages.append([(stride, size)])
        stride, rest = stride * size, rest // size
    return core, stages


def partners(total, digits):
    shifts = [()]
    for _, size in digits:
        shifts = [s + (k,) for s in shifts for k in range(size)]
    result = []
    for shift in shifts[1:]:
        pairs = []
        for index in range(total):
            to = index
            for (stride, size), k in zip(digits, shift):
                digit = index // stride % size
                to += ((digit + k) % size - digit) * stride
            pairs.append((index, to))
        result.append(pairs)
    return result


def per_device(field, solid, cotangent, w_in, b_in, w_out, b_out):
    local, pops, depth, plane = field.shape
    hid = w_in.shape[1]
    space, traj = lax.axis_size("space"), lax.axis_size("traj")
    axes = ("space", "traj")
    up = [(i, (i + 1) % space) for i in range(space)]
    down = [(j, i) for i, j in up]
    herm, herm_t = hermite_operands()
    edge = REACH + 1
    mid, ext = depth + 2 * edge, depth + 16
    work = mid - 2
    half = plane // 2
    field = field.reshape(pops * depth, plane)
    cot = cotangent.reshape(pops * depth, plane)
    solid = solid.reshape(depth, plane)

    def pops_buf(rows, count=QP):
        return ((2, count * rows, half), F32)

    send_up, send_dn, post, h0, mb0, w1, w_in_p, w2, w_out_p, b_col = call(
        first_kernel,
        [
            ((SEND_ONE, plane), F32),
            ((SEND_ONE, plane), F32),
            pops_buf(depth, Q),
            ((hid, depth * plane), BF),
            ((MP, depth * plane), BF),
            ((hid, MP), BF),
            ((MP, hid), BF),
            ((QP, hid), BF),
            ((hid, QP), BF),
            ((QP, plane), F32),
        ],
        [pops_buf(depth), ((MP, hid), F32), ((QP, hid), F32)],
        [field, cot, solid, w_in, b_in.reshape(1, hid), w_out, b_out.reshape(1, pops), herm],
        10**9,
    )
    below = lax.ppermute(send_up, "space", up)
    above = lax.ppermute(send_dn, "space", down)
    send_up, send_dn, g2, wall, h1, mb1, h2, mb2, da2, gb2, gsum = call(
        second_kernel,
        [
            ((SEND_TWO, plane), F32),
            ((SEND_TWO, plane), F32),
            pops_buf(depth, Q),
            ((mid, plane), F32),
            ((hid, work * plane), BF),
            ((MP, work * plane), BF),
            ((hid, depth * plane), BF),
            ((MP, depth * plane), BF),
            ((hid, depth * plane), BF),
            ((QP, depth * plane), BF),
            ((QP, plane), F32),
        ],
        [pops_buf(ext), pops_buf(mid), pops_buf(mid), pops_buf(depth), pops_buf(mid), pops_buf(depth)],
        [post, below, above, cot, solid, w1, w_in_p, w2, w_out_p, b_col, herm, herm_t],
        3 * 10**9,
    )
    below = lax.ppermute(send_up, "space", up)
    above = lax.ppermute(send_dn, "space", down)
    (acc,) = call(sums_kernel, [((MP + QP, hid), F32)], [], [mb2, da2, gb2, h2], 10**9)
    d_field, sums = call(
        third_kernel,
        [((pops * depth, plane), F32), ((64, hid), F32)],
        [
            pops_buf(ext), pops_buf(mid), pops_buf(mid), pops_buf(mid), pops_buf(mid), pops_buf(depth),
            ((hid, work * plane), BF), ((hid, depth * plane), BF),
            ((QP, depth * plane), BF), ((QP, depth * plane), BF), pops_buf(depth),
        ],
        [g2, below, above, wall, h1, mb1, h0, mb0, acc, gsum, w_in_p, w_out_p, herm_t],
        3 * 10**9,
    )

    core, stages = factor_stages(space, traj)
    total = space * traj
    me = lax.axis_index("space") % core
    swap = partners(total, [(traj, core)])[0]
    rows = sums.shape[0] // 2
    mine = lax.dynamic_slice_in_dim(sums, me * rows, rows, 0)
    other = lax.dynamic_slice_in_dim(sums, (1 - me) * rows, rows, 0)
    mine = mine + lax.ppermute(other, axes, swap)
    for digits in stages:
        moved = [lax.ppermute(mine, axes, pairs) for pairs in partners(total, digits)]
        for value in moved:
            mine = mine + value
    other = lax.ppermute(mine, axes, swap)

    cells = traj * local * space * depth * plane * STEPS
    scale = 1.0 / math.sqrt(float(cells))
    g_w_in, g_b_in, g_w_out, g_b_out = call(
        lambda *refs: last_kernel(scale, *refs),
        [((MOM, hid), F32), ((1, hid), F32), ((hid, pops), F32), ((1, pops), F32)],
        [],
        [me.reshape(1).astype(jnp.int32), mine, other],
        10**6,
        smem=(0,),
    )
    return (
        d_field.reshape(local, pops, depth, plane),
        g_w_in,
        g_b_in.reshape(hid),
        g_w_out,
        g_b_out.reshape(pops),
    )


def solution(mesh):
    return jax.shard_map(
        per_device,
        mesh=mesh,
        in_specs=(
            P("traj", None, "space", None),
            P("traj", "space", None),
            P("traj", None, "space", None),
            P(),
            P(),
            P(),
            P(),
        ),
        out_specs=(P("traj", None, "space", None), P(), P(), P(), P()),
        check_vma=False,
    )
```

```python
import math

import jax
import jax.numpy as jnp
import numpy as np
from jax import lax
from jax.experimental import pallas as pl
from jax.experimental.pallas import tpu as pltpu
from jax.sharding import PartitionSpec as P

STEPS = 3
NX = 16
NY = 16
Q = 39
QP = 48
MOM = 20
MP = 32
REACH = 3
BLOCK = 40
CHUNK = 128
MIB = 1024 * 1024
BF = jnp.bfloat16
F32 = jnp.float32


def velocity_table():
    rows = [(0, 0, 0)]
    for axis_one in range(3):
        for sign in (1, -1):
            entry = [0, 0, 0]
            entry[axis_one] = sign
            rows.append(tuple(entry))
    for along_x in (1, -1):
        for along_y in (1, -1):
            for along_z in (1, -1):
                rows.append((along_x, along_y, along_z))
    for axis_one in range(3):
        for sign in (1, -1):
            entry = [0, 0, 0]
            entry[axis_one] = 2 * sign
            rows.append(tuple(entry))
    for first, second in ((0, 1), (0, 2), (1, 2)):
        for sign_one in (2, -2):
            for sign_two in (2, -2):
                entry = [0, 0, 0]
                entry[first] = sign_one
                entry[second] = sign_two
                rows.append(tuple(entry))
    for axis_one in range(3):
        for sign in (1, -1):
            entry = [0, 0, 0]
            entry[axis_one] = 3 * sign
            rows.append(tuple(entry))
    return rows


def opposite_index(velocity):
    return [velocity.index((-row[0], -row[1], -row[2])) for row in velocity]


def hermite_table(velocity):
    sound = 2.0 / 3.0
    ident = [[1.0 if a == b else 0.0 for b in range(3)] for a in range(3)]
    speed = [[float(v) for v in row] for row in velocity]
    rows = [[1.0 for row in speed]]
    for first in range(3):
        rows.append([row[first] for row in speed])
    for first in range(3):
        for second in range(first, 3):
            rows.append([row[first] * row[second] - sound * ident[first][second] for row in speed])
    for first in range(3):
        for second in range(first, 3):
            for third in range(second, 3):
                rows.append(
                    [
                        row[first] * row[second] * row[third]
                        - sound
                        * (
                            row[first] * ident[second][third]
                            + row[second] * ident[first][third]
                            + row[third] * ident[first][second]
                        )
                        for row in speed
                    ]
                )
    normed = []
    for values in rows:
        length = math.sqrt(sum((v * v for v in values)))
        normed.append([v / length for v in values])
    return np.asarray(normed, np.float32)


VEL = velocity_table()
OPP = opposite_index(VEL)
HERM = hermite_table(VEL)


def reaching(sign):
    return [(k, q) for k in range(1, REACH + 1) for q in range(Q) if sign * VEL[q][2] >= k]


N_REACH = len(reaching(1))
SEND_ONE = REACH * BLOCK + 2 * N_REACH + REACH + 1
SEND_TWO = REACH * BLOCK + N_REACH + 6


def split_hi_lo(table):
    hi = table.astype(BF)
    lo = (table - np.asarray(hi, np.float32)).astype(BF)
    return hi, lo


def hermite_operands():
    wide = np.zeros((MP, QP), np.float32)
    wide[:MOM, :Q] = HERM
    hi, lo = split_hi_lo(wide)
    forward = np.concatenate([hi, hi, lo], axis=1)
    hi, lo = split_hi_lo(np.ascontiguousarray(wide.T))
    backward = np.concatenate([hi, hi, lo], axis=1)
    return jnp.asarray(forward), jnp.asarray(backward)


def dot(a, b):
    return jnp.dot(a, b, preferred_element_type=F32)


def dot_nt(a, b, precision=None):
    return lax.dot_general(
        a, b, (((1,), (1,)), ((), ())), preferred_element_type=F32, precision=precision
    )


def halves(value):
    lanes = value.shape[1] // 2
    return value[:, :lanes], value[:, lanes:]


def get_layer(buf, layer, stride, count=QP):
    return jnp.concatenate([buf[half, pl.ds(layer, count, stride=stride), :] for half in (0, 1)], axis=1)


def put_layer(buf, layer, stride, value):
    count = value.shape[0]
    for half, part in enumerate(halves(value)):
        buf[half, pl.ds(layer, count, stride=stride), :] = part


def get_rows(buf, q, stride, first, count):
    start = q * stride + first
    return jnp.concatenate([buf[half, start : start + count, :] for half in (0, 1)], axis=1)


def put_rows(buf, q, stride, first, value):
    start = q * stride + first
    for half, part in enumerate(halves(value)):
        buf[half, start : start + value.shape[0], :] = part


def clear_pad(buf, stride):
    lanes = buf.shape[2]
    for half in (0, 1):
        buf[half, Q * stride : QP * stride, :] = jnp.zeros(((QP - Q) * stride, lanes), F32)


def roll_plane(value, along_x, along_y):
    lanes = value.shape[1]
    shift = NY * along_x + along_y

    def turned(by):
        by = by % lanes
        return value if by == 0 else pltpu.roll(value, by, 1)

    if along_y == 0:
        return turned(shift)
    column = lax.broadcasted_iota(jnp.int32, value.shape, 1) % NY
    if along_y > 0:
        return jnp.where(column < along_y, turned(shift - NY), turned(shift))
    return jnp.where(column >= NY + along_y, turned(shift + NY), turned(shift))


def split_concat(value):
    hi = value.astype(BF)
    lo = (value - hi.astype(F32)).astype(BF)
    return jnp.concatenate([hi, lo, hi], axis=0)


def moments_of(x, herm):
    moments = dot(herm, split_concat(x))
    row = lax.broadcasted_iota(jnp.int32, moments.shape, 0)
    ones = jnp.where((row >= MOM) & (row < MOM + 3), 1.0, 0.0)
    return (moments + ones).astype(BF)


def hidden_into(h, w1, mb):
    for start in range(0, w1.shape[0], CHUNK):
        act = dot(w1[start : start + CHUNK, :], mb)
        h[start : start + CHUNK, :] = jnp.tanh(act).astype(BF)


def d_act_into(da, h, w_out, gb):
    for start in range(0, w_out.shape[0], CHUNK):
        d_hidden = dot(w_out[start : start + CHUNK, :], gb)
        hidden = h[start : start + CHUNK, :].astype(F32)
        da[start : start + CHUNK, :] = (d_hidden * (1.0 - hidden * hidden)).astype(BF)


def staggered(count, *stages):
    for turn in range(count + len(stages) - 1):
        for late, stage in enumerate(stages):
            if 0 <= turn - late < count:
                stage(turn - late)


def add_sums(acc, mb, da, gb, h):
    acc[0:MP, :] += dot_nt(mb, da[...])
    acc[MP : MP + QP, :] += dot_nt(gb, h[...])


class Copies:
    def __init__(self, sems):
        self.sems, self.used, self.open = sems, 0, []

    def start(self, source, target):
        copy = pltpu.make_async_copy(source, target, self.sems.at[self.used])
        self.used += 1
        copy.start()
        self.open.append(copy)
        return copy

    def wait(self):
        for copy in self.open:
            copy.wait()
        self.open = []


def first_kernel(
    w_in_h, b_in_h, w_out_h, b_out_h, herm_h, field_h, solid_h, cot_h,
    send_up, send_dn, post, mb0_h, w1_o, w_in_o, w2_o, w_out_o, b_col_o,
    state, wide, tall, w_in, b_in, w_out, b_out, herm, field, solid, cot, h, mb0, sems,
):
    sources = (w_in_h, b_in_h, w_out_h, b_out_h, herm_h, field_h, solid_h, cot_h)
    targets = (w_in, b_in, w_out, b_out, herm, field, solid, cot)
    moves = Copies(sems)
    copies = [moves.start(a, b) for a, b in zip(sources, targets)]
    moves.open = []
    depth, plane = solid.shape
    hid = w_in.shape[1]
    for copy in copies[:4]:
        copy.wait()
    wide[...] = jnp.zeros(wide.shape, F32)
    wide[:MOM, :] = w_in[...].astype(F32)
    w_in_o[...] = wide[...].astype(BF)
    rest = b_in[...]
    for part in range(3):
        piece = rest.astype(BF).astype(F32)
        wide[MOM + part : MOM + part + 1, :] = piece
        rest = rest - piece
    w1_o[...] = wide[...].T.astype(BF)
    tall[...] = jnp.zeros(tall.shape, F32)
    tall[:Q, :] = w_out[...].astype(F32)
    w2_o[...] = tall[...].astype(BF)
    w_out_o[...] = tall[...].T.astype(BF)
    tall[0:8, :] = jnp.zeros((8, hid), F32)
    tall[0:1, 0:Q] = b_out[...]
    column = tall[0:8, 0:128].T
    b_col_o[...] = jnp.broadcast_to(column[:QP, 0:1], (QP, plane))

    for copy in copies[4:6]:
        copy.wait()
    for q in range(Q):
        put_rows(state, q, depth, 0, field[q * depth : (q + 1) * depth, :])
    clear_pad(state, depth)
    for z in range(depth):
        mb0[z] = moments_of(get_layer(state, z, depth), herm[...])
    moves.start(mb0, mb0_h)

    def hide(z):
        hidden_into(h.at[z % 2], w1_o, mb0[z])

    def finish(z):
        out = get_layer(state, z, depth) + dot(w2_o[...], h[z % 2]) + b_col_o[...]
        out = out[:Q]
        put_layer(post, z, depth, out)
        if z < REACH:
            send_dn[z * BLOCK : z * BLOCK + Q, :] = out
        if depth - 1 - z < REACH:
            d = depth - 1 - z
            send_up[d * BLOCK : d * BLOCK + Q, :] = out

    staggered(depth, hide, finish)
    for copy in copies[6:]:
        copy.wait()
    wall = solid[...].astype(F32)
    for sign, send in ((1, send_up), (-1, send_dn)):
        layer = (lambda d: depth - d) if sign > 0 else (lambda d: d - 1)
        row = REACH * BLOCK
        for k, q in reaching(sign):
            send[row : row + 1, :] = get_rows(post, q, depth, layer(REACH + k), 1)
            row += 1
        for k, q in reaching(-sign):
            z = layer(k)
            at = q * depth + z
            send[row : row + 1, :] = cot[at : at + 1, :] * (1.0 - wall[z : z + 1, :])
            row += 1
        for d in range(1, REACH + 1):
            send[row : row + 1, :] = wall[layer(d) : layer(d) + 1, :]
            row += 1
    moves.wait()


def second_kernel(
    post, below, above, cot, solid, w1, w_in, w2, w_out, b_col, herm, herm_t,
    send_up, send_dn, g2, wall_o, h1_h, mb1_h, mb2_h, gb2_h,
    p0, s1, p1, s2, gx, gp2, h1, mb1, mb2, gb2, h2, da2, dm, sems,
):
    moves = Copies(sems)
    depth, plane = solid.shape
    edge = REACH + 1
    mid = depth + 2 * edge
    ext = depth + 16
    wall_o[...] = jnp.zeros(wall_o.shape, F32)
    wall_o[edge : edge + depth, :] = solid[...].astype(F32)
    row = REACH * BLOCK + 2 * N_REACH
    for d in range(1, REACH + 1):
        wall_o[edge - d : edge - d + 1, :] = below[row + d - 1 : row + d, :]
        wall_o[edge + depth + d - 1 : edge + depth + d, :] = above[row + d - 1 : row + d, :]
    wall_ext = wall_o[0:mid, :]
    wall = wall_o[edge : edge + depth, :]

    for q in range(Q):
        put_rows(p0, q, ext, 8, get_rows(post, q, depth, 0, depth))
    for d in range(1, REACH + 1):
        put_layer(p0, 8 - d, ext, below[(d - 1) * BLOCK : (d - 1) * BLOCK + Q, :])
        put_layer(p0, 7 + depth + d, ext, above[(d - 1) * BLOCK : (d - 1) * BLOCK + Q, :])
    row = REACH * BLOCK
    for n, (k, q) in enumerate(reaching(1)):
        put_rows(p0, q, ext, 8 - REACH - k, below[row + n : row + n + 1, :])
    for n, (k, q) in enumerate(reaching(-1)):
        put_rows(p0, q, ext, 7 + depth + REACH + k, above[row + n : row + n + 1, :])

    for q in range(Q):
        ex, ey, ez = VEL[q]
        moved = roll_plane(get_rows(p0, q, ext, 8 - edge - ez, mid), ex, ey)
        bounced = get_rows(p0, OPP[q], ext, 8 - edge, mid)
        put_rows(s1, q, mid, 0, jnp.where(wall_ext > 0.5, bounced, moved))
    clear_pad(s1, mid)
    def moments(n):
        mb1[n] = moments_of(get_layer(s1, n + 1, mid), herm[...])

    def hide(n):
        hidden_into(h1.at[n], w1, mb1[n])
        moves.start(h1.at[n], h1_h.at[n])

    def finish(n):
        out = get_layer(s1, n + 1, mid) + dot(w2[...], h1[n]) + b_col[...]
        put_layer(p1, n + 1, mid, out[:Q])

    staggered(mid - 2, moments, hide, finish)
    moves.start(mb1, mb1_h)

    for q in range(Q):
        ex, ey, ez = VEL[q]
        moved = roll_plane(get_rows(p1, q, mid, edge - ez, depth), ex, ey)
        bounced = get_rows(p1, OPP[q], mid, edge, depth)
        put_rows(s2, q, depth, 0, jnp.where(wall > 0.5, bounced, moved))
    clear_pad(s2, depth)
    for q in range(Q):
        put_rows(gx, q, mid, edge, cot[q * depth : (q + 1) * depth, :] * (1.0 - wall))
    row = REACH * BLOCK + N_REACH
    for n, (k, q) in enumerate(reaching(-1)):
        put_rows(gx, q, mid, edge - k, below[row + n : row + n + 1, :])
    for n, (k, q) in enumerate(reaching(1)):
        put_rows(gx, q, mid, edge + depth - 1 + k, above[row + n : row + n + 1, :])
    for q in range(Q):
        ex, ey, ez = VEL[q]
        moved = roll_plane(get_rows(gx, q, mid, edge + ez, depth), -ex, -ey)
        at = OPP[q] * depth
        put_rows(gp2, q, depth, 0, moved + wall * cot[at : at + depth, :])
    clear_pad(gp2, depth)

    total = jnp.zeros((QP, plane), F32)
    for z in range(depth):
        mb2[z] = moments_of(get_layer(s2, z, depth), herm[...])
        gp = get_layer(gp2, z, depth)
        gb2[z] = gp.astype(BF)
        total = total + gp
    wall_o[mid : mid + QP, :] = total
    moves.start(mb2, mb2_h)
    moves.start(gb2, gb2_h)

    def hide_two(z):
        hidden_into(h2.at[z % 2], w1, mb2[z])

    def act(z):
        d_act_into(da2.at[z % 2], h2.at[z % 2], w_out, gb2[z])

    def back(z):
        dm[z % 2] = split_concat(dot(w_in[...], da2[z % 2]))

    def finish_two(z):
        g = (get_layer(gp2, z, depth) + dot(herm_t[...], dm[z % 2]))[:Q]
        put_layer(g2, z, depth, g)
        if z < REACH:
            send_dn[z * BLOCK : z * BLOCK + Q, :] = g
        if depth - 1 - z < REACH:
            d = depth - 1 - z
            send_up[d * BLOCK : d * BLOCK + Q, :] = g

    staggered(depth, hide_two, act, back, finish_two)

    for sign, send in ((1, send_up), (-1, send_dn)):
        row = REACH * BLOCK
        for k, q in reaching(-sign):
            z = depth - REACH - k if sign > 0 else REACH + k - 1
            open_cells = 1.0 - wall_o[edge + z : edge + z + 1, :]
            send[row : row + 1, :] = get_rows(g2, q, depth, z, 1) * open_cells
            row += 1
    moves.wait()


def sums_kernel(
    mb2_h, gb2_h, mb0_h, mb1_h, h1_h, w1, w_out, acc, h0, mb0, h1, mb1, mb2, gb2, h2, da2, sems
):
    moves = Copies(sems)
    pairs = ((mb2_h, mb2), (gb2_h, gb2), (mb0_h, mb0), (mb1_h, mb1), (h1_h, h1))
    copies = [moves.start(source, target) for source, target in pairs]
    acc[...] = jnp.zeros(acc.shape, F32)
    for copy in copies[:3]:
        copy.wait()

    def hide(z):
        hidden_into(h2.at[z % 3], w1, mb2[z])

    def act(z):
        d_act_into(da2.at[z % 2], h2.at[z % 3], w_out, gb2[z])

    def add(z):
        add_sums(acc, mb2[z], da2.at[z % 2], gb2[z], h2.at[z % 3])

    def hide_first(z):
        hidden_into(h0.at[z], w1, mb0[z])

    staggered(mb2.shape[0], hide, act, add, hide_first)
    for copy in copies[3:]:
        copy.wait()


def third_kernel(
    g2, below, above, wall_i, h1, mb1, h0, mb0, acc_i, w_in, w_out, herm_t,
    d_field, sums,
    gx, raw, gp1, g1, raw1, gp0, out0, gb, da, dm, acc,
):
    plane = wall_i.shape[1]
    mid = wall_i.shape[0] - QP
    edge = REACH + 1
    depth = mid - 2 * edge
    ext = depth + 16
    acc[...] = acc_i[...]
    wall_ext = wall_i[0:mid, :]
    open_ext = 1.0 - wall_ext
    wall = wall_i[edge : edge + depth, :]

    for q in range(Q):
        put_rows(raw, q, mid, edge, get_rows(g2, q, depth, 0, depth))
    for d in range(1, REACH + 1):
        put_layer(raw, edge - d, mid, below[(d - 1) * BLOCK : (d - 1) * BLOCK + Q, :])
        put_layer(raw, edge + depth - 1 + d, mid, above[(d - 1) * BLOCK : (d - 1) * BLOCK + Q, :])
    for q in range(Q):
        put_rows(gx, q, ext, 8 - edge, get_rows(raw, q, mid, 0, mid) * open_ext)
    row = REACH * BLOCK
    for n, (k, q) in enumerate(reaching(-1)):
        put_rows(gx, q, ext, 8 - REACH - k, below[row + n : row + n + 1, :])
    for n, (k, q) in enumerate(reaching(1)):
        put_rows(gx, q, ext, 7 + depth + REACH + k, above[row + n : row + n + 1, :])
    for q in range(Q):
        ex, ey, ez = VEL[q]
        moved = roll_plane(get_rows(gx, q, ext, 8 - edge + ez, mid), -ex, -ey)
        put_rows(gp1, q, mid, 0, moved + wall_ext * get_rows(raw, OPP[q], mid, 0, mid))
    clear_pad(gp1, mid)

    total = wall_i[mid : mid + QP, :]
    for i in range(edge, edge + depth):
        total = total + get_layer(gp1, i, mid)

    def act_one(n):
        gb[n % 4] = get_layer(gp1, n + 1, mid).astype(BF)
        d_act_into(da.at[n % 4], h1.at[n], w_out, gb[n % 4])

    def back(n):
        dm[n % 2] = split_concat(dot(w_in[...], da[n % 4]))

    def finish_one(n):
        i = n + 1
        g = (get_layer(gp1, i, mid) + dot(herm_t[...], dm[n % 2]))[:Q]
        put_layer(raw1, i, mid, g)
        put_layer(g1, i, mid, g * open_ext[i : i + 1, :])

    def add_one(n):
        if edge <= n + 1 < edge + depth:
            add_sums(acc, mb1[n], da.at[n % 4], gb[n % 4], h1.at[n])

    staggered(mid - 2, act_one, back, finish_one, add_one)

    for q in range(Q):
        ex, ey, ez = VEL[q]
        moved = roll_plane(get_rows(g1, q, mid, edge + ez, depth), -ex, -ey)
        put_rows(gp0, q, depth, 0, moved + wall * get_rows(raw1, OPP[q], mid, edge, depth))
    clear_pad(gp0, depth)
    for z in range(depth):
        total = total + get_layer(gp0, z, depth)

    def act_two(z):
        gb[z % 4] = get_layer(gp0, z, depth).astype(BF)
        d_act_into(da.at[z % 4], h0.at[z], w_out, gb[z % 4])

    def finish_two(z):
        g = (get_layer(gp0, z, depth) + dot(herm_t[...], dm[z % 2]))[:Q]
        put_layer(out0, z, depth, g)

    def add_two(z):
        add_sums(acc, mb0[z], da.at[z % 4], gb[z % 4], h0.at[z])

    staggered(depth, act_two, back, finish_two, add_two)
    for q in range(Q):
        d_field[q * depth : (q + 1) * depth, :] = get_rows(out0, q, depth, 0, depth)

    sums[0:24, :] = acc[0:24, :]
    sums[24 : 24 + Q + 1, :] = acc[MP : MP + Q + 1, :]
    line = dot_nt(jnp.ones((8, plane), F32), total, lax.Precision.HIGHEST)
    sums[MOM + 1 : MOM + 2, 0:QP] = line[0:1, :]


def last_kernel(scale, core, mine, other, g_w_in, g_b_in, g_w_out, g_b_out):
    first = core[0] == 0
    low = jnp.where(first, mine[...], other[...]) * scale
    high = jnp.where(first, other[...], mine[...]) * scale
    g_w_in[...] = low[:MOM, :]
    g_b_in[...] = low[MOM : MOM + 1, :]
    g_b_out[...] = low[MOM + 1 : MOM + 2, :Q]
    g_w_out[0:8, :] = low[24:, :]
    g_w_out[8:Q, :] = high[: Q - 8, :]


def call(kernel, outs, scratch, args, flops, limit, smem=(), hbm=()):
    vmem = pl.BlockSpec(memory_space=pltpu.VMEM)
    scalars = pl.BlockSpec(memory_space=pltpu.SMEM)
    hbm_spec = pl.BlockSpec(memory_space=pltpu.HBM)
    return pl.pallas_call(
        kernel,
        out_shape=[
            out[2](out[0], out[1]) if len(out) > 2 else jax.ShapeDtypeStruct(*out) for out in outs
        ],
        in_specs=[
            scalars if n in smem else hbm_spec if n in hbm else vmem for n in range(len(args))
        ],
        out_specs=[hbm_spec if len(out) > 2 else vmem for out in outs],
        scratch_shapes=[
            pltpu.VMEM(shape, kind) if kind != "sem" else pltpu.SemaphoreType.DMA(shape)
            for shape, kind in scratch
        ],
        compiler_params=pltpu.CompilerParams(vmem_limit_bytes=limit * MIB),
        cost_estimate=pl.CostEstimate(flops=flops, bytes_accessed=2000000, transcendentals=0),
    )(*args)


def outside(value):
    return pltpu.with_memory_space_constraint(value, pltpu.HBM)


def factor_stages(space, traj):
    core = 2 if space % 2 == 0 else 1
    rest = space // core
    stride = traj * core
    stages = []
    first = [(1, traj)] if traj > 1 else []
    if rest % 2 == 0 and traj <= 2:
        first.append((stride, 2))
        stride, rest = stride * 2, rest // 2
    if first:
        stages.append(first)
    while rest > 1:
        size = next((f for f in (4, 3, 2) if rest % f == 0), rest)
        stages.append([(stride, size)])
        stride, rest = stride * size, rest // size
    return core, stages


def partners(total, digits):
    shifts = [()]
    for _, size in digits:
        shifts = [s + (k,) for s in shifts for k in range(size)]
    result = []
    for shift in shifts[1:]:
        pairs = []
        for index in range(total):
            to = index
            for (stride, size), k in zip(digits, shift):
                digit = index // stride % size
                to += ((digit + k) % size - digit) * stride
            pairs.append((index, to))
        result.append(pairs)
    return result


def per_device(field, solid, cotangent, w_in, b_in, w_out, b_out):
    local, pops, depth, plane = field.shape
    hid = w_in.shape[1]
    space, traj = lax.axis_size("space"), lax.axis_size("traj")
    axes = ("space", "traj")
    up = [(i, (i + 1) % space) for i in range(space)]
    down = [(j, i) for i, j in up]
    herm, herm_t = hermite_operands()
    edge = REACH + 1
    mid, ext = depth + 2 * edge, depth + 16
    work = mid - 2
    half = plane // 2
    field = field.reshape(pops * depth, plane)
    cot = cotangent.reshape(pops * depth, plane)
    solid = solid.reshape(depth, plane)

    def pops_buf(rows, count=QP):
        return ((2, count * rows, half), F32)

    raw = [w_in, b_in.reshape(1, hid), w_out.T, b_out.reshape(1, pops), herm, field, solid, cot]
    raw = [outside(value) for value in raw]
    send_up, send_dn, post, mb0, w1, w_in_p, w2, w_out_p, b_col = call(
        first_kernel,
        [
            ((SEND_ONE, plane), F32),
            ((SEND_ONE, plane), F32),
            pops_buf(depth, Q),
            ((depth, MP, plane), BF, pltpu.HBM),
            ((hid, MP), BF),
            ((MP, hid), BF),
            ((QP, hid), BF),
            ((hid, QP), BF),
            ((QP, plane), F32),
        ],
        [pops_buf(depth), ((MP, hid), F32), ((QP, hid), F32)]
        + [(value.shape, value.dtype) for value in raw]
        + [((2, hid, plane), BF), ((depth, MP, plane), BF), ((len(raw) + 1,), "sem")],
        raw,
        10**9,
        5,
        hbm=range(len(raw)),
    )
    below = lax.ppermute(send_up, "space", up)
    above = lax.ppermute(send_dn, "space", down)
    send_up, send_dn, g2, wall, h1, mb1, mb2, gb2 = call(
        second_kernel,
        [
            ((SEND_TWO, plane), F32),
            ((SEND_TWO, plane), F32),
            pops_buf(depth, Q),
            ((mid + QP, plane), F32),
            ((work, hid, plane), BF, pltpu.HBM),
            ((work, MP, plane), BF, pltpu.HBM),
            ((depth, MP, plane), BF, pltpu.HBM),
            ((depth, QP, plane), BF, pltpu.HBM),
        ],
        [
            pops_buf(ext), pops_buf(mid), pops_buf(mid), pops_buf(depth), pops_buf(mid), pops_buf(depth),
            ((work, hid, plane), BF), ((work, MP, plane), BF), ((depth, MP, plane), BF),
            ((depth, QP, plane), BF), ((2, hid, plane), BF), ((2, hid, plane), BF),
            ((2, 3 * MP, plane), BF), ((work + 3,), "sem"),
        ],
        [post, below, above, cot, solid, w1, w_in_p, w2, w_out_p, b_col, herm, herm_t],
        10**9,
        12,
    )
    below = lax.ppermute(send_up, "space", up)
    above = lax.ppermute(send_dn, "space", down)
    acc, h0, mb0, h1, mb1 = call(
        sums_kernel,
        [
            ((MP + QP, hid), F32),
            ((depth, hid, plane), BF), ((depth, MP, plane), BF),
            ((work, hid, plane), BF), ((work, MP, plane), BF),
        ],
        [
            ((depth, MP, plane), BF), ((depth, QP, plane), BF),
            ((3, hid, plane), BF), ((2, hid, plane), BF), ((5,), "sem"),
        ],
        [outside(mb2), outside(gb2), outside(mb0), outside(mb1), outside(h1), w1, w_out_p],
        10**9,
        4,
        hbm=range(5),
    )
    d_field, sums = call(
        third_kernel,
        [((pops * depth, plane), F32), ((64, hid), F32)],
        [
            pops_buf(ext), pops_buf(mid), pops_buf(mid), pops_buf(mid), pops_buf(mid), pops_buf(depth),
            pops_buf(depth), ((4, QP, plane), BF),
            ((4, hid, plane), BF), ((2, 3 * MP, plane), BF), ((MP + QP, hid), F32),
        ],
        [g2, below, above, wall, h1, mb1, h0, mb0, acc, w_in_p, w_out_p, herm_t],
        10**9,
        9,
    )

    core, stages = factor_stages(space, traj)
    total = space * traj
    me = lax.axis_index("space") % core
    swap = partners(total, [(traj, core)])[0]
    rows = sums.shape[0] // 2
    mine = lax.dynamic_slice_in_dim(sums, me * rows, rows, 0)
    other = lax.dynamic_slice_in_dim(sums, (1 - me) * rows, rows, 0)
    mine = mine + lax.ppermute(other, axes, swap)
    for digits in stages:
        moved = [lax.ppermute(mine, axes, pairs) for pairs in partners(total, digits)]
        for value in moved:
            mine = mine + value
    other = lax.ppermute(mine, axes, swap)

    cells = traj * local * space * depth * plane * STEPS
    scale = 1.0 / math.sqrt(float(cells))
    g_w_in, g_b_in, g_w_out, g_b_out = call(
        lambda *refs: last_kernel(scale, *refs),
        [((MOM, hid), F32), ((1, hid), F32), ((pops, hid), F32), ((1, pops), F32)],
        [],
        [me.reshape(1).astype(jnp.int32), mine, other],
        10**9,
        1,
        smem=(0,),
    )
    return (
        d_field.reshape(local, pops, depth, plane),
        g_w_in,
        g_b_in.reshape(hid),
        g_w_out.T,
        g_b_out.reshape(pops),
    )


def solution(mesh):
    return jax.shard_map(
        per_device,
        mesh=mesh,
        in_specs=(
            P("traj", None, "space", None),
            P("traj", "space", None),
            P("traj", None, "space", None),
            P(),
            P(),
            P(),
            P(),
        ),
        out_specs=(P("traj", None, "space", None), P(), P(), P(), P()),
        check_vma=False,
    )
```

```python
import math

import jax
import jax.numpy as jnp
import numpy as np
from jax import lax
from jax.experimental import pallas as pl
from jax.experimental.pallas import tpu as pltpu
from jax.sharding import PartitionSpec as P

STEPS = 3
NX = 16
NY = 16
Q = 39
QP = 48
MOM = 20
MP = 32
REACH = 3
BLOCK = 40
CHUNK = 128
MIB = 1024 * 1024
BF = jnp.bfloat16
F32 = jnp.float32


def velocity_table():
    rows = [(0, 0, 0)]
    for axis_one in range(3):
        for sign in (1, -1):
            entry = [0, 0, 0]
            entry[axis_one] = sign
            rows.append(tuple(entry))
    for along_x in (1, -1):
        for along_y in (1, -1):
            for along_z in (1, -1):
                rows.append((along_x, along_y, along_z))
    for axis_one in range(3):
        for sign in (1, -1):
            entry = [0, 0, 0]
            entry[axis_one] = 2 * sign
            rows.append(tuple(entry))
    for first, second in ((0, 1), (0, 2), (1, 2)):
        for sign_one in (2, -2):
            for sign_two in (2, -2):
                entry = [0, 0, 0]
                entry[first] = sign_one
                entry[second] = sign_two
                rows.append(tuple(entry))
    for axis_one in range(3):
        for sign in (1, -1):
            entry = [0, 0, 0]
            entry[axis_one] = 3 * sign
            rows.append(tuple(entry))
    return rows


def opposite_index(velocity):
    return [velocity.index((-row[0], -row[1], -row[2])) for row in velocity]


def hermite_table(velocity):
    sound = 2.0 / 3.0
    ident = [[1.0 if a == b else 0.0 for b in range(3)] for a in range(3)]
    speed = [[float(v) for v in row] for row in velocity]
    rows = [[1.0 for row in speed]]
    for first in range(3):
        rows.append([row[first] for row in speed])
    for first in range(3):
        for second in range(first, 3):
            rows.append([row[first] * row[second] - sound * ident[first][second] for row in speed])
    for first in range(3):
        for second in range(first, 3):
            for third in range(second, 3):
                rows.append(
                    [
                        row[first] * row[second] * row[third]
                        - sound
                        * (
                            row[first] * ident[second][third]
                            + row[second] * ident[first][third]
                            + row[third] * ident[first][second]
                        )
                        for row in speed
                    ]
                )
    normed = []
    for values in rows:
        length = math.sqrt(sum((v * v for v in values)))
        normed.append([v / length for v in values])
    return np.asarray(normed, np.float32)


VEL = velocity_table()
OPP = opposite_index(VEL)
HERM = hermite_table(VEL)


def reaching(sign):
    return [(k, q) for k in range(1, REACH + 1) for q in range(Q) if sign * VEL[q][2] >= k]


N_REACH = len(reaching(1))
SEND_ONE = REACH * BLOCK + 2 * N_REACH + REACH + 1
SEND_TWO = REACH * BLOCK + N_REACH + 6


def split_hi_lo(table):
    hi = table.astype(BF)
    lo = (table - np.asarray(hi, np.float32)).astype(BF)
    return hi, lo


def hermite_operands():
    wide = np.zeros((MP, QP), np.float32)
    wide[:MOM, :Q] = HERM
    hi, lo = split_hi_lo(wide)
    forward = np.concatenate([hi, hi, lo], axis=1)
    hi, lo = split_hi_lo(np.ascontiguousarray(wide.T))
    backward = np.concatenate([hi, hi, lo], axis=1)
    return jnp.asarray(forward), jnp.asarray(backward)


def dot(a, b):
    return jnp.dot(a, b, preferred_element_type=F32)


def dot_nt(a, b, precision=None):
    return lax.dot_general(
        a, b, (((1,), (1,)), ((), ())), preferred_element_type=F32, precision=precision
    )


def halves(value):
    lanes = value.shape[1] // 2
    return value[:, :lanes], value[:, lanes:]


def get_layer(buf, layer, stride, count=QP):
    return jnp.concatenate([buf[half, pl.ds(layer, count, stride=stride), :] for half in (0, 1)], axis=1)


def put_layer(buf, layer, stride, value):
    count = value.shape[0]
    for half, part in enumerate(halves(value)):
        buf[half, pl.ds(layer, count, stride=stride), :] = part


def get_rows(buf, q, stride, first, count):
    start = q * stride + first
    return jnp.concatenate([buf[half, start : start + count, :] for half in (0, 1)], axis=1)


def put_rows(buf, q, stride, first, value):
    start = q * stride + first
    for half, part in enumerate(halves(value)):
        buf[half, start : start + value.shape[0], :] = part


def clear_pad(buf, stride):
    lanes = buf.shape[2]
    for half in (0, 1):
        buf[half, Q * stride : QP * stride, :] = jnp.zeros(((QP - Q) * stride, lanes), F32)


def roll_plane(value, along_x, along_y):
    lanes = value.shape[1]
    shift = NY * along_x + along_y

    def turned(by):
        by = by % lanes
        return value if by == 0 else pltpu.roll(value, by, 1)

    if along_y == 0:
        return turned(shift)
    column = lax.broadcasted_iota(jnp.int32, value.shape, 1) % NY
    if along_y > 0:
        return jnp.where(column < along_y, turned(shift - NY), turned(shift))
    return jnp.where(column >= NY + along_y, turned(shift + NY), turned(shift))


def split_concat(value):
    hi = value.astype(BF)
    lo = (value - hi.astype(F32)).astype(BF)
    return jnp.concatenate([hi, lo, hi], axis=0)


def moments_of(x, herm):
    moments = dot(herm, split_concat(x))
    row = lax.broadcasted_iota(jnp.int32, moments.shape, 0)
    ones = jnp.where((row >= MOM) & (row < MOM + 3), 1.0, 0.0)
    return (moments + ones).astype(BF)


def hidden_into(h, w1, mb):
    for start in range(0, w1.shape[0], CHUNK):
        act = dot(w1[start : start + CHUNK, :], mb)
        h[start : start + CHUNK, :] = jnp.tanh(act).astype(BF)


def d_act_into(da, h, w_out, gb):
    for start in range(0, w_out.shape[0], CHUNK):
        d_hidden = dot(w_out[start : start + CHUNK, :], gb)
        hidden = h[start : start + CHUNK, :].astype(F32)
        da[start : start + CHUNK, :] = (d_hidden * (1.0 - hidden * hidden)).astype(BF)


def staggered(count, *stages):
    for turn in range(count + len(stages) - 1):
        for late, stage in enumerate(stages):
            if 0 <= turn - late < count:
                stage(turn - late)


def add_sums(acc, mb, da, gb, h):
    acc[0:MP, :] += dot_nt(mb, da[...])
    acc[MP : MP + QP, :] += dot_nt(gb, h[...])


class Copies:
    def __init__(self, sems):
        self.sems, self.used, self.open = sems, 0, []

    def start(self, source, target):
        copy = pltpu.make_async_copy(source, target, self.sems.at[self.used])
        self.used += 1
        copy.start()
        self.open.append(copy)
        return copy

    def wait(self):
        for copy in self.open:
            copy.wait()
        self.open = []


def first_kernel(
    core, w_in_h, b_in_h, w_out_h, b_out_h, herm_h, field_h, solid_h, cot_h,
    send_on, send_off, post, mb0_h, w1_o, w2_o, b_col_o,
    state, wide, tall, w_in, b_in, w_out, b_out, herm, field, solid, cot, h, mb0, ways, sems,
):
    send_up, send_dn = ways.at[0], ways.at[1]
    sources = (w_in_h, b_in_h, w_out_h, b_out_h, herm_h, field_h, solid_h, cot_h)
    targets = (w_in, b_in, w_out, b_out, herm, field, solid, cot)
    moves = Copies(sems)
    copies = [moves.start(a, b) for a, b in zip(sources, targets)]
    moves.open = []
    depth, plane = solid.shape
    hid = w_in.shape[1]
    for copy in copies[:4]:
        copy.wait()
    wide[...] = jnp.zeros(wide.shape, F32)
    wide[:MOM, :] = w_in[...].astype(F32)
    rest = b_in[...]
    for part in range(3):
        piece = rest.astype(BF).astype(F32)
        wide[MOM + part : MOM + part + 1, :] = piece
        rest = rest - piece
    w1_o[...] = wide[...].T.astype(BF)
    tall[...] = jnp.zeros(tall.shape, F32)
    tall[:Q, :] = w_out[...].astype(F32)
    w2_o[...] = tall[...].astype(BF)
    tall[0:8, :] = jnp.zeros((8, hid), F32)
    tall[0:1, 0:Q] = b_out[...]
    column = tall[0:8, 0:128].T
    b_col_o[...] = jnp.broadcast_to(column[:QP, 0:1], (QP, plane))

    for copy in copies[4:6]:
        copy.wait()
    for q in range(Q):
        put_rows(state, q, depth, 0, field[q * depth : (q + 1) * depth, :])
    clear_pad(state, depth)
    for z in range(depth):
        mb0[z] = moments_of(get_layer(state, z, depth), herm[...])
    moves.start(mb0, mb0_h)

    def hide(z):
        hidden_into(h.at[z], w1_o, mb0[z])

    def finish(z):
        out = get_layer(state, z, depth) + dot(w2_o[...], h[z]) + b_col_o[...]
        out = out[:Q]
        put_layer(post, z, depth, out)
        if z < REACH:
            send_dn[z * BLOCK : z * BLOCK + Q, :] = out
        if depth - 1 - z < REACH:
            d = depth - 1 - z
            send_up[d * BLOCK : d * BLOCK + Q, :] = out

    staggered(depth, hide, finish)
    for copy in copies[6:]:
        copy.wait()
    wall = solid[...].astype(F32)
    for sign, send in ((1, send_up), (-1, send_dn)):
        layer = (lambda d: depth - d) if sign > 0 else (lambda d: d - 1)
        row = REACH * BLOCK
        for k, q in reaching(sign):
            send[row : row + 1, :] = get_rows(post, q, depth, layer(REACH + k), 1)
            row += 1
        for k, q in reaching(-sign):
            z = layer(k)
            at = q * depth + z
            send[row : row + 1, :] = cot[at : at + 1, :] * (1.0 - wall[z : z + 1, :])
            row += 1
        for d in range(1, REACH + 1):
            send[row : row + 1, :] = wall[layer(d) : layer(d) + 1, :]
            row += 1
    send_on[...] = ways[core[0]]
    send_off[...] = ways[1 - core[0]]
    moves.wait()


def between_kernel(
    w_in_h, w_out_h, mb0_h, w1, h0_h, w_in_o, w_out_o, w_in, w_out, mb0, h0, wide, tall, sems
):
    moves = Copies(sems)
    copies = [moves.start(a, b) for a, b in ((mb0_h, mb0), (w_in_h, w_in), (w_out_h, w_out))]
    moves.open = []
    copies[0].wait()
    for z in range(mb0.shape[0]):
        hidden_into(h0.at[z], w1, mb0[z])
        moves.start(h0.at[z], h0_h.at[z])
    for copy in copies[1:]:
        copy.wait()
    wide[...] = jnp.zeros(wide.shape, F32)
    wide[:MOM, :] = w_in[...].astype(F32)
    w_in_o[...] = wide[...].astype(BF)
    tall[...] = jnp.zeros(tall.shape, F32)
    tall[:Q, :] = w_out[...].astype(F32)
    w_out_o[...] = tall[...].T.astype(BF)
    moves.wait()


def by_side(core, run):
    for place, side in ((0, 1), (1, -1)):
        pl.when(core[0] == place)(lambda side=side: run(side))


def near_layers(side, depth):
    edge = REACH + 1
    return (edge + REACH, 2 * edge + depth - 1) if side > 0 else (1, edge + depth - REACH)


def far_layers(side, depth):
    edge = REACH + 1
    return (1, edge + REACH) if side > 0 else (edge + depth - REACH, 2 * edge + depth - 1)


def fill_wall(wall, solid, below, above):
    depth = solid.shape[0]
    edge = REACH + 1
    wall[...] = jnp.zeros(wall.shape, F32)
    wall[edge : edge + depth, :] = solid[...].astype(F32)
    row = REACH * BLOCK + 2 * N_REACH
    for d in range(1, REACH + 1):
        if below is not None:
            wall[edge - d : edge - d + 1, :] = below[row + d - 1 : row + d, :]
        if above is not None:
            wall[edge + depth + d - 1 : edge + depth + d, :] = above[row + d - 1 : row + d, :]


def fill_blocks(buf, zero_row, stride, below, above, depth):
    for d in range(1, REACH + 1):
        rows = slice((d - 1) * BLOCK, (d - 1) * BLOCK + Q)
        if below is not None:
            put_layer(buf, zero_row - d, stride, below[rows, :])
        if above is not None:
            put_layer(buf, zero_row + depth - 1 + d, stride, above[rows, :])


def fill_single(buf, zero_row, stride, below, above, depth, row, sign, beyond):
    if below is not None:
        for n, (k, q) in enumerate(reaching(sign)):
            put_rows(buf, q, stride, zero_row - beyond - k, below[row + n : row + n + 1, :])
    if above is not None:
        for n, (k, q) in enumerate(reaching(-sign)):
            put_rows(buf, q, stride, zero_row + depth - 1 + beyond + k, above[row + n : row + n + 1, :])


def fill_post(p0, post, below, above, depth):
    ext = depth + 16
    for q in range(Q):
        put_rows(p0, q, ext, 8, get_rows(post, q, depth, 0, depth))
    fill_blocks(p0, 8, ext, below, above, depth)
    fill_single(p0, 8, ext, below, above, depth, REACH * BLOCK, 1, REACH)


def stream_post(target, rows, p0, wall, base, depth):
    ext = depth + 16
    start = 8 - REACH - 1 + base
    solid = wall[base : base + rows, :] > 0.5
    for q in range(Q):
        ex, ey, ez = VEL[q]
        moved = roll_plane(get_rows(p0, q, ext, start - ez, rows), ex, ey)
        bounced = get_rows(p0, OPP[q], ext, start, rows)
        put_rows(target, q, rows, 0, jnp.where(solid, bounced, moved))
    clear_pad(target, rows)


def collide_layers(first, last, s1, rows, base, p1, h1, mb1, w1, w2, b_col, herm, after):
    def moments(n):
        mb1[n] = moments_of(get_layer(s1, first + n - base, rows), herm[...])

    def hide(n):
        hidden_into(h1.at[n], w1, mb1[n])
        after(n)

    def finish(n):
        out = get_layer(s1, first + n - base, rows) + dot(w2[...], h1[n]) + b_col[...]
        p1(first + n, out[:Q])

    staggered(last - first, moments, hide, finish)


def near_kernel(
    core, post, on, solid, w1, w2, b_col, herm,
    p1, h1_h, mb1_h,
    p0, s1, wall, h1, mb1, sems,
):
    depth = solid.shape[0]
    mid = depth + 2 * REACH + 2
    count = h1.shape[0]
    copies = [pltpu.make_async_copy(h1.at[n], h1_h.at[n], sems.at[n]) for n in range(count)]
    last_copy = pltpu.make_async_copy(mb1, mb1_h, sems.at[count])

    def run(side):
        below, above = (None, on) if side > 0 else (on, None)
        fill_wall(wall, solid, below, above)
        fill_post(p0, post, below, above, depth)
        stream_post(s1, mid, p0, wall, 0, depth)
        first, last = near_layers(side, depth)
        collide_layers(
            first, last, s1, mid, 0, lambda i, out: put_layer(p1, i, mid, out),
            h1, mb1, w1, w2, b_col, herm, lambda n: copies[n].start(),
        )

    by_side(core, run)
    last_copy.start()
    for copy in copies:
        copy.wait()
    last_copy.wait()


def second_kernel(
    core, post, on, off, cot, solid, p1_near, w1, w_in, w2, w_out, b_col, herm, herm_t,
    send_on, send_off, g2, wall_o, h1_h, mb1_h, mb2_h, gb2_h,
    p0, s1, p1, s2, gx, gp2, h1, mb1, mb2, gb2, h2, da2, dm, ways, sems,
):
    moves = Copies(sems)
    send_up, send_dn = ways.at[0], ways.at[1]
    depth, plane = solid.shape
    edge = REACH + 1
    mid = depth + 2 * edge
    some = s1.shape[1] // QP
    wall_ext = wall_o.at[0:mid, :]
    for q in range(Q):
        put_rows(p1, q, mid, 0, get_rows(p1_near, q, mid, 0, mid))

    def run(side):
        below, above = (off, on) if side > 0 else (on, off)
        fill_wall(wall_ext, solid, below, above)
        fill_post(p0, post, below, above, depth)
        base = 0 if side > 0 else mid - some
        stream_post(s1, some, p0, wall_ext, base, depth)
        first, last = far_layers(side, depth)
        collide_layers(
            first, last, s1, some, base, lambda i, out: put_layer(p1, i, mid, out),
            h1, mb1, w1, w2, b_col, herm, lambda n: None,
        )
        for q in range(Q):
            put_rows(gx, q, mid, edge, cot[q * depth : (q + 1) * depth, :] * (1.0 - wall_o[edge : edge + depth, :]))
        fill_single(gx, edge, mid, below, above, depth, REACH * BLOCK + N_REACH, -1, 0)

    by_side(core, run)
    moves.start(h1, h1_h)
    moves.start(mb1, mb1_h)
    wall = wall_o[edge : edge + depth, :]

    for q in range(Q):
        ex, ey, ez = VEL[q]
        moved = roll_plane(get_rows(p1, q, mid, edge - ez, depth), ex, ey)
        bounced = get_rows(p1, OPP[q], mid, edge, depth)
        put_rows(s2, q, depth, 0, jnp.where(wall > 0.5, bounced, moved))
    clear_pad(s2, depth)
    for q in range(Q):
        ex, ey, ez = VEL[q]
        moved = roll_plane(get_rows(gx, q, mid, edge + ez, depth), -ex, -ey)
        at = OPP[q] * depth
        put_rows(gp2, q, depth, 0, moved + wall * cot[at : at + depth, :])
    clear_pad(gp2, depth)

    total = jnp.zeros((QP, plane), F32)
    for z in range(depth):
        mb2[z] = moments_of(get_layer(s2, z, depth), herm[...])
        gp = get_layer(gp2, z, depth)
        gb2[z] = gp.astype(BF)
        total = total + gp
    wall_o[mid : mid + QP, :] = total
    moves.start(mb2, mb2_h)
    moves.start(gb2, gb2_h)

    def hide_two(z):
        hidden_into(h2.at[z], w1, mb2[z])

    def act(z):
        d_act_into(da2.at[z], h2.at[z], w_out, gb2[z])

    def back(z):
        dm[z] = split_concat(dot(w_in[...], da2[z]))

    def finish_two(z):
        g = (get_layer(gp2, z, depth) + dot(herm_t[...], dm[z]))[:Q]
        put_layer(g2, z, depth, g)
        if z < REACH:
            send_dn[z * BLOCK : z * BLOCK + Q, :] = g
        if depth - 1 - z < REACH:
            d = depth - 1 - z
            send_up[d * BLOCK : d * BLOCK + Q, :] = g

    staggered(depth, hide_two, act, back, finish_two)

    for sign, send in ((1, send_up), (-1, send_dn)):
        row = REACH * BLOCK
        for k, q in reaching(-sign):
            z = depth - REACH - k if sign > 0 else REACH + k - 1
            open_cells = 1.0 - wall_o[edge + z : edge + z + 1, :]
            send[row : row + 1, :] = get_rows(g2, q, depth, z, 1) * open_cells
            row += 1
    send_on[...] = ways[core[0]]
    send_off[...] = ways[1 - core[0]]
    moves.wait()


def fill_g2(raw, gx, g2, open_ext, below, above, depth):
    edge = REACH + 1
    mid, ext = depth + 2 * edge, depth + 16
    for q in range(Q):
        put_rows(raw, q, mid, edge, get_rows(g2, q, depth, 0, depth))
    fill_blocks(raw, edge, mid, below, above, depth)
    for q in range(Q):
        put_rows(gx, q, ext, 8 - edge, get_rows(raw, q, mid, 0, mid) * open_ext)
    fill_single(gx, 8, ext, below, above, depth, REACH * BLOCK, -1, REACH)


def stream_g2(target, rows, raw, gx, wall, base, depth):
    edge = REACH + 1
    mid, ext = depth + 2 * edge, depth + 16
    solid = wall[base : base + rows, :]
    for q in range(Q):
        ex, ey, ez = VEL[q]
        moved = roll_plane(get_rows(gx, q, ext, 8 - edge + base + ez, rows), -ex, -ey)
        put_rows(target, q, rows, 0, moved + solid * get_rows(raw, OPP[q], mid, base, rows))
    clear_pad(target, rows)


def adjoint_layers(first, last, depth, gp1, rows, base, raw1, g1, wall, h, mb, acc, gb, da, dm, w_in, w_out, herm_t):
    edge = REACH + 1
    mid = depth + 2 * edge

    def act(n):
        gb[n] = get_layer(gp1, first + n - base, rows).astype(BF)
        d_act_into(da.at[n], h.at[n], w_out, gb[n])

    def back(n):
        dm[n] = split_concat(dot(w_in[...], da[n]))

    def finish(n):
        i = first + n
        g = (get_layer(gp1, i - base, rows) + dot(herm_t[...], dm[n]))[:Q]
        put_layer(raw1, i, mid, g)
        put_layer(g1, i, mid, g * (1.0 - wall[i : i + 1, :]))

    def add(n):
        if edge <= first + n < edge + depth:
            add_sums(acc, mb[n], da.at[n], gb[n], h.at[n])

    staggered(last - first, act, back, finish, add)


def third_near_kernel(
    core, g2, on, wall, w1, w_in, w_out, herm_t,
    mb2_h, gb2_h, mb_near_h, h_near_h, mb_far_h, h_far_h, mb0_h, h0_h,
    raw1, g1, acc, total_o, mb_far, h_far, mb0, h0,
    gx, raw, gp1, gb, da, dm, h2, mb2, gb2, mb_near, h_near, sems,
):
    edge = REACH + 1
    mid = wall.shape[0] - QP
    depth = mid - 2 * edge
    moves = Copies(sems)
    sources = (mb2_h, gb2_h, mb_near_h, h_near_h, mb_far_h, h_far_h, mb0_h, h0_h)
    targets = (mb2, gb2, mb_near, h_near, mb_far, h_far, mb0, h0)
    pairs = list(zip(sources, targets))
    copies = [moves.start(source, target) for source, target in pairs[:2]]
    acc[...] = jnp.zeros(acc.shape, F32)

    def stream(side):
        below, above = (None, on) if side > 0 else (on, None)
        fill_g2(raw, gx, g2, 1.0 - wall[0:mid, :], below, above, depth)
        stream_g2(gp1, mid, raw, gx, wall, 0, depth)

    by_side(core, stream)
    for copy in copies[:2]:
        copy.wait()
    copies += [moves.start(source, target) for source, target in pairs[2:4]]

    def hide(z):
        hidden_into(h2.at[z], w1, mb2[z])

    def act(z):
        d_act_into(da.at[z], h2.at[z], w_out, gb2[z])

    def add(z):
        add_sums(acc, mb2[z], da.at[z], gb2[z], h2.at[z])

    staggered(depth, hide, act, add)
    for copy in copies[2:4]:
        copy.wait()
    copies += [moves.start(source, target) for source, target in pairs[4:]]

    def run(side):
        first, last = near_layers(side, depth)
        total = wall[mid : mid + QP, :]
        for i in range(max(first, edge), min(last, edge + depth)):
            total = total + get_layer(gp1, i, mid)
        total_o[...] = total
        adjoint_layers(
            first, last, depth, gp1, mid, 0, raw1, g1, wall, h_near, mb_near, acc, gb, da, dm,
            w_in, w_out, herm_t,
        )

    by_side(core, run)
    for copy in copies[4:]:
        copy.wait()


def third_kernel(
    core, g2, on, off, wall_i, h1, mb1, h0, mb0, raw_near, g_near, acc_i, total_i, w_in, w_out, herm_t,
    sums, da0_h, gp0_h,
    gx, raw, gp1, g1, raw1, gp0, gb, da, dm, acc, total_s, sems,
):
    moves = Copies(sems)
    plane = wall_i.shape[1]
    mid = wall_i.shape[0] - QP
    edge = REACH + 1
    depth = mid - 2 * edge
    some = gp1.shape[1] // QP
    acc[...] = acc_i[...]
    for q in range(Q):
        put_rows(raw1, q, mid, 0, get_rows(raw_near, q, mid, 0, mid))
        put_rows(g1, q, mid, 0, get_rows(g_near, q, mid, 0, mid))

    def run(side):
        below, above = (off, on) if side > 0 else (on, off)
        fill_g2(raw, gx, g2, 1.0 - wall_i[0:mid, :], below, above, depth)
        base = 0 if side > 0 else mid - some
        stream_g2(gp1, some, raw, gx, wall_i, base, depth)
        first, last = far_layers(side, depth)
        total = total_i[...]
        for i in range(max(first, edge), min(last, edge + depth)):
            total = total + get_layer(gp1, i - base, some)
        total_s[...] = total
        adjoint_layers(
            first, last, depth, gp1, some, base, raw1, g1, wall_i, h1, mb1, acc, gb, da, dm, w_in, w_out, herm_t
        )

    by_side(core, run)
    wall = wall_i[edge : edge + depth, :]
    total = total_s[...]
    for q in range(Q):
        ex, ey, ez = VEL[q]
        moved = roll_plane(get_rows(g1, q, mid, edge + ez, depth), -ex, -ey)
        put_rows(gp0, q, depth, 0, moved + wall * get_rows(raw1, OPP[q], mid, edge, depth))
    clear_pad(gp0, depth)
    moves.start(gp0, gp0_h)
    for z in range(depth):
        total = total + get_layer(gp0, z, depth)

    def act_two(z):
        gb[z] = get_layer(gp0, z, depth).astype(BF)
        d_act_into(da.at[z], h0.at[z], w_out, gb[z])
        moves.start(da.at[z], da0_h.at[z])

    def add_two(z):
        add_sums(acc, mb0[z], da.at[z], gb[z], h0.at[z])

    staggered(depth, act_two, add_two)
    sums[0:24, :] = acc[0:24, :]
    sums[24 : 24 + Q + 1, :] = acc[MP : MP + Q + 1, :]
    line = dot_nt(jnp.ones((8, plane), F32), total, lax.Precision.HIGHEST)
    sums[MOM + 1 : MOM + 2, 0:QP] = line[0:1, :]
    moves.wait()


def field_kernel(after, da0_h, gp0_h, w_in, herm_t, d_field, da0, gp0, out0, dm, sems):
    del after
    depth = da0.shape[0]
    moves = Copies(sems)
    copies = [moves.start(gp0_h, gp0)] + [moves.start(da0_h.at[z], da0.at[z]) for z in range(depth)]

    def back(z):
        copies[z + 1].wait()
        dm[z] = split_concat(dot(w_in[...], da0[z]))

    def finish(z):
        g = (get_layer(gp0, z, depth) + dot(herm_t[...], dm[z]))[:Q]
        put_layer(out0, z, depth, g)

    copies[0].wait()
    staggered(depth, back, finish)
    for q in range(Q):
        d_field[q * depth : (q + 1) * depth, :] = get_rows(out0, q, depth, 0, depth)


def last_kernel(scale, core, mine, other, g_w_in, g_b_in, g_w_out, g_b_out):
    first = core[0] == 0
    low = jnp.where(first, mine[...], other[...]) * scale
    high = jnp.where(first, other[...], mine[...]) * scale
    g_w_in[...] = low[:MOM, :]
    g_b_in[...] = low[MOM : MOM + 1, :]
    g_b_out[...] = low[MOM + 1 : MOM + 2, :Q]
    g_w_out[0:8, :] = low[24:, :]
    g_w_out[8:Q, :] = high[: Q - 8, :]


def call(kernel, outs, scratch, args, flops, limit, smem=(), hbm=()):
    vmem = pl.BlockSpec(memory_space=pltpu.VMEM)
    scalars = pl.BlockSpec(memory_space=pltpu.SMEM)
    hbm_spec = pl.BlockSpec(memory_space=pltpu.HBM)
    return pl.pallas_call(
        kernel,
        out_shape=[
            out[2](out[0], out[1]) if len(out) > 2 else jax.ShapeDtypeStruct(*out) for out in outs
        ],
        in_specs=[
            scalars if n in smem else hbm_spec if n in hbm else vmem for n in range(len(args))
        ],
        out_specs=[hbm_spec if len(out) > 2 else vmem for out in outs],
        scratch_shapes=[
            pltpu.VMEM(shape, kind) if kind != "sem" else pltpu.SemaphoreType.DMA(shape)
            for shape, kind in scratch
        ],
        compiler_params=pltpu.CompilerParams(vmem_limit_bytes=limit * MIB),
        cost_estimate=pl.CostEstimate(flops=flops, bytes_accessed=2000000, transcendentals=0),
    )(*args)


def outside(value):
    return pltpu.with_memory_space_constraint(value, pltpu.HBM)


def factor_stages(space, traj):
    core = 2 if space % 2 == 0 else 1
    rest = space // core
    stride = traj * core
    stages = []
    first = [(1, traj)] if traj > 1 else []
    if rest % 2 == 0 and traj <= 2:
        first.append((stride, 2))
        stride, rest = stride * 2, rest // 2
    if first:
        stages.append(first)
    while rest > 1:
        size = next((f for f in (4, 3, 2) if rest % f == 0), rest)
        stages.append([(stride, size)])
        stride, rest = stride * size, rest // size
    return core, stages


def partners(total, digits):
    shifts = [()]
    for _, size in digits:
        shifts = [s + (k,) for s in shifts for k in range(size)]
    result = []
    for shift in shifts[1:]:
        pairs = []
        for index in range(total):
            to = index
            for (stride, size), k in zip(digits, shift):
                digit = index // stride % size
                to += ((digit + k) % size - digit) * stride
            pairs.append((index, to))
        result.append(pairs)
    return result


def per_device(field, solid, cotangent, w_in, b_in, w_out, b_out):
    local, pops, depth, plane = field.shape
    hid = w_in.shape[1]
    space, traj = lax.axis_size("space"), lax.axis_size("traj")
    axes = ("space", "traj")
    chip = [(i, i + 1 - 2 * (i % 2)) for i in range(space)]
    next_chip = [(i, (i - 1 + 2 * (i % 2)) % space) for i in range(space)]
    place = lax.axis_index("space") % 2
    core_id = place.reshape(1).astype(jnp.int32)
    herm, herm_t = hermite_operands()
    edge = REACH + 1
    mid, ext = depth + 2 * edge, depth + 16
    near, far, some = depth, 2 * REACH, 8
    half = plane // 2
    field = field.reshape(pops * depth, plane)
    cot = cotangent.reshape(pops * depth, plane)
    solid = solid.reshape(depth, plane)

    def pops_buf(rows, count=QP):
        return ((2, count * rows, half), F32)

    raw = [w_in, b_in.reshape(1, hid), w_out.T, b_out.reshape(1, pops), herm, field, solid, cot]
    raw = [outside(value) for value in raw]
    send_on, send_off, post, mb0, w1, w2, b_col = call(
        first_kernel,
        [
            ((SEND_ONE, plane), F32),
            ((SEND_ONE, plane), F32),
            pops_buf(depth, Q),
            ((depth, MP, plane), BF, pltpu.HBM),
            ((hid, MP), BF),
            ((QP, hid), BF),
            ((QP, plane), F32),
        ],
        [pops_buf(depth), ((MP, hid), F32), ((QP, hid), F32)]
        + [(value.shape, value.dtype) for value in raw]
        + [((depth, hid, plane), BF), ((depth, MP, plane), BF), ((2, SEND_ONE, plane), F32)]
        + [((len(raw) + 1,), "sem")],
        [core_id] + raw,
        10**9,
        7,
        smem=(0,),
        hbm=range(1, len(raw) + 1),
    )
    on = lax.ppermute(send_on, "space", chip)
    off = lax.ppermute(send_off, "space", next_chip)
    h0, w_in_p, w_out_p = call(
        between_kernel,
        [((depth, hid, plane), BF, pltpu.HBM), ((MP, hid), BF), ((hid, QP), BF)],
        [
            (w_in.shape, BF), (w_out.T.shape, BF), ((depth, MP, plane), BF), ((depth, hid, plane), BF),
            ((MP, hid), F32), ((QP, hid), F32), ((depth + 3,), "sem"),
        ],
        [raw[0], raw[2], outside(mb0), w1],
        10**9,
        4,
        hbm=range(3),
    )
    p1, h_near, mb_near = call(
        near_kernel,
        [pops_buf(mid, Q), ((near, hid, plane), BF, pltpu.HBM), ((near, MP, plane), BF, pltpu.HBM)],
        [
            pops_buf(ext), pops_buf(mid), ((mid, plane), F32),
            ((near, hid, plane), BF), ((near, MP, plane), BF), ((near + 1,), "sem"),
        ],
        [core_id, post, on, solid, w1, w2, b_col, herm],
        10**9,
        6,
        smem=(0,),
    )
    send_on, send_off, g2, wall, h_far, mb_far, mb2, gb2 = call(
        second_kernel,
        [
            ((SEND_TWO, plane), F32),
            ((SEND_TWO, plane), F32),
            pops_buf(depth, Q),
            ((mid + QP, plane), F32),
            ((far, hid, plane), BF, pltpu.HBM),
            ((far, MP, plane), BF, pltpu.HBM),
            ((depth, MP, plane), BF, pltpu.HBM),
            ((depth, QP, plane), BF, pltpu.HBM),
        ],
        [
            pops_buf(ext), pops_buf(some), pops_buf(mid), pops_buf(depth), pops_buf(mid), pops_buf(depth),
            ((far, hid, plane), BF), ((far, MP, plane), BF), ((depth, MP, plane), BF),
            ((depth, QP, plane), BF), ((depth, hid, plane), BF), ((depth, hid, plane), BF),
            ((depth, 3 * MP, plane), BF), ((2, SEND_TWO, plane), F32), ((4,), "sem"),
        ],
        [core_id, post, on, off, cot, solid, p1, w1, w_in_p, w2, w_out_p, b_col, herm, herm_t],
        10**9,
        16,
        smem=(0,),
    )
    on = lax.ppermute(send_on, "space", chip)
    off = lax.ppermute(send_off, "space", next_chip)
    saved = [outside(value) for value in (mb2, gb2, mb_near, h_near, mb_far, h_far, mb0, h0)]
    raw_near, g_near, acc, total_g, mb_far, h_far, mb0, h0 = call(
        third_near_kernel,
        [pops_buf(mid, Q), pops_buf(mid, Q), ((MP + QP, hid), F32), ((QP, plane), F32)]
        + [(value.shape, BF) for value in saved[4:]],
        [
            pops_buf(ext), pops_buf(mid), pops_buf(mid), ((depth, QP, plane), BF),
            ((depth, hid, plane), BF), ((depth, 3 * MP, plane), BF), ((depth, hid, plane), BF),
        ]
        + [(value.shape, BF) for value in saved[:4]]
        + [((len(saved),), "sem")],
        [core_id, g2, on, wall, w1, w_in_p, w_out_p, herm_t] + saved,
        10**9,
        14,
        smem=(0,),
        hbm=range(8, 16),
    )
    sums, da0, gp0 = call(
        third_kernel,
        [((64, hid), F32), ((depth, hid, plane), BF, pltpu.HBM), pops_buf(depth) + (pltpu.HBM,)],
        [
            pops_buf(ext), pops_buf(mid), pops_buf(some), pops_buf(mid), pops_buf(mid), pops_buf(depth),
            ((depth, QP, plane), BF), ((depth, hid, plane), BF), ((depth, 3 * MP, plane), BF),
            ((MP + QP, hid), F32), ((QP, plane), F32), ((depth + 1,), "sem"),
        ],
        [
            core_id, g2, on, off, wall, h_far, mb_far, h0, mb0, raw_near, g_near, acc, total_g,
            w_in_p, w_out_p, herm_t,
        ],
        10**9,
        12,
        smem=(0,),
    )

    core, stages = factor_stages(space, traj)
    total = space * traj
    me = lax.axis_index("space") % core
    swap = partners(total, [(traj, core)])[0]
    rows = sums.shape[0] // 2
    mine = lax.dynamic_slice_in_dim(sums, me * rows, rows, 0)
    other = lax.dynamic_slice_in_dim(sums, (1 - me) * rows, rows, 0)
    mine = mine + lax.ppermute(other, axes, swap)
    for digits in stages:
        moved = [lax.ppermute(mine, axes, pairs) for pairs in partners(total, digits)]
        for value in moved:
            mine = mine + value
        if digits is stages[0]:
            (d_field,) = call(
                field_kernel,
                [((pops * depth, plane), F32)],
                [
                    ((depth, hid, plane), BF), pops_buf(depth), pops_buf(depth),
                    ((depth, 3 * MP, plane), BF), ((depth + 1,), "sem"),
                ],
                [mine, outside(da0), outside(gp0), w_in_p, herm_t],
                10**9,
                6,
                hbm=(1, 2),
            )
    mine, d_field = lax.optimization_barrier((mine, d_field))
    other = lax.ppermute(mine, axes, swap)

    cells = traj * local * space * depth * plane * STEPS
    scale = 1.0 / math.sqrt(float(cells))
    g_w_in, g_b_in, g_w_out, g_b_out = call(
        lambda *refs: last_kernel(scale, *refs),
        [((MOM, hid), F32), ((1, hid), F32), ((pops, hid), F32), ((1, pops), F32)],
        [],
        [core_id, mine, other],
        10**9,
        1,
        smem=(0,),
    )
    return (
        d_field.reshape(local, pops, depth, plane),
        g_w_in,
        g_b_in.reshape(hid),
        g_w_out.T,
        g_b_out.reshape(pops),
    )


def solution(mesh):
    return jax.shard_map(
        per_device,
        mesh=mesh,
        in_specs=(
            P("traj", None, "space", None),
            P("traj", "space", None),
            P("traj", None, "space", None),
            P(),
            P(),
            P(),
            P(),
        ),
        out_specs=(P("traj", None, "space", None), P(), P(), P(), P()),
        check_vma=False,
    )
```

```python
import math

import jax
import jax.numpy as jnp
import numpy as np
from jax import lax
from jax.experimental import pallas as pl
from jax.experimental.pallas import tpu as pltpu
from jax.sharding import PartitionSpec as P

STEPS = 3
NX = 16
NY = 16
Q = 39
QP = 48
MOM = 20
MP = 32
REACH = 3
BLOCK = 40
CHUNK = 128
MIB = 1024 * 1024
BF = jnp.bfloat16
F32 = jnp.float32


def velocity_table():
    rows = [(0, 0, 0)]
    for axis_one in range(3):
        for sign in (1, -1):
            entry = [0, 0, 0]
            entry[axis_one] = sign
            rows.append(tuple(entry))
    for along_x in (1, -1):
        for along_y in (1, -1):
            for along_z in (1, -1):
                rows.append((along_x, along_y, along_z))
    for axis_one in range(3):
        for sign in (1, -1):
            entry = [0, 0, 0]
            entry[axis_one] = 2 * sign
            rows.append(tuple(entry))
    for first, second in ((0, 1), (0, 2), (1, 2)):
        for sign_one in (2, -2):
            for sign_two in (2, -2):
                entry = [0, 0, 0]
                entry[first] = sign_one
                entry[second] = sign_two
                rows.append(tuple(entry))
    for axis_one in range(3):
        for sign in (1, -1):
            entry = [0, 0, 0]
            entry[axis_one] = 3 * sign
            rows.append(tuple(entry))
    return rows


def opposite_index(velocity):
    return [velocity.index((-row[0], -row[1], -row[2])) for row in velocity]


def hermite_table(velocity):
    sound = 2.0 / 3.0
    ident = [[1.0 if a == b else 0.0 for b in range(3)] for a in range(3)]
    speed = [[float(v) for v in row] for row in velocity]
    rows = [[1.0 for row in speed]]
    for first in range(3):
        rows.append([row[first] for row in speed])
    for first in range(3):
        for second in range(first, 3):
            rows.append([row[first] * row[second] - sound * ident[first][second] for row in speed])
    for first in range(3):
        for second in range(first, 3):
            for third in range(second, 3):
                rows.append(
                    [
                        row[first] * row[second] * row[third]
                        - sound
                        * (
                            row[first] * ident[second][third]
                            + row[second] * ident[first][third]
                            + row[third] * ident[first][second]
                        )
                        for row in speed
                    ]
                )
    normed = []
    for values in rows:
        length = math.sqrt(sum((v * v for v in values)))
        normed.append([v / length for v in values])
    return np.asarray(normed, np.float32)


VEL = velocity_table()
OPP = opposite_index(VEL)
HERM = hermite_table(VEL)


def reaching(sign):
    return [(k, q) for k in range(1, REACH + 1) for q in range(Q) if sign * VEL[q][2] >= k]


N_REACH = len(reaching(1))
SEND_ONE = REACH * BLOCK + 2 * N_REACH + REACH + 1
SEND_TWO = REACH * BLOCK + N_REACH + 6


def split_hi_lo(table):
    hi = table.astype(BF)
    lo = (table - np.asarray(hi, np.float32)).astype(BF)
    return hi, lo


def hermite_operands():
    wide = np.zeros((MP, QP), np.float32)
    wide[:MOM, :Q] = HERM
    hi, lo = split_hi_lo(wide)
    forward = np.concatenate([hi, hi, lo], axis=1)
    hi, lo = split_hi_lo(np.ascontiguousarray(wide.T))
    backward = np.concatenate([hi, hi, lo], axis=1)
    return jnp.asarray(forward), jnp.asarray(backward)


def dot(a, b):
    return jnp.dot(a, b, preferred_element_type=F32)


def dot_nt(a, b, precision=None):
    return lax.dot_general(
        a, b, (((1,), (1,)), ((), ())), preferred_element_type=F32, precision=precision
    )


def halves(value):
    lanes = value.shape[1] // 2
    return value[:, :lanes], value[:, lanes:]


def get_layer(buf, layer, stride, count=QP):
    return jnp.concatenate([buf[half, pl.ds(layer, count, stride=stride), :] for half in (0, 1)], axis=1)


def put_layer(buf, layer, stride, value):
    count = value.shape[0]
    for half, part in enumerate(halves(value)):
        buf[half, pl.ds(layer, count, stride=stride), :] = part


def get_rows(buf, q, stride, first, count):
    start = q * stride + first
    return jnp.concatenate([buf[half, start : start + count, :] for half in (0, 1)], axis=1)


def put_rows(buf, q, stride, first, value):
    start = q * stride + first
    for half, part in enumerate(halves(value)):
        buf[half, start : start + value.shape[0], :] = part


def clear_pad(buf, stride):
    lanes = buf.shape[2]
    for half in (0, 1):
        buf[half, Q * stride : QP * stride, :] = jnp.zeros(((QP - Q) * stride, lanes), F32)


def roll_plane(value, along_x, along_y):
    lanes = value.shape[1]
    shift = NY * along_x + along_y

    def turned(by):
        by = by % lanes
        return value if by == 0 else pltpu.roll(value, by, 1)

    if along_y == 0:
        return turned(shift)
    column = lax.broadcasted_iota(jnp.int32, value.shape, 1) % NY
    if along_y > 0:
        return jnp.where(column < along_y, turned(shift - NY), turned(shift))
    return jnp.where(column >= NY + along_y, turned(shift + NY), turned(shift))


def split_concat(value):
    hi = value.astype(BF)
    lo = (value - hi.astype(F32)).astype(BF)
    return jnp.concatenate([hi, lo, hi], axis=0)


def moments_of(x, herm):
    moments = dot(herm, split_concat(x))
    row = lax.broadcasted_iota(jnp.int32, moments.shape, 0)
    ones = jnp.where((row >= MOM) & (row < MOM + 3), 1.0, 0.0)
    return (moments + ones).astype(BF)


def hidden_into(h, w1, mb):
    for start in range(0, w1.shape[0], CHUNK):
        act = dot(w1[start : start + CHUNK, :], mb)
        h[start : start + CHUNK, :] = jnp.tanh(act).astype(BF)


def d_act_into(da, h, w_out, gb):
    for start in range(0, w_out.shape[0], CHUNK):
        d_hidden = dot(w_out[start : start + CHUNK, :], gb)
        hidden = h[start : start + CHUNK, :].astype(F32)
        da[start : start + CHUNK, :] = (d_hidden * (1.0 - hidden * hidden)).astype(BF)


def staggered(count, *stages):
    for turn in range(count + len(stages) - 1):
        for late, stage in enumerate(stages):
            if 0 <= turn - late < count:
                stage(turn - late)


def add_sums(acc, mb, da, gb, h):
    acc[0:MP, :] += dot_nt(mb, da[...])
    acc[MP : MP + QP, :] += dot_nt(gb, h[...])


class Copies:
    def __init__(self, sems):
        self.sems, self.used, self.open = sems, 0, []

    def start(self, source, target):
        copy = pltpu.make_async_copy(source, target, self.sems.at[self.used])
        self.used += 1
        copy.start()
        self.open.append(copy)
        return copy

    def wait(self):
        for copy in self.open:
            copy.wait()
        self.open = []


def first_kernel(
    core, w_in_h, b_in_h, w_out_h, b_out_h, herm_h, field_h, solid_h, cot_h,
    send_on, send_off, post, mb0_h, w1_o, w2_o, b_col_o,
    state, wide, tall, w_in, b_in, w_out, b_out, herm, field, solid, cot, h, mb0, ways, sems,
):
    send_up, send_dn = ways.at[0], ways.at[1]
    sources = (w_in_h, b_in_h, w_out_h, b_out_h, herm_h, field_h, solid_h, cot_h)
    targets = (w_in, b_in, w_out, b_out, herm, field, solid, cot)
    moves = Copies(sems)
    copies = [moves.start(a, b) for a, b in zip(sources, targets)]
    moves.open = []
    depth, plane = solid.shape
    hid = w_in.shape[1]
    for copy in copies[:4]:
        copy.wait()
    wide[...] = jnp.zeros(wide.shape, F32)
    wide[:MOM, :] = w_in[...].astype(F32)
    rest = b_in[...]
    for part in range(3):
        piece = rest.astype(BF).astype(F32)
        wide[MOM + part : MOM + part + 1, :] = piece
        rest = rest - piece
    w1_o[...] = wide[...].T.astype(BF)
    tall[...] = jnp.zeros(tall.shape, F32)
    tall[:Q, :] = w_out[...].astype(F32)
    w2_o[...] = tall[...].astype(BF)
    tall[0:8, :] = jnp.zeros((8, hid), F32)
    tall[0:1, 0:Q] = b_out[...]
    column = tall[0:8, 0:128].T
    b_col_o[...] = jnp.broadcast_to(column[:QP, 0:1], (QP, plane))

    for copy in copies[4:6]:
        copy.wait()
    for q in range(Q):
        put_rows(state, q, depth, 0, field[q * depth : (q + 1) * depth, :])
    clear_pad(state, depth)
    for z in range(depth):
        mb0[z] = moments_of(get_layer(state, z, depth), herm[...])
    moves.start(mb0, mb0_h)

    def hide(z):
        hidden_into(h.at[z], w1_o, mb0[z])

    def finish(z):
        out = get_layer(state, z, depth) + dot(w2_o[...], h[z]) + b_col_o[...]
        out = out[:Q]
        put_layer(post, z, depth, out)
        if z < REACH:
            send_dn[z * BLOCK : z * BLOCK + Q, :] = out
        if depth - 1 - z < REACH:
            d = depth - 1 - z
            send_up[d * BLOCK : d * BLOCK + Q, :] = out

    staggered(depth, hide, finish)
    for copy in copies[6:]:
        copy.wait()
    wall = solid[...].astype(F32)
    for sign, send in ((1, send_up), (-1, send_dn)):
        layer = (lambda d: depth - d) if sign > 0 else (lambda d: d - 1)
        row = REACH * BLOCK
        for k, q in reaching(sign):
            send[row : row + 1, :] = get_rows(post, q, depth, layer(REACH + k), 1)
            row += 1
        for k, q in reaching(-sign):
            z = layer(k)
            at = q * depth + z
            send[row : row + 1, :] = cot[at : at + 1, :] * (1.0 - wall[z : z + 1, :])
            row += 1
        for d in range(1, REACH + 1):
            send[row : row + 1, :] = wall[layer(d) : layer(d) + 1, :]
            row += 1
    send_on[...] = ways[core[0]]
    send_off[...] = ways[1 - core[0]]
    moves.wait()


def between_kernel(
    w_in_h, w_out_h, mb0_h, w1, h0_h, w_in_o, w_out_o, w_in, w_out, mb0, h0, wide, tall, sems
):
    moves = Copies(sems)
    copies = [moves.start(a, b) for a, b in ((mb0_h, mb0), (w_in_h, w_in), (w_out_h, w_out))]
    moves.open = []
    copies[0].wait()
    for z in range(mb0.shape[0]):
        hidden_into(h0.at[z], w1, mb0[z])
        moves.start(h0.at[z], h0_h.at[z])
    for copy in copies[1:]:
        copy.wait()
    wide[...] = jnp.zeros(wide.shape, F32)
    wide[:MOM, :] = w_in[...].astype(F32)
    w_in_o[...] = wide[...].astype(BF)
    tall[...] = jnp.zeros(tall.shape, F32)
    tall[:Q, :] = w_out[...].astype(F32)
    w_out_o[...] = tall[...].T.astype(BF)
    moves.wait()


def by_side(core, run):
    for place, side in ((0, 1), (1, -1)):
        pl.when(core[0] == place)(lambda side=side: run(side))


def near_layers(side, depth):
    edge = REACH + 1
    return (edge + REACH, 2 * edge + depth - 1) if side > 0 else (1, edge + depth - REACH)


def far_layers(side, depth):
    edge = REACH + 1
    return (1, edge + REACH) if side > 0 else (edge + depth - REACH, 2 * edge + depth - 1)


def fill_wall(wall, solid, below, above):
    depth = solid.shape[0]
    edge = REACH + 1
    wall[...] = jnp.zeros(wall.shape, F32)
    wall[edge : edge + depth, :] = solid[...].astype(F32)
    row = REACH * BLOCK + 2 * N_REACH
    for d in range(1, REACH + 1):
        if below is not None:
            wall[edge - d : edge - d + 1, :] = below[row + d - 1 : row + d, :]
        if above is not None:
            wall[edge + depth + d - 1 : edge + depth + d, :] = above[row + d - 1 : row + d, :]


def fill_blocks(buf, zero_row, stride, below, above, depth):
    for d in range(1, REACH + 1):
        rows = slice((d - 1) * BLOCK, (d - 1) * BLOCK + Q)
        if below is not None:
            put_layer(buf, zero_row - d, stride, below[rows, :])
        if above is not None:
            put_layer(buf, zero_row + depth - 1 + d, stride, above[rows, :])


def fill_single(buf, zero_row, stride, below, above, depth, row, sign, beyond):
    if below is not None:
        for n, (k, q) in enumerate(reaching(sign)):
            put_rows(buf, q, stride, zero_row - beyond - k, below[row + n : row + n + 1, :])
    if above is not None:
        for n, (k, q) in enumerate(reaching(-sign)):
            put_rows(buf, q, stride, zero_row + depth - 1 + beyond + k, above[row + n : row + n + 1, :])


def fill_post(p0, post, below, above, depth):
    ext = depth + 16
    for q in range(Q):
        put_rows(p0, q, ext, 8, get_rows(post, q, depth, 0, depth))
    fill_blocks(p0, 8, ext, below, above, depth)
    fill_single(p0, 8, ext, below, above, depth, REACH * BLOCK, 1, REACH)


def stream_post(target, rows, p0, wall, base, depth):
    ext = depth + 16
    start = 8 - REACH - 1 + base
    solid = wall[base : base + rows, :] > 0.5
    for q in range(Q):
        ex, ey, ez = VEL[q]
        moved = roll_plane(get_rows(p0, q, ext, start - ez, rows), ex, ey)
        bounced = get_rows(p0, OPP[q], ext, start, rows)
        put_rows(target, q, rows, 0, jnp.where(solid, bounced, moved))
    clear_pad(target, rows)


def collide_layers(first, last, s1, rows, base, p1, h1, mb1, w1, w2, b_col, herm, after):
    def moments(n):
        mb1[n] = moments_of(get_layer(s1, first + n - base, rows), herm[...])

    def hide(n):
        hidden_into(h1.at[n], w1, mb1[n])
        after(n)

    def finish(n):
        out = get_layer(s1, first + n - base, rows) + dot(w2[...], h1[n]) + b_col[...]
        p1(first + n, out[:Q])

    staggered(last - first, moments, hide, finish)


def near_kernel(
    core, post, on, solid, w1, w2, b_col, herm,
    p1, h1_h, mb1_h,
    p0, s1, wall, h1, mb1, sems,
):
    depth = solid.shape[0]
    mid = depth + 2 * REACH + 2
    count = h1.shape[0]
    copies = [pltpu.make_async_copy(h1.at[n], h1_h.at[n], sems.at[n]) for n in range(count)]
    last_copy = pltpu.make_async_copy(mb1, mb1_h, sems.at[count])

    def run(side):
        below, above = (None, on) if side > 0 else (on, None)
        fill_wall(wall, solid, below, above)
        fill_post(p0, post, below, above, depth)
        stream_post(s1, mid, p0, wall, 0, depth)
        first, last = near_layers(side, depth)
        collide_layers(
            first, last, s1, mid, 0, lambda i, out: put_layer(p1, i, mid, out),
            h1, mb1, w1, w2, b_col, herm, lambda n: copies[n].start(),
        )

    by_side(core, run)
    last_copy.start()
    for copy in copies:
        copy.wait()
    last_copy.wait()


def second_kernel(
    core, post, on, off, cot, solid, p1_near, w1, w_in, w2, w_out, b_col, herm, herm_t,
    send_on, send_off, g2, wall_o, h1_h, mb1_h, mb2_h, gb2_h,
    p0, s1, p1, s2, gx, gp2, h1, mb1, mb2, gb2, h2, da2, dm, ways, sems,
):
    moves = Copies(sems)
    send_up, send_dn = ways.at[0], ways.at[1]
    depth, plane = solid.shape
    edge = REACH + 1
    mid = depth + 2 * edge
    some = s1.shape[1] // QP
    wall_ext = wall_o.at[0:mid, :]
    for q in range(Q):
        put_rows(p1, q, mid, 0, get_rows(p1_near, q, mid, 0, mid))

    def run(side):
        below, above = (off, on) if side > 0 else (on, off)
        fill_wall(wall_ext, solid, below, above)
        fill_post(p0, post, below, above, depth)
        base = 0 if side > 0 else mid - some
        stream_post(s1, some, p0, wall_ext, base, depth)
        first, last = far_layers(side, depth)
        collide_layers(
            first, last, s1, some, base, lambda i, out: put_layer(p1, i, mid, out),
            h1, mb1, w1, w2, b_col, herm, lambda n: None,
        )
        for q in range(Q):
            put_rows(gx, q, mid, edge, cot[q * depth : (q + 1) * depth, :] * (1.0 - wall_o[edge : edge + depth, :]))
        fill_single(gx, edge, mid, below, above, depth, REACH * BLOCK + N_REACH, -1, 0)

    by_side(core, run)
    moves.start(h1, h1_h)
    moves.start(mb1, mb1_h)
    wall = wall_o[edge : edge + depth, :]

    for q in range(Q):
        ex, ey, ez = VEL[q]
        moved = roll_plane(get_rows(p1, q, mid, edge - ez, depth), ex, ey)
        bounced = get_rows(p1, OPP[q], mid, edge, depth)
        put_rows(s2, q, depth, 0, jnp.where(wall > 0.5, bounced, moved))
    clear_pad(s2, depth)
    for q in range(Q):
        ex, ey, ez = VEL[q]
        moved = roll_plane(get_rows(gx, q, mid, edge + ez, depth), -ex, -ey)
        at = OPP[q] * depth
        put_rows(gp2, q, depth, 0, moved + wall * cot[at : at + depth, :])
    clear_pad(gp2, depth)

    total = jnp.zeros((QP, plane), F32)
    for z in range(depth):
        mb2[z] = moments_of(get_layer(s2, z, depth), herm[...])
        gp = get_layer(gp2, z, depth)
        gb2[z] = gp.astype(BF)
        total = total + gp
    wall_o[mid : mid + QP, :] = total
    moves.start(mb2, mb2_h)
    moves.start(gb2, gb2_h)

    def hide_two(z):
        hidden_into(h2.at[z], w1, mb2[z])

    def act(z):
        d_act_into(da2.at[z], h2.at[z], w_out, gb2[z])

    def back(z):
        dm[z] = split_concat(dot(w_in[...], da2[z]))

    def finish_two(z):
        g = (get_layer(gp2, z, depth) + dot(herm_t[...], dm[z]))[:Q]
        put_layer(g2, z, depth, g)
        if z < REACH:
            send_dn[z * BLOCK : z * BLOCK + Q, :] = g
        if depth - 1 - z < REACH:
            d = depth - 1 - z
            send_up[d * BLOCK : d * BLOCK + Q, :] = g

    staggered(depth, hide_two, act, back, finish_two)

    for sign, send in ((1, send_up), (-1, send_dn)):
        row = REACH * BLOCK
        for k, q in reaching(-sign):
            z = depth - REACH - k if sign > 0 else REACH + k - 1
            open_cells = 1.0 - wall_o[edge + z : edge + z + 1, :]
            send[row : row + 1, :] = get_rows(g2, q, depth, z, 1) * open_cells
            row += 1
    send_on[...] = ways[core[0]]
    send_off[...] = ways[1 - core[0]]
    moves.wait()


def fill_g2(raw, gx, g2, open_ext, below, above, depth):
    edge = REACH + 1
    mid, ext = depth + 2 * edge, depth + 16
    for q in range(Q):
        put_rows(raw, q, mid, edge, get_rows(g2, q, depth, 0, depth))
    fill_blocks(raw, edge, mid, below, above, depth)
    for q in range(Q):
        put_rows(gx, q, ext, 8 - edge, get_rows(raw, q, mid, 0, mid) * open_ext)
    fill_single(gx, 8, ext, below, above, depth, REACH * BLOCK, -1, REACH)


def stream_g2(target, rows, raw, gx, wall, base, depth):
    edge = REACH + 1
    mid, ext = depth + 2 * edge, depth + 16
    solid = wall[base : base + rows, :]
    for q in range(Q):
        ex, ey, ez = VEL[q]
        moved = roll_plane(get_rows(gx, q, ext, 8 - edge + base + ez, rows), -ex, -ey)
        put_rows(target, q, rows, 0, moved + solid * get_rows(raw, OPP[q], mid, base, rows))
    clear_pad(target, rows)


def adjoint_layers(first, last, depth, gp1, rows, base, raw1, g1, wall, h, mb, acc, gb, da, dm, w_in, w_out, herm_t):
    edge = REACH + 1
    mid = depth + 2 * edge

    def act(n):
        gb[n] = get_layer(gp1, first + n - base, rows).astype(BF)
        d_act_into(da.at[n], h.at[n], w_out, gb[n])

    def back(n):
        dm[n] = split_concat(dot(w_in[...], da[n]))

    def finish(n):
        i = first + n
        g = (get_layer(gp1, i - base, rows) + dot(herm_t[...], dm[n]))[:Q]
        put_layer(raw1, i, mid, g)
        put_layer(g1, i, mid, g * (1.0 - wall[i : i + 1, :]))

    def add(n):
        if edge <= first + n < edge + depth:
            add_sums(acc, mb[n], da.at[n], gb[n], h.at[n])

    staggered(last - first, act, back, finish, add)


def third_near_kernel(
    core, g2, on, wall, w1, w_in, w_out, herm_t,
    mb2_h, gb2_h, mb_near_h, h_near_h, mb_far_h, h_far_h, mb0_h, h0_h,
    raw1, g1, acc, total_o, mb_far, h_far, mb0, h0,
    gx, raw, gp1, gb, da, dm, h2, mb2, gb2, mb_near, h_near, sems,
):
    edge = REACH + 1
    mid = wall.shape[0] - QP
    depth = mid - 2 * edge
    moves = Copies(sems)
    sources = (mb2_h, gb2_h, mb_near_h, h_near_h, mb_far_h, h_far_h, mb0_h, h0_h)
    targets = (mb2, gb2, mb_near, h_near, mb_far, h_far, mb0, h0)
    pairs = list(zip(sources, targets))
    copies = [moves.start(source, target) for source, target in pairs[:2]]
    acc[...] = jnp.zeros(acc.shape, F32)

    def stream(side):
        below, above = (None, on) if side > 0 else (on, None)
        fill_g2(raw, gx, g2, 1.0 - wall[0:mid, :], below, above, depth)
        stream_g2(gp1, mid, raw, gx, wall, 0, depth)

    by_side(core, stream)
    for copy in copies[:2]:
        copy.wait()
    copies += [moves.start(source, target) for source, target in pairs[2:4]]

    def hide(z):
        hidden_into(h2.at[z], w1, mb2[z])

    def act(z):
        d_act_into(da.at[z], h2.at[z], w_out, gb2[z])

    def add(z):
        add_sums(acc, mb2[z], da.at[z], gb2[z], h2.at[z])

    staggered(depth, hide, act, add)
    for copy in copies[2:4]:
        copy.wait()
    copies += [moves.start(source, target) for source, target in pairs[4:]]

    def run(side):
        first, last = near_layers(side, depth)
        total = wall[mid : mid + QP, :]
        for i in range(max(first, edge), min(last, edge + depth)):
            total = total + get_layer(gp1, i, mid)
        total_o[...] = total
        adjoint_layers(
            first, last, depth, gp1, mid, 0, raw1, g1, wall, h_near, mb_near, acc, gb, da, dm,
            w_in, w_out, herm_t,
        )

    by_side(core, run)
    for copy in copies[4:]:
        copy.wait()


def third_kernel(
    core, g2, on, off, wall_i, h1, mb1, h0, mb0, raw_near, g_near, acc_i, total_i, w_in, w_out, herm_t,
    sums, da0_h, gp0_h,
    gx, raw, gp1, g1, raw1, gp0, gb, da, dm, acc, total_s, sems,
):
    moves = Copies(sems)
    plane = wall_i.shape[1]
    mid = wall_i.shape[0] - QP
    edge = REACH + 1
    depth = mid - 2 * edge
    some = gp1.shape[1] // QP
    acc[...] = acc_i[...]
    for q in range(Q):
        put_rows(raw1, q, mid, 0, get_rows(raw_near, q, mid, 0, mid))
        put_rows(g1, q, mid, 0, get_rows(g_near, q, mid, 0, mid))

    def run(side):
        below, above = (off, on) if side > 0 else (on, off)
        fill_g2(raw, gx, g2, 1.0 - wall_i[0:mid, :], below, above, depth)
        base = 0 if side > 0 else mid - some
        stream_g2(gp1, some, raw, gx, wall_i, base, depth)
        first, last = far_layers(side, depth)
        total = total_i[...]
        for i in range(max(first, edge), min(last, edge + depth)):
            total = total + get_layer(gp1, i - base, some)
        total_s[...] = total
        adjoint_layers(
            first, last, depth, gp1, some, base, raw1, g1, wall_i, h1, mb1, acc, gb, da, dm, w_in, w_out, herm_t
        )

    by_side(core, run)
    wall = wall_i[edge : edge + depth, :]
    total = total_s[...]
    for q in range(Q):
        ex, ey, ez = VEL[q]
        moved = roll_plane(get_rows(g1, q, mid, edge + ez, depth), -ex, -ey)
        put_rows(gp0, q, depth, 0, moved + wall * get_rows(raw1, OPP[q], mid, edge, depth))
    clear_pad(gp0, depth)
    moves.start(gp0, gp0_h)
    for z in range(depth):
        total = total + get_layer(gp0, z, depth)

    def act_two(z):
        gb[z] = get_layer(gp0, z, depth).astype(BF)
        d_act_into(da.at[z], h0.at[z], w_out, gb[z])
        moves.start(da.at[z], da0_h.at[z])

    def rest(z):
        del z

    def add_two(z):
        add_sums(acc, mb0[z], da.at[z], gb[z], h0.at[z])

    staggered(depth, act_two, rest, rest, rest, add_two)
    sums[0:24, :] = acc[0:24, :]
    sums[24 : 24 + Q + 1, :] = acc[MP : MP + Q + 1, :]
    line = dot_nt(jnp.ones((8, plane), F32), total, lax.Precision.HIGHEST)
    sums[MOM + 1 : MOM + 2, 0:QP] = line[0:1, :]
    moves.wait()


def field_kernel(after, da0_h, gp0_h, w_in, herm_t, d_field, da0, gp0, out0, dm, sems):
    del after
    depth = da0.shape[0]
    moves = Copies(sems)
    copies = [moves.start(gp0_h, gp0)] + [moves.start(da0_h.at[z], da0.at[z]) for z in range(depth)]

    def back(z):
        copies[z + 1].wait()
        dm[z] = split_concat(dot(w_in[...], da0[z]))

    def finish(z):
        g = (get_layer(gp0, z, depth) + dot(herm_t[...], dm[z]))[:Q]
        put_layer(out0, z, depth, g)

    copies[0].wait()
    staggered(depth, back, finish)
    for q in range(Q):
        d_field[q * depth : (q + 1) * depth, :] = get_rows(out0, q, depth, 0, depth)


def last_kernel(scale, core, mine, other, g_w_in, g_b_in, g_w_out, g_b_out):
    first = core[0] == 0
    low = jnp.where(first, mine[...], other[...]) * scale
    high = jnp.where(first, other[...], mine[...]) * scale
    g_w_in[...] = low[:MOM, :]
    g_b_in[...] = low[MOM : MOM + 1, :]
    g_b_out[...] = low[MOM + 1 : MOM + 2, :Q]
    g_w_out[0:8, :] = low[24:, :]
    g_w_out[8:Q, :] = high[: Q - 8, :]


def call(kernel, outs, scratch, args, flops, limit, smem=(), hbm=()):
    vmem = pl.BlockSpec(memory_space=pltpu.VMEM)
    scalars = pl.BlockSpec(memory_space=pltpu.SMEM)
    hbm_spec = pl.BlockSpec(memory_space=pltpu.HBM)
    return pl.pallas_call(
        kernel,
        out_shape=[
            out[2](out[0], out[1]) if len(out) > 2 else jax.ShapeDtypeStruct(*out) for out in outs
        ],
        in_specs=[
            scalars if n in smem else hbm_spec if n in hbm else vmem for n in range(len(args))
        ],
        out_specs=[hbm_spec if len(out) > 2 else vmem for out in outs],
        scratch_shapes=[
            pltpu.VMEM(shape, kind) if kind != "sem" else pltpu.SemaphoreType.DMA(shape)
            for shape, kind in scratch
        ],
        compiler_params=pltpu.CompilerParams(vmem_limit_bytes=limit * MIB),
        cost_estimate=pl.CostEstimate(flops=flops, bytes_accessed=2000000, transcendentals=0),
    )(*args)


def outside(value):
    return pltpu.with_memory_space_constraint(value, pltpu.HBM)


def factor_stages(space, traj):
    core = 2 if space % 2 == 0 else 1
    rest = space // core
    stride = traj * core
    stages = []
    first = [(1, traj)] if traj > 1 else []
    if rest % 2 == 0 and traj <= 2:
        first.append((stride, 2))
        stride, rest = stride * 2, rest // 2
    if first:
        stages.append(first)
    while rest > 1:
        size = next((f for f in (4, 3, 2) if rest % f == 0), rest)
        stages.append([(stride, size)])
        stride, rest = stride * size, rest // size
    return core, stages


def partners(total, digits):
    shifts = [()]
    for _, size in digits:
        shifts = [s + (k,) for s in shifts for k in range(size)]
    result = []
    order = shifts[1:]
    if len(digits) == 1 and len(order) == 3:
        order = [(k,) for k in [1,3,2]]
    for shift in order:
        pairs = []
        for index in range(total):
            to = index
            for (stride, size), k in zip(digits, shift):
                digit = index // stride % size
                other = digit ^ k if size & (size - 1) == 0 else (digit + k) % size
                to += (other - digit) * stride
            pairs.append((index, to))
        result.append(pairs)
    return result


def per_device(field, solid, cotangent, w_in, b_in, w_out, b_out):
    local, pops, depth, plane = field.shape
    hid = w_in.shape[1]
    space, traj = lax.axis_size("space"), lax.axis_size("traj")
    axes = ("space", "traj")
    chip = [(i, i + 1 - 2 * (i % 2)) for i in range(space)]
    next_chip = [(i, (i - 1 + 2 * (i % 2)) % space) for i in range(space)]
    place = lax.axis_index("space") % 2
    core_id = place.reshape(1).astype(jnp.int32)
    herm, herm_t = hermite_operands()
    edge = REACH + 1
    mid, ext = depth + 2 * edge, depth + 16
    near, far, some = depth, 2 * REACH, 8
    half = plane // 2
    field = field.reshape(pops * depth, plane)
    cot = cotangent.reshape(pops * depth, plane)
    solid = solid.reshape(depth, plane)

    def pops_buf(rows, count=QP):
        return ((2, count * rows, half), F32)

    raw = [w_in, b_in.reshape(1, hid), w_out.T, b_out.reshape(1, pops), herm, field, solid, cot]
    raw = [outside(value) for value in raw]
    send_on, send_off, post, mb0, w1, w2, b_col = call(
        first_kernel,
        [
            ((SEND_ONE, plane), F32),
            ((SEND_ONE, plane), F32),
            pops_buf(depth, Q),
            ((depth, MP, plane), BF, pltpu.HBM),
            ((hid, MP), BF),
            ((QP, hid), BF),
            ((QP, plane), F32),
        ],
        [pops_buf(depth), ((MP, hid), F32), ((QP, hid), F32)]
        + [(value.shape, value.dtype) for value in raw]
        + [((depth, hid, plane), BF), ((depth, MP, plane), BF), ((2, SEND_ONE, plane), F32)]
        + [((len(raw) + 1,), "sem")],
        [core_id] + raw,
        10**9,
        7,
        smem=(0,),
        hbm=range(1, len(raw) + 1),
    )
    on = lax.ppermute(send_on, "space", chip)
    off = lax.ppermute(send_off, "space", next_chip)
    h0, w_in_p, w_out_p = call(
        between_kernel,
        [((depth, hid, plane), BF, pltpu.HBM), ((MP, hid), BF), ((hid, QP), BF)],
        [
            (w_in.shape, BF), (w_out.T.shape, BF), ((depth, MP, plane), BF), ((depth, hid, plane), BF),
            ((MP, hid), F32), ((QP, hid), F32), ((depth + 3,), "sem"),
        ],
        [raw[0], raw[2], outside(mb0), w1],
        10**9,
        4,
        hbm=range(3),
    )
    p1, h_near, mb_near = call(
        near_kernel,
        [pops_buf(mid, Q), ((near, hid, plane), BF, pltpu.HBM), ((near, MP, plane), BF, pltpu.HBM)],
        [
            pops_buf(ext), pops_buf(mid), ((mid, plane), F32),
            ((near, hid, plane), BF), ((near, MP, plane), BF), ((near + 1,), "sem"),
        ],
        [core_id, post, on, solid, w1, w2, b_col, herm],
        10**9,
        6,
        smem=(0,),
    )
    send_on, send_off, g2, wall, h_far, mb_far, mb2, gb2 = call(
        second_kernel,
        [
            ((SEND_TWO, plane), F32),
            ((SEND_TWO, plane), F32),
            pops_buf(depth, Q),
            ((mid + QP, plane), F32),
            ((far, hid, plane), BF, pltpu.HBM),
            ((far, MP, plane), BF, pltpu.HBM),
            ((depth, MP, plane), BF, pltpu.HBM),
            ((depth, QP, plane), BF, pltpu.HBM),
        ],
        [
            pops_buf(ext), pops_buf(some), pops_buf(mid), pops_buf(depth), pops_buf(mid), pops_buf(depth),
            ((far, hid, plane), BF), ((far, MP, plane), BF), ((depth, MP, plane), BF),
            ((depth, QP, plane), BF), ((depth, hid, plane), BF), ((depth, hid, plane), BF),
            ((depth, 3 * MP, plane), BF), ((2, SEND_TWO, plane), F32), ((4,), "sem"),
        ],
        [core_id, post, on, off, cot, solid, p1, w1, w_in_p, w2, w_out_p, b_col, herm, herm_t],
        10**9,
        16,
        smem=(0,),
    )
    on = lax.ppermute(send_on, "space", chip)
    off = lax.ppermute(send_off, "space", next_chip)
    saved = [outside(value) for value in (mb2, gb2, mb_near, h_near, mb_far, h_far, mb0, h0)]
    raw_near, g_near, acc, total_g, mb_far, h_far, mb0, h0 = call(
        third_near_kernel,
        [pops_buf(mid, Q), pops_buf(mid, Q), ((MP + QP, hid), F32), ((QP, plane), F32)]
        + [(value.shape, BF) for value in saved[4:]],
        [
            pops_buf(ext), pops_buf(mid), pops_buf(mid), ((depth, QP, plane), BF),
            ((depth, hid, plane), BF), ((depth, 3 * MP, plane), BF), ((depth, hid, plane), BF),
        ]
        + [(value.shape, BF) for value in saved[:4]]
        + [((len(saved),), "sem")],
        [core_id, g2, on, wall, w1, w_in_p, w_out_p, herm_t] + saved,
        10**9,
        14,
        smem=(0,),
        hbm=range(8, 16),
    )
    sums, da0, gp0 = call(
        third_kernel,
        [((64, hid), F32), ((depth, hid, plane), BF, pltpu.HBM), pops_buf(depth) + (pltpu.HBM,)],
        [
            pops_buf(ext), pops_buf(mid), pops_buf(some), pops_buf(mid), pops_buf(mid), pops_buf(depth),
            ((depth, QP, plane), BF), ((depth, hid, plane), BF), ((depth, 3 * MP, plane), BF),
            ((MP + QP, hid), F32), ((QP, plane), F32), ((depth + 1,), "sem"),
        ],
        [
            core_id, g2, on, off, wall, h_far, mb_far, h0, mb0, raw_near, g_near, acc, total_g,
            w_in_p, w_out_p, herm_t,
        ],
        10**9,
        12,
        smem=(0,),
    )

    core, stages = factor_stages(space, traj)
    total = space * traj
    me = lax.axis_index("space") % core
    swap = partners(total, [(traj, core)])[0]
    rows = sums.shape[0] // 2
    mine = lax.dynamic_slice_in_dim(sums, me * rows, rows, 0)
    other = lax.dynamic_slice_in_dim(sums, (1 - me) * rows, rows, 0)
    mine = mine + lax.ppermute(other, axes, swap)
    for digits in stages:
        moved = [lax.ppermute(mine, axes, pairs) for pairs in partners(total, digits)]
        for value in moved:
            mine = mine + value
        if digits is stages[0]:
            (d_field,) = call(
                field_kernel,
                [((pops * depth, plane), F32)],
                [
                    ((depth, hid, plane), BF), pops_buf(depth), pops_buf(depth),
                    ((depth, 3 * MP, plane), BF), ((depth + 1,), "sem"),
                ],
                [mine, outside(da0), outside(gp0), w_in_p, herm_t],
                10**9,
                6,
                hbm=(1, 2),
            )
    mine, d_field = lax.optimization_barrier((mine, d_field))
    other = lax.ppermute(mine, axes, swap)

    cells = traj * local * space * depth * plane * STEPS
    scale = 1.0 / math.sqrt(float(cells))
    g_w_in, g_b_in, g_w_out, g_b_out = call(
        lambda *refs: last_kernel(scale, *refs),
        [((MOM, hid), F32), ((1, hid), F32), ((pops, hid), F32), ((1, pops), F32)],
        [],
        [core_id, mine, other],
        10**9,
        1,
        smem=(0,),
    )
    return (
        d_field.reshape(local, pops, depth, plane),
        g_w_in,
        g_b_in.reshape(hid),
        g_w_out.T,
        g_b_out.reshape(pops),
    )


def solution(mesh):
    return jax.shard_map(
        per_device,
        mesh=mesh,
        in_specs=(
            P("traj", None, "space", None),
            P("traj", "space", None),
            P("traj", None, "space", None),
            P(),
            P(),
            P(),
            P(),
        ),
        out_specs=(P("traj", None, "space", None), P(), P(), P(), P()),
        check_vma=False,
    )
```

```python
import math

import jax
import jax.numpy as jnp
import numpy as np
from jax import lax
from jax.experimental import pallas as pl
from jax.experimental.pallas import tpu as pltpu
from jax.sharding import PartitionSpec as P

STEPS = 3
NX = 16
NY = 16
Q = 39
QP = 48
MOM = 20
MP = 32
REACH = 3
BLOCK = 40
CHUNK = 128
MIB = 1024 * 1024
BF = jnp.bfloat16
F32 = jnp.float32


def velocity_table():
    rows = [(0, 0, 0)]
    for axis_one in range(3):
        for sign in (1, -1):
            entry = [0, 0, 0]
            entry[axis_one] = sign
            rows.append(tuple(entry))
    for along_x in (1, -1):
        for along_y in (1, -1):
            for along_z in (1, -1):
                rows.append((along_x, along_y, along_z))
    for axis_one in range(3):
        for sign in (1, -1):
            entry = [0, 0, 0]
            entry[axis_one] = 2 * sign
            rows.append(tuple(entry))
    for first, second in ((0, 1), (0, 2), (1, 2)):
        for sign_one in (2, -2):
            for sign_two in (2, -2):
                entry = [0, 0, 0]
                entry[first] = sign_one
                entry[second] = sign_two
                rows.append(tuple(entry))
    for axis_one in range(3):
        for sign in (1, -1):
            entry = [0, 0, 0]
            entry[axis_one] = 3 * sign
            rows.append(tuple(entry))
    return rows


def opposite_index(velocity):
    return [velocity.index((-row[0], -row[1], -row[2])) for row in velocity]


def hermite_table(velocity):
    sound = 2.0 / 3.0
    ident = [[1.0 if a == b else 0.0 for b in range(3)] for a in range(3)]
    speed = [[float(v) for v in row] for row in velocity]
    rows = [[1.0 for row in speed]]
    for first in range(3):
        rows.append([row[first] for row in speed])
    for first in range(3):
        for second in range(first, 3):
            rows.append([row[first] * row[second] - sound * ident[first][second] for row in speed])
    for first in range(3):
        for second in range(first, 3):
            for third in range(second, 3):
                rows.append(
                    [
                        row[first] * row[second] * row[third]
                        - sound
                        * (
                            row[first] * ident[second][third]
                            + row[second] * ident[first][third]
                            + row[third] * ident[first][second]
                        )
                        for row in speed
                    ]
                )
    normed = []
    for values in rows:
        length = math.sqrt(sum((v * v for v in values)))
        normed.append([v / length for v in values])
    return np.asarray(normed, np.float32)


VEL = velocity_table()
OPP = opposite_index(VEL)
HERM = hermite_table(VEL)


def reaching(sign):
    return [(k, q) for k in range(1, REACH + 1) for q in range(Q) if sign * VEL[q][2] >= k]


N_REACH = len(reaching(1))
SEND_ONE = REACH * BLOCK + 2 * N_REACH + REACH + 1
SEND_TWO = REACH * BLOCK + N_REACH + 6


def split_hi_lo(table):
    hi = table.astype(BF)
    lo = (table - np.asarray(hi, np.float32)).astype(BF)
    return hi, lo


def hermite_operands():
    wide = np.zeros((MP, QP), np.float32)
    wide[:MOM, :Q] = HERM
    hi, lo = split_hi_lo(wide)
    forward = np.concatenate([hi, hi, lo], axis=1)
    hi, lo = split_hi_lo(np.ascontiguousarray(wide.T))
    backward = np.concatenate([hi, hi, lo], axis=1)
    return jnp.asarray(forward), jnp.asarray(backward)


def dot(a, b):
    return jnp.dot(a, b, preferred_element_type=F32)


def dot_nt(a, b, precision=None):
    return lax.dot_general(
        a, b, (((1,), (1,)), ((), ())), preferred_element_type=F32, precision=precision
    )


def halves(value):
    lanes = value.shape[1] // 2
    return value[:, :lanes], value[:, lanes:]


def get_layer(buf, layer, stride, count=QP):
    return jnp.concatenate([buf[half, pl.ds(layer, count, stride=stride), :] for half in (0, 1)], axis=1)


def put_layer(buf, layer, stride, value):
    count = value.shape[0]
    for half, part in enumerate(halves(value)):
        buf[half, pl.ds(layer, count, stride=stride), :] = part


def get_rows(buf, q, stride, first, count):
    start = q * stride + first
    return jnp.concatenate([buf[half, start : start + count, :] for half in (0, 1)], axis=1)


def put_rows(buf, q, stride, first, value):
    start = q * stride + first
    for half, part in enumerate(halves(value)):
        buf[half, start : start + value.shape[0], :] = part


def clear_pad(buf, stride):
    lanes = buf.shape[2]
    for half in (0, 1):
        buf[half, Q * stride : QP * stride, :] = jnp.zeros(((QP - Q) * stride, lanes), F32)


def roll_plane(value, along_x, along_y):
    lanes = value.shape[1]
    shift = NY * along_x + along_y

    def turned(by):
        by = by % lanes
        return value if by == 0 else pltpu.roll(value, by, 1)

    if along_y == 0:
        return turned(shift)
    column = lax.broadcasted_iota(jnp.int32, value.shape, 1) % NY
    if along_y > 0:
        return jnp.where(column < along_y, turned(shift - NY), turned(shift))
    return jnp.where(column >= NY + along_y, turned(shift + NY), turned(shift))


def split_concat(value):
    hi = value.astype(BF)
    lo = (value - hi.astype(F32)).astype(BF)
    return jnp.concatenate([hi, lo, hi], axis=0)


def moments_of(x, herm):
    moments = dot(herm, split_concat(x))
    row = lax.broadcasted_iota(jnp.int32, moments.shape, 0)
    ones = jnp.where((row >= MOM) & (row < MOM + 3), 1.0, 0.0)
    return (moments + ones).astype(BF)


def hidden_into(h, w1, mb):
    for start in range(0, w1.shape[0], CHUNK):
        act = dot(w1[start : start + CHUNK, :], mb)
        h[start : start + CHUNK, :] = jnp.tanh(act).astype(BF)


def d_act_into(da, h, w_out, gb):
    for start in range(0, w_out.shape[0], CHUNK):
        d_hidden = dot(w_out[start : start + CHUNK, :], gb)
        hidden = h[start : start + CHUNK, :].astype(F32)
        da[start : start + CHUNK, :] = (d_hidden * (1.0 - hidden * hidden)).astype(BF)


def staggered(count, *stages, beside=()):
    turns = count + len(stages) - 1
    for turn in range(turns):
        for late, stage in enumerate(stages):
            if 0 <= turn - late < count:
                stage(turn - late)
        for work in beside[turn * len(beside) // turns : (turn + 1) * len(beside) // turns]:
            work()


def add_sums(acc, mb, da, gb, h):
    acc[0:MP, :] += dot_nt(mb, da[...])
    acc[MP : MP + QP, :] += dot_nt(gb, h[...])


class Copies:
    def __init__(self, sems):
        self.sems, self.used, self.open = sems, 0, []

    def start(self, source, target):
        copy = pltpu.make_async_copy(source, target, self.sems.at[self.used])
        self.used += 1
        copy.start()
        self.open.append(copy)
        return copy

    def wait(self):
        for copy in self.open:
            copy.wait()
        self.open = []


def first_kernel(
    core, w_in_h, b_in_h, w_out_h, b_out_h, herm_h, field_h, solid_h, cot_h,
    send_on, send_off, post, mb0_h, w1_o, w2_o, b_col_o,
    state, wide, tall, w_in, b_in, w_out, b_out, herm, field, solid, cot, h, mb0, ways, sems,
):
    send_up, send_dn = ways.at[0], ways.at[1]
    sources = (w_in_h, b_in_h, w_out_h, b_out_h, herm_h, field_h, solid_h, cot_h)
    targets = (w_in, b_in, w_out, b_out, herm, field, solid, cot)
    moves = Copies(sems)
    copies = [moves.start(a, b) for a, b in zip(sources, targets)]
    moves.open = []
    depth, plane = solid.shape
    hid = w_in.shape[1]
    for copy in copies[:6]:
        copy.wait()
    wide[...] = jnp.zeros(wide.shape, F32)
    wide[:MOM, :] = w_in[...].astype(F32)
    rest = b_in[...]
    for part in range(3):
        piece = rest.astype(BF).astype(F32)
        wide[MOM + part : MOM + part + 1, :] = piece
        rest = rest - piece
    w1_o[...] = wide[...].T.astype(BF)
    tall[...] = jnp.zeros(tall.shape, F32)
    tall[:Q, :] = w_out[...].astype(F32)
    w2_o[...] = tall[...].astype(BF)
    tall[0:8, :] = jnp.zeros((8, hid), F32)
    tall[0:1, 0:Q] = b_out[...]
    column = tall[0:8, 0:128].T
    b_col_o[...] = jnp.broadcast_to(column[:QP, 0:1], (QP, plane))

    for q in range(Q):
        put_rows(state, q, depth, 0, field[q * depth : (q + 1) * depth, :])
    clear_pad(state, depth)
    for z in range(depth):
        mb0[z] = moments_of(get_layer(state, z, depth), herm[...])
    moves.start(mb0, mb0_h)

    def hide(z):
        hidden_into(h.at[z], w1_o, mb0[z])

    def finish(z):
        out = get_layer(state, z, depth) + dot(w2_o[...], h[z]) + b_col_o[...]
        out = out[:Q]
        put_layer(post, z, depth, out)
        if z < REACH:
            send_dn[z * BLOCK : z * BLOCK + Q, :] = out
        if depth - 1 - z < REACH:
            d = depth - 1 - z
            send_up[d * BLOCK : d * BLOCK + Q, :] = out

    staggered(depth, hide, finish)
    for copy in copies[6:]:
        copy.wait()
    wall = solid[...].astype(F32)
    for sign, send in ((1, send_up), (-1, send_dn)):
        layer = (lambda d: depth - d) if sign > 0 else (lambda d: d - 1)
        row = REACH * BLOCK
        for k, q in reaching(sign):
            send[row : row + 1, :] = get_rows(post, q, depth, layer(REACH + k), 1)
            row += 1
        for k, q in reaching(-sign):
            z = layer(k)
            at = q * depth + z
            send[row : row + 1, :] = cot[at : at + 1, :] * (1.0 - wall[z : z + 1, :])
            row += 1
        for d in range(1, REACH + 1):
            send[row : row + 1, :] = wall[layer(d) : layer(d) + 1, :]
            row += 1
    send_on[...] = ways[core[0]]
    send_off[...] = ways[1 - core[0]]
    moves.wait()


def between_kernel(
    w_in_h, w_out_h, mb0_h, w1, h0_h, w_in_o, w_out_o, w_in, w_out, mb0, h0, wide, tall, sems
):
    moves = Copies(sems)
    copies = [moves.start(a, b) for a, b in ((mb0_h, mb0), (w_in_h, w_in), (w_out_h, w_out))]
    moves.open = []
    copies[0].wait()
    for z in range(mb0.shape[0]):
        hidden_into(h0.at[z], w1, mb0[z])
        moves.start(h0.at[z], h0_h.at[z])
    for copy in copies[1:]:
        copy.wait()
    wide[...] = jnp.zeros(wide.shape, F32)
    wide[:MOM, :] = w_in[...].astype(F32)
    w_in_o[...] = wide[...].astype(BF)
    tall[...] = jnp.zeros(tall.shape, F32)
    tall[:Q, :] = w_out[...].astype(F32)
    w_out_o[...] = tall[...].T.astype(BF)
    moves.wait()


def by_side(core, run):
    for place, side in ((0, 1), (1, -1)):
        pl.when(core[0] == place)(lambda side=side: run(side))


def near_layers(side, depth):
    edge = REACH + 1
    return (edge + REACH, 2 * edge + depth - 1) if side > 0 else (1, edge + depth - REACH)


def far_layers(side, depth):
    edge = REACH + 1
    return (1, edge + REACH) if side > 0 else (edge + depth - REACH, 2 * edge + depth - 1)


def fill_wall(wall, solid, below, above):
    depth = solid.shape[0]
    edge = REACH + 1
    wall[...] = jnp.zeros(wall.shape, F32)
    wall[edge : edge + depth, :] = solid[...].astype(F32)
    row = REACH * BLOCK + 2 * N_REACH
    for d in range(1, REACH + 1):
        if below is not None:
            wall[edge - d : edge - d + 1, :] = below[row + d - 1 : row + d, :]
        if above is not None:
            wall[edge + depth + d - 1 : edge + depth + d, :] = above[row + d - 1 : row + d, :]


def fill_blocks(buf, zero_row, stride, below, above, depth):
    for d in range(1, REACH + 1):
        rows = slice((d - 1) * BLOCK, (d - 1) * BLOCK + Q)
        if below is not None:
            put_layer(buf, zero_row - d, stride, below[rows, :])
        if above is not None:
            put_layer(buf, zero_row + depth - 1 + d, stride, above[rows, :])


def fill_single(buf, zero_row, stride, below, above, depth, row, sign, beyond):
    if below is not None:
        for n, (k, q) in enumerate(reaching(sign)):
            put_rows(buf, q, stride, zero_row - beyond - k, below[row + n : row + n + 1, :])
    if above is not None:
        for n, (k, q) in enumerate(reaching(-sign)):
            put_rows(buf, q, stride, zero_row + depth - 1 + beyond + k, above[row + n : row + n + 1, :])


def fill_post(p0, post, below, above, depth):
    ext = depth + 16
    for q in range(Q):
        put_rows(p0, q, ext, 8, get_rows(post, q, depth, 0, depth))
    fill_blocks(p0, 8, ext, below, above, depth)
    fill_single(p0, 8, ext, below, above, depth, REACH * BLOCK, 1, REACH)


def stream_post(target, rows, p0, wall, base, depth):
    ext = depth + 16
    start = 8 - REACH - 1 + base
    solid = wall[base : base + rows, :] > 0.5
    for q in range(Q):
        ex, ey, ez = VEL[q]
        moved = roll_plane(get_rows(p0, q, ext, start - ez, rows), ex, ey)
        bounced = get_rows(p0, OPP[q], ext, start, rows)
        put_rows(target, q, rows, 0, jnp.where(solid, bounced, moved))
    clear_pad(target, rows)


def collide_layers(first, last, s1, rows, base, p1, h1, mb1, w1, w2, b_col, herm, after, beside=()):
    def moments(n):
        mb1[n] = moments_of(get_layer(s1, first + n - base, rows), herm[...])

    def hide(n):
        hidden_into(h1.at[n], w1, mb1[n])
        after(n)

    def finish(n):
        out = get_layer(s1, first + n - base, rows) + dot(w2[...], h1[n]) + b_col[...]
        p1(first + n, out[:Q])

    staggered(last - first, moments, hide, finish, beside=beside)


def near_kernel(
    core, post, on, solid, w1, w2, b_col, herm,
    p1, h1_h, mb1_h,
    p0, s1, wall, h1, mb1, sems,
):
    depth = solid.shape[0]
    mid = depth + 2 * REACH + 2
    count = h1.shape[0]
    copies = [pltpu.make_async_copy(h1.at[n], h1_h.at[n], sems.at[n]) for n in range(count)]
    last_copy = pltpu.make_async_copy(mb1, mb1_h, sems.at[count])

    def run(side):
        below, above = (None, on) if side > 0 else (on, None)
        fill_wall(wall, solid, below, above)
        fill_post(p0, post, below, above, depth)
        stream_post(s1, mid, p0, wall, 0, depth)
        first, last = near_layers(side, depth)
        collide_layers(
            first, last, s1, mid, 0, lambda i, out: put_layer(p1, i, mid, out),
            h1, mb1, w1, w2, b_col, herm, lambda n: copies[n].start(),
        )

    by_side(core, run)
    last_copy.start()
    for copy in copies:
        copy.wait()
    last_copy.wait()


def second_kernel(
    core, post, on, off, cot, solid, p1_near, w1, w_in, w2, w_out, b_col, herm, herm_t,
    send_on, send_off, g2, wall_o, h1_h, mb1_h, mb2_h, gb2_h,
    p0, s1, p1, s2, gx, gp2, h1, mb1, mb2, gb2, h2, da2, dm, ways, sems,
):
    moves = Copies(sems)
    send_up, send_dn = ways.at[0], ways.at[1]
    depth, plane = solid.shape
    edge = REACH + 1
    mid = depth + 2 * edge
    some = s1.shape[1] // QP
    wall_ext = wall_o.at[0:mid, :]
    for q in range(Q):
        put_rows(p1, q, mid, 0, get_rows(p1_near, q, mid, 0, mid))

    def gpost(q):
        ex, ey, ez = VEL[q]
        wall = wall_o[edge : edge + depth, :]
        put_rows(gx, q, mid, edge, cot[q * depth : (q + 1) * depth, :] * (1.0 - wall))
        moved = roll_plane(get_rows(gx, q, mid, edge + ez, depth), -ex, -ey)
        at = OPP[q] * depth
        put_rows(gp2, q, depth, 0, moved + wall * cot[at : at + depth, :])

    clear_pad(gp2, depth)

    def run(side):
        below, above = (off, on) if side > 0 else (on, off)
        fill_wall(wall_ext, solid, below, above)
        fill_post(p0, post, below, above, depth)
        base = 0 if side > 0 else mid - some
        stream_post(s1, some, p0, wall_ext, base, depth)
        fill_single(gx, edge, mid, below, above, depth, REACH * BLOCK + N_REACH, -1, 0)
        first, last = far_layers(side, depth)
        collide_layers(
            first, last, s1, some, base, lambda i, out: put_layer(p1, i, mid, out),
            h1, mb1, w1, w2, b_col, herm, lambda n: None, [lambda q=q: gpost(q) for q in range(Q)],
        )

    by_side(core, run)
    moves.start(h1, h1_h)
    moves.start(mb1, mb1_h)
    wall = wall_o[edge : edge + depth, :]

    for q in range(Q):
        ex, ey, ez = VEL[q]
        moved = roll_plane(get_rows(p1, q, mid, edge - ez, depth), ex, ey)
        bounced = get_rows(p1, OPP[q], mid, edge, depth)
        put_rows(s2, q, depth, 0, jnp.where(wall > 0.5, bounced, moved))
    clear_pad(s2, depth)

    total = jnp.zeros((QP, plane), F32)
    for z in range(depth):
        mb2[z] = moments_of(get_layer(s2, z, depth), herm[...])
        gp = get_layer(gp2, z, depth)
        gb2[z] = gp.astype(BF)
        total = total + gp
    wall_o[mid : mid + QP, :] = total
    moves.start(mb2, mb2_h)
    moves.start(gb2, gb2_h)

    def hide_two(z):
        hidden_into(h2.at[z], w1, mb2[z])

    def act(z):
        d_act_into(da2.at[z], h2.at[z], w_out, gb2[z])

    def back(z):
        dm[z] = split_concat(dot(w_in[...], da2[z]))

    def finish_two(z):
        g = (get_layer(gp2, z, depth) + dot(herm_t[...], dm[z]))[:Q]
        put_layer(g2, z, depth, g)
        if z < REACH:
            send_dn[z * BLOCK : z * BLOCK + Q, :] = g
        if depth - 1 - z < REACH:
            d = depth - 1 - z
            send_up[d * BLOCK : d * BLOCK + Q, :] = g

    staggered(depth, hide_two, act, back, finish_two)

    for sign, send in ((1, send_up), (-1, send_dn)):
        row = REACH * BLOCK
        for k, q in reaching(-sign):
            z = depth - REACH - k if sign > 0 else REACH + k - 1
            open_cells = 1.0 - wall_o[edge + z : edge + z + 1, :]
            send[row : row + 1, :] = get_rows(g2, q, depth, z, 1) * open_cells
            row += 1
    send_on[...] = ways[core[0]]
    send_off[...] = ways[1 - core[0]]
    moves.wait()


def fill_g2(raw, gx, g2, open_ext, below, above, depth):
    edge = REACH + 1
    mid, ext = depth + 2 * edge, depth + 16
    for q in range(Q):
        put_rows(raw, q, mid, edge, get_rows(g2, q, depth, 0, depth))
    fill_blocks(raw, edge, mid, below, above, depth)
    for q in range(Q):
        put_rows(gx, q, ext, 8 - edge, get_rows(raw, q, mid, 0, mid) * open_ext)
    fill_single(gx, 8, ext, below, above, depth, REACH * BLOCK, -1, REACH)


def stream_g2(target, rows, raw, gx, wall, base, depth):
    edge = REACH + 1
    mid, ext = depth + 2 * edge, depth + 16
    solid = wall[base : base + rows, :]
    for q in range(Q):
        ex, ey, ez = VEL[q]
        moved = roll_plane(get_rows(gx, q, ext, 8 - edge + base + ez, rows), -ex, -ey)
        put_rows(target, q, rows, 0, moved + solid * get_rows(raw, OPP[q], mid, base, rows))
    clear_pad(target, rows)


def adjoint_layers(first, last, depth, gp1, rows, base, raw1, g1, wall, h, mb, acc, gb, da, dm, w_in, w_out, herm_t):
    edge = REACH + 1
    mid = depth + 2 * edge

    def act(n):
        gb[n] = get_layer(gp1, first + n - base, rows).astype(BF)
        d_act_into(da.at[n], h.at[n], w_out, gb[n])

    def back(n):
        dm[n] = split_concat(dot(w_in[...], da[n]))

    def finish(n):
        i = first + n
        g = (get_layer(gp1, i - base, rows) + dot(herm_t[...], dm[n]))[:Q]
        put_layer(raw1, i, mid, g)
        put_layer(g1, i, mid, g * (1.0 - wall[i : i + 1, :]))

    def add(n):
        if edge <= first + n < edge + depth:
            add_sums(acc, mb[n], da.at[n], gb[n], h.at[n])

    staggered(last - first, act, back, finish, add)


def third_near_kernel(
    core, g2, on, wall, w1, w_in, w_out, herm_t,
    mb2_h, gb2_h, mb_near_h, h_near_h, mb_far_h, h_far_h, mb0_h, h0_h,
    raw1, g1, acc, total_o, mb_far, h_far, mb0, h0,
    gx, raw, gp1, gb, da, dm, h2, mb2, gb2, mb_near, h_near, sems,
):
    edge = REACH + 1
    mid = wall.shape[0] - QP
    depth = mid - 2 * edge
    moves = Copies(sems)
    sources = (mb2_h, gb2_h, mb_near_h, h_near_h, mb_far_h, h_far_h, mb0_h, h0_h)
    targets = (mb2, gb2, mb_near, h_near, mb_far, h_far, mb0, h0)
    pairs = list(zip(sources, targets))
    copies = [moves.start(source, target) for source, target in pairs[:2]]
    acc[...] = jnp.zeros(acc.shape, F32)

    def stream(side):
        below, above = (None, on) if side > 0 else (on, None)
        fill_g2(raw, gx, g2, 1.0 - wall[0:mid, :], below, above, depth)
        stream_g2(gp1, mid, raw, gx, wall, 0, depth)

    by_side(core, stream)
    for copy in copies[:2]:
        copy.wait()
    copies += [moves.start(source, target) for source, target in pairs[2:4]]

    def hide(z):
        hidden_into(h2.at[z], w1, mb2[z])

    def act(z):
        d_act_into(da.at[z], h2.at[z], w_out, gb2[z])

    def add(z):
        add_sums(acc, mb2[z], da.at[z], gb2[z], h2.at[z])

    staggered(depth, hide, act, add)
    for copy in copies[2:4]:
        copy.wait()
    copies += [moves.start(source, target) for source, target in pairs[4:]]

    def run(side):
        first, last = near_layers(side, depth)
        total = wall[mid : mid + QP, :]
        for i in range(max(first, edge), min(last, edge + depth)):
            total = total + get_layer(gp1, i, mid)
        total_o[...] = total
        adjoint_layers(
            first, last, depth, gp1, mid, 0, raw1, g1, wall, h_near, mb_near, acc, gb, da, dm,
            w_in, w_out, herm_t,
        )

    by_side(core, run)
    for copy in copies[4:]:
        copy.wait()


def third_kernel(
    core, g2, on, off, wall_i, h1, mb1, h0, mb0, raw_near, g_near, acc_i, total_i, w_in, w_out, herm_t,
    sums, da0_h, gp0_h,
    gx, raw, gp1, g1, raw1, gp0, gb, da, dm, acc, total_s, sems,
):
    moves = Copies(sems)
    plane = wall_i.shape[1]
    mid = wall_i.shape[0] - QP
    edge = REACH + 1
    depth = mid - 2 * edge
    some = gp1.shape[1] // QP
    acc[...] = acc_i[...]
    for q in range(Q):
        put_rows(raw1, q, mid, 0, get_rows(raw_near, q, mid, 0, mid))
        put_rows(g1, q, mid, 0, get_rows(g_near, q, mid, 0, mid))

    def run(side):
        below, above = (off, on) if side > 0 else (on, off)
        fill_g2(raw, gx, g2, 1.0 - wall_i[0:mid, :], below, above, depth)
        base = 0 if side > 0 else mid - some
        stream_g2(gp1, some, raw, gx, wall_i, base, depth)
        first, last = far_layers(side, depth)
        total = total_i[...]
        for i in range(max(first, edge), min(last, edge + depth)):
            total = total + get_layer(gp1, i - base, some)
        total_s[...] = total
        adjoint_layers(
            first, last, depth, gp1, some, base, raw1, g1, wall_i, h1, mb1, acc, gb, da, dm, w_in, w_out, herm_t
        )

    by_side(core, run)
    wall = wall_i[edge : edge + depth, :]
    total = total_s[...]
    for q in range(Q):
        ex, ey, ez = VEL[q]
        moved = roll_plane(get_rows(g1, q, mid, edge + ez, depth), -ex, -ey)
        put_rows(gp0, q, depth, 0, moved + wall * get_rows(raw1, OPP[q], mid, edge, depth))
    clear_pad(gp0, depth)
    moves.start(gp0, gp0_h)
    for z in range(depth):
        total = total + get_layer(gp0, z, depth)

    def act_two(z):
        gb[z] = get_layer(gp0, z, depth).astype(BF)
        d_act_into(da.at[z], h0.at[z], w_out, gb[z])
        moves.start(da.at[z], da0_h.at[z])

    def rest(z):
        del z

    def add_two(z):
        add_sums(acc, mb0[z], da.at[z], gb[z], h0.at[z])

    staggered(depth, act_two, rest, rest, rest, add_two)
    sums[0:24, :] = acc[0:24, :]
    sums[24 : 24 + Q + 1, :] = acc[MP : MP + Q + 1, :]
    line = dot_nt(jnp.ones((8, plane), F32), total, lax.Precision.HIGHEST)
    sums[MOM + 1 : MOM + 2, 0:QP] = line[0:1, :]
    moves.wait()


def field_kernel(after, da0_h, gp0_h, w_in, herm_t, d_field, da0, gp0, out0, dm, sems):
    del after
    depth = da0.shape[0]
    moves = Copies(sems)
    copies = [moves.start(gp0_h, gp0)] + [moves.start(da0_h.at[z], da0.at[z]) for z in range(depth)]

    def back(z):
        copies[z + 1].wait()
        dm[z] = split_concat(dot(w_in[...], da0[z]))

    def finish(z):
        g = (get_layer(gp0, z, depth) + dot(herm_t[...], dm[z]))[:Q]
        put_layer(out0, z, depth, g)

    copies[0].wait()
    staggered(depth, back, finish)
    for q in range(Q):
        d_field[q * depth : (q + 1) * depth, :] = get_rows(out0, q, depth, 0, depth)


def last_kernel(scale, core, mine, other, g_w_in, g_b_in, g_w_out, g_b_out):
    first = core[0] == 0
    low = jnp.where(first, mine[...], other[...]) * scale
    high = jnp.where(first, other[...], mine[...]) * scale
    g_w_in[...] = low[:MOM, :]
    g_b_in[...] = low[MOM : MOM + 1, :]
    g_b_out[...] = low[MOM + 1 : MOM + 2, :Q]
    g_w_out[0:8, :] = low[24:, :]
    g_w_out[8:Q, :] = high[: Q - 8, :]


def call(kernel, outs, scratch, args, flops, limit, smem=(), hbm=()):
    vmem = pl.BlockSpec(memory_space=pltpu.VMEM)
    scalars = pl.BlockSpec(memory_space=pltpu.SMEM)
    hbm_spec = pl.BlockSpec(memory_space=pltpu.HBM)
    return pl.pallas_call(
        kernel,
        out_shape=[
            out[2](out[0], out[1]) if len(out) > 2 else jax.ShapeDtypeStruct(*out) for out in outs
        ],
        in_specs=[
            scalars if n in smem else hbm_spec if n in hbm else vmem for n in range(len(args))
        ],
        out_specs=[hbm_spec if len(out) > 2 else vmem for out in outs],
        scratch_shapes=[
            pltpu.VMEM(shape, kind) if kind != "sem" else pltpu.SemaphoreType.DMA(shape)
            for shape, kind in scratch
        ],
        compiler_params=pltpu.CompilerParams(vmem_limit_bytes=limit * MIB),
        cost_estimate=pl.CostEstimate(flops=flops, bytes_accessed=2000000, transcendentals=0),
    )(*args)


def outside(value):
    return pltpu.with_memory_space_constraint(value, pltpu.HBM)


def factor_stages(space, traj):
    core = 2 if space % 2 == 0 else 1
    rest = space // core
    stride = traj * core
    stages = []
    first = [(1, traj)] if traj > 1 else []
    if rest % 2 == 0 and traj <= 2:
        first.append((stride, 2))
        stride, rest = stride * 2, rest // 2
    if first:
        stages.append(first)
    while rest > 1:
        size = next((f for f in (4, 3, 2) if rest % f == 0), rest)
        stages.append([(stride, size)])
        stride, rest = stride * size, rest // size
    return core, stages


def partners(total, digits):
    shifts = [()]
    for _, size in digits:
        shifts = [s + (k,) for s in shifts for k in range(size)]
    result = []
    order = shifts[1:]
    if len(digits) == 1 and len(order) == 3:
        order = [(k,) for k in [1,3,2]]
    for shift in order:
        pairs = []
        for index in range(total):
            to = index
            for (stride, size), k in zip(digits, shift):
                digit = index // stride % size
                other = digit ^ k if size & (size - 1) == 0 else (digit + k) % size
                to += (other - digit) * stride
            pairs.append((index, to))
        result.append(pairs)
    return result


def per_device(field, solid, cotangent, w_in, b_in, w_out, b_out):
    local, pops, depth, plane = field.shape
    hid = w_in.shape[1]
    space, traj = lax.axis_size("space"), lax.axis_size("traj")
    axes = ("space", "traj")
    chip = [(i, i + 1 - 2 * (i % 2)) for i in range(space)]
    next_chip = [(i, (i - 1 + 2 * (i % 2)) % space) for i in range(space)]
    place = lax.axis_index("space") % 2
    core_id = place.reshape(1).astype(jnp.int32)
    herm, herm_t = hermite_operands()
    edge = REACH + 1
    mid, ext = depth + 2 * edge, depth + 16
    near, far, some = depth, 2 * REACH, 8
    half = plane // 2
    field = field.reshape(pops * depth, plane)
    cot = cotangent.reshape(pops * depth, plane)
    solid = solid.reshape(depth, plane)

    def pops_buf(rows, count=QP):
        return ((2, count * rows, half), F32)

    raw = [w_in, b_in.reshape(1, hid), w_out.T, b_out.reshape(1, pops), herm, field, solid, cot]
    raw = [outside(value) for value in raw]
    send_on, send_off, post, mb0, w1, w2, b_col = call(
        first_kernel,
        [
            ((SEND_ONE, plane), F32),
            ((SEND_ONE, plane), F32),
            pops_buf(depth, Q),
            ((depth, MP, plane), BF, pltpu.HBM),
            ((hid, MP), BF),
            ((QP, hid), BF),
            ((QP, plane), F32),
        ],
        [pops_buf(depth), ((MP, hid), F32), ((QP, hid), F32)]
        + [(value.shape, value.dtype) for value in raw]
        + [((depth, hid, plane), BF), ((depth, MP, plane), BF), ((2, SEND_ONE, plane), F32)]
        + [((len(raw) + 1,), "sem")],
        [core_id] + raw,
        10**9,
        7,
        smem=(0,),
        hbm=range(1, len(raw) + 1),
    )
    on = lax.ppermute(send_on, "space", chip)
    off = lax.ppermute(send_off, "space", next_chip)
    h0, w_in_p, w_out_p = call(
        between_kernel,
        [((depth, hid, plane), BF, pltpu.HBM), ((MP, hid), BF), ((hid, QP), BF)],
        [
            (w_in.shape, BF), (w_out.T.shape, BF), ((depth, MP, plane), BF), ((depth, hid, plane), BF),
            ((MP, hid), F32), ((QP, hid), F32), ((depth + 3,), "sem"),
        ],
        [raw[0], raw[2], outside(mb0), w1],
        10**9,
        4,
        hbm=range(3),
    )
    p1, h_near, mb_near = call(
        near_kernel,
        [pops_buf(mid, Q), ((near, hid, plane), BF, pltpu.HBM), ((near, MP, plane), BF, pltpu.HBM)],
        [
            pops_buf(ext), pops_buf(mid), ((mid, plane), F32),
            ((near, hid, plane), BF), ((near, MP, plane), BF), ((near + 1,), "sem"),
        ],
        [core_id, post, on, solid, w1, w2, b_col, herm],
        10**9,
        6,
        smem=(0,),
    )
    send_on, send_off, g2, wall, h_far, mb_far, mb2, gb2 = call(
        second_kernel,
        [
            ((SEND_TWO, plane), F32),
            ((SEND_TWO, plane), F32),
            pops_buf(depth, Q),
            ((mid + QP, plane), F32),
            ((far, hid, plane), BF, pltpu.HBM),
            ((far, MP, plane), BF, pltpu.HBM),
            ((depth, MP, plane), BF, pltpu.HBM),
            ((depth, QP, plane), BF, pltpu.HBM),
        ],
        [
            pops_buf(ext), pops_buf(some), pops_buf(mid), pops_buf(depth), pops_buf(mid), pops_buf(depth),
            ((far, hid, plane), BF), ((far, MP, plane), BF), ((depth, MP, plane), BF),
            ((depth, QP, plane), BF), ((depth, hid, plane), BF), ((depth, hid, plane), BF),
            ((depth, 3 * MP, plane), BF), ((2, SEND_TWO, plane), F32), ((4,), "sem"),
        ],
        [core_id, post, on, off, cot, solid, p1, w1, w_in_p, w2, w_out_p, b_col, herm, herm_t],
        10**9,
        16,
        smem=(0,),
    )
    on = lax.ppermute(send_on, "space", chip)
    off = lax.ppermute(send_off, "space", next_chip)
    saved = [outside(value) for value in (mb2, gb2, mb_near, h_near, mb_far, h_far, mb0, h0)]
    raw_near, g_near, acc, total_g, mb_far, h_far, mb0, h0 = call(
        third_near_kernel,
        [pops_buf(mid, Q), pops_buf(mid, Q), ((MP + QP, hid), F32), ((QP, plane), F32)]
        + [(value.shape, BF) for value in saved[4:]],
        [
            pops_buf(ext), pops_buf(mid), pops_buf(mid), ((depth, QP, plane), BF),
            ((depth, hid, plane), BF), ((depth, 3 * MP, plane), BF), ((depth, hid, plane), BF),
        ]
        + [(value.shape, BF) for value in saved[:4]]
        + [((len(saved),), "sem")],
        [core_id, g2, on, wall, w1, w_in_p, w_out_p, herm_t] + saved,
        10**9,
        14,
        smem=(0,),
        hbm=range(8, 16),
    )
    sums, da0, gp0 = call(
        third_kernel,
        [((64, hid), F32), ((depth, hid, plane), BF, pltpu.HBM), pops_buf(depth) + (pltpu.HBM,)],
        [
            pops_buf(ext), pops_buf(mid), pops_buf(some), pops_buf(mid), pops_buf(mid), pops_buf(depth),
            ((depth, QP, plane), BF), ((depth, hid, plane), BF), ((depth, 3 * MP, plane), BF),
            ((MP + QP, hid), F32), ((QP, plane), F32), ((depth + 1,), "sem"),
        ],
        [
            core_id, g2, on, off, wall, h_far, mb_far, h0, mb0, raw_near, g_near, acc, total_g,
            w_in_p, w_out_p, herm_t,
        ],
        10**9,
        12,
        smem=(0,),
    )

    core, stages = factor_stages(space, traj)
    total = space * traj
    me = lax.axis_index("space") % core
    swap = partners(total, [(traj, core)])[0]
    rows = sums.shape[0] // 2
    mine = lax.dynamic_slice_in_dim(sums, me * rows, rows, 0)
    other = lax.dynamic_slice_in_dim(sums, (1 - me) * rows, rows, 0)
    mine = mine + lax.ppermute(other, axes, swap)
    for digits in stages:
        moved = [lax.ppermute(mine, axes, pairs) for pairs in partners(total, digits)]
        for value in moved:
            mine = mine + value
        if digits is stages[0]:
            (d_field,) = call(
                field_kernel,
                [((pops * depth, plane), F32)],
                [
                    ((depth, hid, plane), BF), pops_buf(depth), pops_buf(depth),
                    ((depth, 3 * MP, plane), BF), ((depth + 1,), "sem"),
                ],
                [mine, outside(da0), outside(gp0), w_in_p, herm_t],
                10**9,
                6,
                hbm=(1, 2),
            )
    mine, d_field = lax.optimization_barrier((mine, d_field))
    other = lax.ppermute(mine, axes, swap)

    cells = traj * local * space * depth * plane * STEPS
    scale = 1.0 / math.sqrt(float(cells))
    g_w_in, g_b_in, g_w_out, g_b_out = call(
        lambda *refs: last_kernel(scale, *refs),
        [((MOM, hid), F32), ((1, hid), F32), ((pops, hid), F32), ((1, pops), F32)],
        [],
        [core_id, mine, other],
        10**9,
        1,
        smem=(0,),
    )
    return (
        d_field.reshape(local, pops, depth, plane),
        g_w_in,
        g_b_in.reshape(hid),
        g_w_out.T,
        g_b_out.reshape(pops),
    )


def solution(mesh):
    return jax.shard_map(
        per_device,
        mesh=mesh,
        in_specs=(
            P("traj", None, "space", None),
            P("traj", "space", None),
            P("traj", None, "space", None),
            P(),
            P(),
            P(),
            P(),
        ),
        out_specs=(P("traj", None, "space", None), P(), P(), P(), P()),
        check_vma=False,
    )
```

```python
import math

import jax
import jax.numpy as jnp
import numpy as np
from jax import lax
from jax.experimental import pallas as pl
from jax.experimental.pallas import tpu as pltpu
from jax.sharding import PartitionSpec as P

STEPS = 3
NX = 16
NY = 16
Q = 39
QP = 48
MOM = 20
MP = 32
REACH = 3
BLOCK = 40
CHUNK = 128
MIB = 1024 * 1024
BF = jnp.bfloat16
F32 = jnp.float32


def velocity_table():
    rows = [(0, 0, 0)]
    for axis_one in range(3):
        for sign in (1, -1):
            entry = [0, 0, 0]
            entry[axis_one] = sign
            rows.append(tuple(entry))
    for along_x in (1, -1):
        for along_y in (1, -1):
            for along_z in (1, -1):
                rows.append((along_x, along_y, along_z))
    for axis_one in range(3):
        for sign in (1, -1):
            entry = [0, 0, 0]
            entry[axis_one] = 2 * sign
            rows.append(tuple(entry))
    for first, second in ((0, 1), (0, 2), (1, 2)):
        for sign_one in (2, -2):
            for sign_two in (2, -2):
                entry = [0, 0, 0]
                entry[first] = sign_one
                entry[second] = sign_two
                rows.append(tuple(entry))
    for axis_one in range(3):
        for sign in (1, -1):
            entry = [0, 0, 0]
            entry[axis_one] = 3 * sign
            rows.append(tuple(entry))
    return rows


def opposite_index(velocity):
    return [velocity.index((-row[0], -row[1], -row[2])) for row in velocity]


def hermite_table(velocity):
    sound = 2.0 / 3.0
    ident = [[1.0 if a == b else 0.0 for b in range(3)] for a in range(3)]
    speed = [[float(v) for v in row] for row in velocity]
    rows = [[1.0 for row in speed]]
    for first in range(3):
        rows.append([row[first] for row in speed])
    for first in range(3):
        for second in range(first, 3):
            rows.append([row[first] * row[second] - sound * ident[first][second] for row in speed])
    for first in range(3):
        for second in range(first, 3):
            for third in range(second, 3):
                rows.append(
                    [
                        row[first] * row[second] * row[third]
                        - sound
                        * (
                            row[first] * ident[second][third]
                            + row[second] * ident[first][third]
                            + row[third] * ident[first][second]
                        )
                        for row in speed
                    ]
                )
    normed = []
    for values in rows:
        length = math.sqrt(sum((v * v for v in values)))
        normed.append([v / length for v in values])
    return np.asarray(normed, np.float32)


VEL = velocity_table()
OPP = opposite_index(VEL)
HERM = hermite_table(VEL)


def reaching(sign):
    return [(k, q) for k in range(1, REACH + 1) for q in range(Q) if sign * VEL[q][2] >= k]


N_REACH = len(reaching(1))
SEND_ONE = REACH * BLOCK + 2 * N_REACH + REACH + 1
SEND_TWO = REACH * BLOCK + N_REACH + 6


def split_hi_lo(table):
    hi = table.astype(BF)
    lo = (table - np.asarray(hi, np.float32)).astype(BF)
    return hi, lo


def hermite_operands():
    wide = np.zeros((MP, QP), np.float32)
    wide[:MOM, :Q] = HERM
    hi, lo = split_hi_lo(wide)
    forward = np.concatenate([hi, hi, lo], axis=1)
    hi, lo = split_hi_lo(np.ascontiguousarray(wide.T))
    backward = np.concatenate([hi, hi, lo], axis=1)
    return jnp.asarray(forward), jnp.asarray(backward)


def dot(a, b):
    return jnp.dot(a, b, preferred_element_type=F32)


def dot_nt(a, b, precision=None):
    return lax.dot_general(
        a, b, (((1,), (1,)), ((), ())), preferred_element_type=F32, precision=precision
    )


def halves(value):
    lanes = value.shape[1] // 2
    return value[:, :lanes], value[:, lanes:]


def get_layer(buf, layer, stride, count=QP):
    return jnp.concatenate([buf[half, pl.ds(layer, count, stride=stride), :] for half in (0, 1)], axis=1)


def put_layer(buf, layer, stride, value):
    count = value.shape[0]
    for half, part in enumerate(halves(value)):
        buf[half, pl.ds(layer, count, stride=stride), :] = part


def get_rows(buf, q, stride, first, count):
    start = q * stride + first
    return jnp.concatenate([buf[half, start : start + count, :] for half in (0, 1)], axis=1)


def put_rows(buf, q, stride, first, value):
    start = q * stride + first
    for half, part in enumerate(halves(value)):
        buf[half, start : start + value.shape[0], :] = part


def clear_pad(buf, stride):
    lanes = buf.shape[2]
    for half in (0, 1):
        buf[half, Q * stride : QP * stride, :] = jnp.zeros(((QP - Q) * stride, lanes), F32)


def roll_plane(value, along_x, along_y):
    lanes = value.shape[1]
    shift = NY * along_x + along_y

    def turned(by):
        by = by % lanes
        return value if by == 0 else pltpu.roll(value, by, 1)

    if along_y == 0:
        return turned(shift)
    column = lax.broadcasted_iota(jnp.int32, value.shape, 1) % NY
    if along_y > 0:
        return jnp.where(column < along_y, turned(shift - NY), turned(shift))
    return jnp.where(column >= NY + along_y, turned(shift + NY), turned(shift))


def split_concat(value):
    hi = value.astype(BF)
    lo = (value - hi.astype(F32)).astype(BF)
    return jnp.concatenate([hi, lo, hi], axis=0)


def moments_of(x, herm):
    moments = dot(herm, split_concat(x))
    row = lax.broadcasted_iota(jnp.int32, moments.shape, 0)
    ones = jnp.where((row >= MOM) & (row < MOM + 3), 1.0, 0.0)
    return (moments + ones).astype(BF)


def hidden_into(h, w1, mb):
    for start in range(0, w1.shape[0], CHUNK):
        act = dot(w1[start : start + CHUNK, :], mb)
        h[start : start + CHUNK, :] = jnp.tanh(act).astype(BF)


def d_act_into(da, h, w_out, gb):
    for start in range(0, w_out.shape[0], CHUNK):
        d_hidden = dot(w_out[start : start + CHUNK, :], gb)
        hidden = h[start : start + CHUNK, :].astype(F32)
        da[start : start + CHUNK, :] = (d_hidden * (1.0 - hidden * hidden)).astype(BF)


def staggered(count, *stages, beside=()):
    turns = count + len(stages) - 1
    for turn in range(turns):
        for late, stage in enumerate(stages):
            if 0 <= turn - late < count:
                stage(turn - late)
        for work in beside[turn * len(beside) // turns : (turn + 1) * len(beside) // turns]:
            work()


def add_sums(acc, mb, da, gb, h):
    acc[0:MP, :] += dot_nt(mb, da[...])
    acc[MP : MP + QP, :] += dot_nt(gb, h[...])


class Copies:
    def __init__(self, sems):
        self.sems, self.used, self.open = sems, 0, []

    def start(self, source, target):
        copy = pltpu.make_async_copy(source, target, self.sems.at[self.used])
        self.used += 1
        copy.start()
        self.open.append(copy)
        return copy

    def wait(self):
        for copy in self.open:
            copy.wait()
        self.open = []


def first_kernel(
    core, w_in_h, b_in_h, w_out_h, b_out_h, herm_h, field_h, solid_h, cot_h,
    send_on, send_off, post, mb0_h, w1_o, w2_o, b_col_o,
    state, wide, tall, w_in, b_in, w_out, b_out, herm, field, solid, cot, h, mb0, ways, sems,
):
    send_up, send_dn = ways.at[0], ways.at[1]
    sources = (w_in_h, b_in_h, w_out_h, b_out_h, herm_h, field_h, solid_h, cot_h)
    targets = (w_in, b_in, w_out, b_out, herm, field, solid, cot)
    moves = Copies(sems)
    copies = [moves.start(a, b) for a, b in zip(sources, targets)]
    moves.open = []
    depth, plane = solid.shape
    hid = w_in.shape[1]
    for copy in copies[:6]:
        copy.wait()
    wide[...] = jnp.zeros(wide.shape, F32)
    wide[:MOM, :] = w_in[...].astype(F32)
    rest = b_in[...]
    for part in range(3):
        piece = rest.astype(BF).astype(F32)
        wide[MOM + part : MOM + part + 1, :] = piece
        rest = rest - piece
    w1_o[...] = wide[...].T.astype(BF)
    tall[...] = jnp.zeros(tall.shape, F32)
    tall[:Q, :] = w_out[...].astype(F32)
    w2_o[...] = tall[...].astype(BF)
    tall[0:8, :] = jnp.zeros((8, hid), F32)
    tall[0:1, 0:Q] = b_out[...]
    column = tall[0:8, 0:128].T
    b_col_o[...] = jnp.broadcast_to(column[:QP, 0:1], (QP, plane))

    for q in range(Q):
        put_rows(state, q, depth, 0, field[q * depth : (q + 1) * depth, :])
    clear_pad(state, depth)
    for z in range(depth):
        mb0[z] = moments_of(get_layer(state, z, depth), herm[...])
    moves.start(mb0, mb0_h)

    def hide(z):
        hidden_into(h.at[z], w1_o, mb0[z])

    def finish(z):
        out = get_layer(state, z, depth) + dot(w2_o[...], h[z]) + b_col_o[...]
        out = out[:Q]
        put_layer(post, z, depth, out)
        if z < REACH:
            send_dn[z * BLOCK : z * BLOCK + Q, :] = out
        if depth - 1 - z < REACH:
            d = depth - 1 - z
            send_up[d * BLOCK : d * BLOCK + Q, :] = out

    staggered(depth, hide, finish)
    for copy in copies[6:]:
        copy.wait()
    wall = solid[...].astype(F32)
    for sign, send in ((1, send_up), (-1, send_dn)):
        layer = (lambda d: depth - d) if sign > 0 else (lambda d: d - 1)
        row = REACH * BLOCK
        for k, q in reaching(sign):
            send[row : row + 1, :] = get_rows(post, q, depth, layer(REACH + k), 1)
            row += 1
        for k, q in reaching(-sign):
            z = layer(k)
            at = q * depth + z
            send[row : row + 1, :] = cot[at : at + 1, :] * (1.0 - wall[z : z + 1, :])
            row += 1
        for d in range(1, REACH + 1):
            send[row : row + 1, :] = wall[layer(d) : layer(d) + 1, :]
            row += 1
    send_on[...] = ways[core[0]]
    send_off[...] = ways[1 - core[0]]
    moves.wait()


def between_kernel(
    w_in_h, w_out_h, mb0_h, w1, h0_h, w_in_o, w_out_o, w_in, w_out, mb0, h0, wide, tall, sems
):
    moves = Copies(sems)
    copies = [moves.start(a, b) for a, b in ((mb0_h, mb0), (w_in_h, w_in), (w_out_h, w_out))]
    moves.open = []
    copies[0].wait()
    for z in range(mb0.shape[0]):
        hidden_into(h0.at[z], w1, mb0[z])
        moves.start(h0.at[z], h0_h.at[z])
    for copy in copies[1:]:
        copy.wait()
    wide[...] = jnp.zeros(wide.shape, F32)
    wide[:MOM, :] = w_in[...].astype(F32)
    w_in_o[...] = wide[...].astype(BF)
    tall[...] = jnp.zeros(tall.shape, F32)
    tall[:Q, :] = w_out[...].astype(F32)
    w_out_o[...] = tall[...].T.astype(BF)
    moves.wait()


def by_side(core, run):
    for place, side in ((0, 1), (1, -1)):
        pl.when(core[0] == place)(lambda side=side: run(side))


def near_layers(side, depth):
    edge = REACH + 1
    return (edge + REACH, 2 * edge + depth - 1) if side > 0 else (1, edge + depth - REACH)


def far_layers(side, depth):
    edge = REACH + 1
    return (1, edge + REACH) if side > 0 else (edge + depth - REACH, 2 * edge + depth - 1)


def fill_wall(wall, solid, below, above):
    depth = solid.shape[0]
    edge = REACH + 1
    wall[...] = jnp.zeros(wall.shape, F32)
    wall[edge : edge + depth, :] = solid[...].astype(F32)
    row = REACH * BLOCK + 2 * N_REACH
    for d in range(1, REACH + 1):
        if below is not None:
            wall[edge - d : edge - d + 1, :] = below[row + d - 1 : row + d, :]
        if above is not None:
            wall[edge + depth + d - 1 : edge + depth + d, :] = above[row + d - 1 : row + d, :]


def fill_blocks(buf, zero_row, stride, below, above, depth):
    for d in range(1, REACH + 1):
        rows = slice((d - 1) * BLOCK, (d - 1) * BLOCK + Q)
        if below is not None:
            put_layer(buf, zero_row - d, stride, below[rows, :])
        if above is not None:
            put_layer(buf, zero_row + depth - 1 + d, stride, above[rows, :])


def fill_single(buf, zero_row, stride, below, above, depth, row, sign, beyond):
    if below is not None:
        for n, (k, q) in enumerate(reaching(sign)):
            put_rows(buf, q, stride, zero_row - beyond - k, below[row + n : row + n + 1, :])
    if above is not None:
        for n, (k, q) in enumerate(reaching(-sign)):
            put_rows(buf, q, stride, zero_row + depth - 1 + beyond + k, above[row + n : row + n + 1, :])


def fill_post(p0, post, below, above, depth):
    ext = depth + 16
    for q in range(Q):
        put_rows(p0, q, ext, 8, get_rows(post, q, depth, 0, depth))
    fill_blocks(p0, 8, ext, below, above, depth)
    fill_single(p0, 8, ext, below, above, depth, REACH * BLOCK, 1, REACH)


def stream_post(target, rows, p0, wall, base, depth):
    ext = depth + 16
    start = 8 - REACH - 1 + base
    solid = wall[base : base + rows, :] > 0.5
    for q in range(Q):
        ex, ey, ez = VEL[q]
        moved = roll_plane(get_rows(p0, q, ext, start - ez, rows), ex, ey)
        bounced = get_rows(p0, OPP[q], ext, start, rows)
        put_rows(target, q, rows, 0, jnp.where(solid, bounced, moved))
    clear_pad(target, rows)


def collide_layers(first, last, s1, rows, base, p1, h1, mb1, w1, w2, b_col, herm, after, beside=()):
    def moments(n):
        mb1[n] = moments_of(get_layer(s1, first + n - base, rows), herm[...])

    def hide(n):
        hidden_into(h1.at[n], w1, mb1[n])
        after(n)

    def finish(n):
        out = get_layer(s1, first + n - base, rows) + dot(w2[...], h1[n]) + b_col[...]
        p1(first + n, out[:Q])

    staggered(last - first, moments, hide, finish, beside=beside)


def near_kernel(
    core, post, on, solid, w1, w2, b_col, herm,
    p1, h1_h, mb1_h,
    p0, s1, wall, h1, mb1, sems,
):
    depth = solid.shape[0]
    mid = depth + 2 * REACH + 2
    count = h1.shape[0]
    copies = [pltpu.make_async_copy(h1.at[n], h1_h.at[n], sems.at[n]) for n in range(count)]
    last_copy = pltpu.make_async_copy(mb1, mb1_h, sems.at[count])

    def run(side):
        below, above = (None, on) if side > 0 else (on, None)
        fill_wall(wall, solid, below, above)
        fill_post(p0, post, below, above, depth)
        stream_post(s1, mid, p0, wall, 0, depth)
        first, last = near_layers(side, depth)
        collide_layers(
            first, last, s1, mid, 0, lambda i, out: put_layer(p1, i, mid, out),
            h1, mb1, w1, w2, b_col, herm, lambda n: copies[n].start(),
        )

    by_side(core, run)
    last_copy.start()
    for copy in copies:
        copy.wait()
    last_copy.wait()


def second_kernel(
    core, post, on, off, cot, solid, p1_near, w1, w_in, w2, w_out, b_col, herm, herm_t,
    send_on, send_off, g2, wall_o, h1_h, mb1_h, mb2_h, gb2_h,
    p0, s1, p1, s2, gx, gp2, h1, mb1, mb2, gb2, h2, da2, dm, ways, sems,
):
    moves = Copies(sems)
    send_up, send_dn = ways.at[0], ways.at[1]
    depth, plane = solid.shape
    edge = REACH + 1
    mid = depth + 2 * edge
    some = s1.shape[1] // QP
    wall_ext = wall_o.at[0:mid, :]
    for q in range(Q):
        put_rows(p1, q, mid, 0, get_rows(p1_near, q, mid, 0, mid))

    def gpost(q):
        ex, ey, ez = VEL[q]
        wall = wall_o[edge : edge + depth, :]
        put_rows(gx, q, mid, edge, cot[q * depth : (q + 1) * depth, :] * (1.0 - wall))
        moved = roll_plane(get_rows(gx, q, mid, edge + ez, depth), -ex, -ey)
        at = OPP[q] * depth
        put_rows(gp2, q, depth, 0, moved + wall * cot[at : at + depth, :])

    clear_pad(gp2, depth)

    def run(side):
        below, above = (off, on) if side > 0 else (on, off)
        fill_wall(wall_ext, solid, below, above)
        fill_post(p0, post, below, above, depth)
        base = 0 if side > 0 else mid - some
        stream_post(s1, some, p0, wall_ext, base, depth)
        fill_single(gx, edge, mid, below, above, depth, REACH * BLOCK + N_REACH, -1, 0)
        first, last = far_layers(side, depth)
        collide_layers(
            first, last, s1, some, base, lambda i, out: put_layer(p1, i, mid, out),
            h1, mb1, w1, w2, b_col, herm, lambda n: None, [lambda q=q: gpost(q) for q in range(Q)],
        )

    by_side(core, run)
    moves.start(h1, h1_h)
    moves.start(mb1, mb1_h)
    wall = wall_o[edge : edge + depth, :]

    for q in range(Q):
        ex, ey, ez = VEL[q]
        moved = roll_plane(get_rows(p1, q, mid, edge - ez, depth), ex, ey)
        bounced = get_rows(p1, OPP[q], mid, edge, depth)
        put_rows(s2, q, depth, 0, jnp.where(wall > 0.5, bounced, moved))
    clear_pad(s2, depth)

    total = jnp.zeros((QP, plane), F32)
    for z in range(depth):
        mb2[z] = moments_of(get_layer(s2, z, depth), herm[...])
        gp = get_layer(gp2, z, depth)
        gb2[z] = gp.astype(BF)
        total = total + gp
    wall_o[mid : mid + QP, :] = total
    moves.start(mb2, mb2_h)
    moves.start(gb2, gb2_h)

    def hide_two(z):
        hidden_into(h2.at[z], w1, mb2[z])

    def act(z):
        d_act_into(da2.at[z], h2.at[z], w_out, gb2[z])

    def back(z):
        dm[z] = split_concat(dot(w_in[...], da2[z]))

    def finish_two(z):
        g = (get_layer(gp2, z, depth) + dot(herm_t[...], dm[z]))[:Q]
        put_layer(g2, z, depth, g)
        if z < REACH:
            send_dn[z * BLOCK : z * BLOCK + Q, :] = g
        if depth - 1 - z < REACH:
            d = depth - 1 - z
            send_up[d * BLOCK : d * BLOCK + Q, :] = g

    staggered(depth, hide_two, act, back, finish_two)

    for sign, send in ((1, send_up), (-1, send_dn)):
        row = REACH * BLOCK
        for k, q in reaching(-sign):
            z = depth - REACH - k if sign > 0 else REACH + k - 1
            open_cells = 1.0 - wall_o[edge + z : edge + z + 1, :]
            send[row : row + 1, :] = get_rows(g2, q, depth, z, 1) * open_cells
            row += 1
    send_on[...] = ways[core[0]]
    send_off[...] = ways[1 - core[0]]
    moves.wait()


def fill_g2(raw, gx, g2, open_ext, below, above, depth):
    edge = REACH + 1
    mid, ext = depth + 2 * edge, depth + 16
    for q in range(Q):
        put_rows(raw, q, mid, edge, get_rows(g2, q, depth, 0, depth))
    fill_blocks(raw, edge, mid, below, above, depth)
    for q in range(Q):
        put_rows(gx, q, ext, 8 - edge, get_rows(raw, q, mid, 0, mid) * open_ext)
    fill_single(gx, 8, ext, below, above, depth, REACH * BLOCK, -1, REACH)


def stream_g2(target, rows, raw, gx, wall, base, depth):
    edge = REACH + 1
    mid, ext = depth + 2 * edge, depth + 16
    solid = wall[base : base + rows, :]
    for q in range(Q):
        ex, ey, ez = VEL[q]
        moved = roll_plane(get_rows(gx, q, ext, 8 - edge + base + ez, rows), -ex, -ey)
        put_rows(target, q, rows, 0, moved + solid * get_rows(raw, OPP[q], mid, base, rows))
    clear_pad(target, rows)


def adjoint_layers(first, last, depth, gp1, rows, base, raw1, g1, wall, h, mb, acc, gb, da, dm, w_in, w_out, herm_t):
    edge = REACH + 1
    mid = depth + 2 * edge

    def act(n):
        gb[n] = get_layer(gp1, first + n - base, rows).astype(BF)
        d_act_into(da.at[n], h.at[n], w_out, gb[n])

    def back(n):
        dm[n] = split_concat(dot(w_in[...], da[n]))

    def finish(n):
        i = first + n
        g = (get_layer(gp1, i - base, rows) + dot(herm_t[...], dm[n]))[:Q]
        put_layer(raw1, i, mid, g)
        put_layer(g1, i, mid, g * (1.0 - wall[i : i + 1, :]))

    def add(n):
        if edge <= first + n < edge + depth:
            add_sums(acc, mb[n], da.at[n], gb[n], h.at[n])

    staggered(last - first, act, lambda n: None, back, finish, add)


def third_near_kernel(
    core, g2, on, wall, w1, w_in, w_out, herm_t,
    mb2_h, gb2_h, mb_near_h, h_near_h, mb_far_h, h_far_h, mb0_h, h0_h,
    raw1, g1, acc, total_o, mb_far, h_far, mb0, h0,
    gx, raw, gp1, gb, da, dm, h2, mb2, gb2, mb_near, h_near, sems,
):
    edge = REACH + 1
    mid = wall.shape[0] - QP
    depth = mid - 2 * edge
    moves = Copies(sems)
    sources = (mb2_h, gb2_h, mb_near_h, h_near_h, mb_far_h, h_far_h, mb0_h, h0_h)
    targets = (mb2, gb2, mb_near, h_near, mb_far, h_far, mb0, h0)
    pairs = list(zip(sources, targets))
    copies = [moves.start(source, target) for source, target in pairs[:4]]
    acc[...] = jnp.zeros(acc.shape, F32)

    def stream(side):
        below, above = (None, on) if side > 0 else (on, None)
        fill_g2(raw, gx, g2, 1.0 - wall[0:mid, :], below, above, depth)
        stream_g2(gp1, mid, raw, gx, wall, 0, depth)

    by_side(core, stream)
    for copy in copies[:2]:
        copy.wait()
    copies += [moves.start(source, target) for source, target in pairs[4:]]

    def hide(z):
        hidden_into(h2.at[z], w1, mb2[z])

    def act(z):
        d_act_into(da.at[z], h2.at[z], w_out, gb2[z])

    def add(z):
        add_sums(acc, mb2[z], da.at[z], gb2[z], h2.at[z])

    staggered(depth, hide, act, add)
    for copy in copies[2:4]:
        copy.wait()

    def run(side):
        first, last = near_layers(side, depth)
        total = wall[mid : mid + QP, :]
        for i in range(max(first, edge), min(last, edge + depth)):
            total = total + get_layer(gp1, i, mid)
        total_o[...] = total
        adjoint_layers(
            first, last, depth, gp1, mid, 0, raw1, g1, wall, h_near, mb_near, acc, gb, da, dm,
            w_in, w_out, herm_t,
        )

    by_side(core, run)
    for copy in copies[4:]:
        copy.wait()


def third_kernel(
    core, g2, on, off, wall_i, h1, mb1, h0, mb0, raw_near, g_near, acc_i, total_i, w_in, w_out, herm_t,
    sums, da0_h, gp0_h,
    gx, raw, gp1, g1, raw1, gp0, gb, da, dm, acc, total_s, sems,
):
    moves = Copies(sems)
    plane = wall_i.shape[1]
    mid = wall_i.shape[0] - QP
    edge = REACH + 1
    depth = mid - 2 * edge
    some = gp1.shape[1] // QP
    acc[...] = acc_i[...]
    for q in range(Q):
        put_rows(raw1, q, mid, 0, get_rows(raw_near, q, mid, 0, mid))
        put_rows(g1, q, mid, 0, get_rows(g_near, q, mid, 0, mid))

    def run(side):
        below, above = (off, on) if side > 0 else (on, off)
        fill_g2(raw, gx, g2, 1.0 - wall_i[0:mid, :], below, above, depth)
        base = 0 if side > 0 else mid - some
        stream_g2(gp1, some, raw, gx, wall_i, base, depth)
        first, last = far_layers(side, depth)
        total = total_i[...]
        for i in range(max(first, edge), min(last, edge + depth)):
            total = total + get_layer(gp1, i - base, some)
        total_s[...] = total
        adjoint_layers(
            first, last, depth, gp1, some, base, raw1, g1, wall_i, h1, mb1, acc, gb, da, dm, w_in, w_out, herm_t
        )

    by_side(core, run)
    wall = wall_i[edge : edge + depth, :]
    total = total_s[...]
    for q in range(Q):
        ex, ey, ez = VEL[q]
        moved = roll_plane(get_rows(g1, q, mid, edge + ez, depth), -ex, -ey)
        put_rows(gp0, q, depth, 0, moved + wall * get_rows(raw1, OPP[q], mid, edge, depth))
    clear_pad(gp0, depth)
    moves.start(gp0, gp0_h)
    for z in range(depth):
        total = total + get_layer(gp0, z, depth)

    def act_two(z):
        gb[z] = get_layer(gp0, z, depth).astype(BF)
        d_act_into(da.at[z], h0.at[z], w_out, gb[z])
        moves.start(da.at[z], da0_h.at[z])

    def rest(z):
        del z

    def add_two(z):
        add_sums(acc, mb0[z], da.at[z], gb[z], h0.at[z])

    staggered(depth, act_two, rest, rest, rest, add_two)
    sums[0:24, :] = acc[0:24, :]
    sums[24 : 24 + Q + 1, :] = acc[MP : MP + Q + 1, :]
    line = dot_nt(jnp.ones((8, plane), F32), total, lax.Precision.HIGHEST)
    sums[MOM + 1 : MOM + 2, 0:QP] = line[0:1, :]
    moves.wait()


def field_kernel(after, da0_h, gp0_h, w_in, herm_t, d_field, da0, gp0, out0, dm, sems):
    del after
    depth = da0.shape[0]
    moves = Copies(sems)
    copies = [moves.start(gp0_h, gp0)] + [moves.start(da0_h.at[z], da0.at[z]) for z in range(depth)]

    def back(z):
        copies[z + 1].wait()
        dm[z] = split_concat(dot(w_in[...], da0[z]))

    def finish(z):
        g = (get_layer(gp0, z, depth) + dot(herm_t[...], dm[z]))[:Q]
        put_layer(out0, z, depth, g)

    copies[0].wait()
    staggered(depth, back, finish)
    for q in range(Q):
        d_field[q * depth : (q + 1) * depth, :] = get_rows(out0, q, depth, 0, depth)


def last_kernel(scale, core, mine, other, g_w_in, g_b_in, g_w_out, g_b_out):
    first = core[0] == 0
    low = jnp.where(first, mine[...], other[...]) * scale
    high = jnp.where(first, other[...], mine[...]) * scale
    g_w_in[...] = low[:MOM, :]
    g_b_in[...] = low[MOM : MOM + 1, :]
    g_b_out[...] = low[MOM + 1 : MOM + 2, :Q]
    g_w_out[0:8, :] = low[24:, :]
    g_w_out[8:Q, :] = high[: Q - 8, :]


def call(kernel, outs, scratch, args, flops, limit, smem=(), hbm=()):
    vmem = pl.BlockSpec(memory_space=pltpu.VMEM)
    scalars = pl.BlockSpec(memory_space=pltpu.SMEM)
    hbm_spec = pl.BlockSpec(memory_space=pltpu.HBM)
    return pl.pallas_call(
        kernel,
        out_shape=[
            out[2](out[0], out[1]) if len(out) > 2 else jax.ShapeDtypeStruct(*out) for out in outs
        ],
        in_specs=[
            scalars if n in smem else hbm_spec if n in hbm else vmem for n in range(len(args))
        ],
        out_specs=[hbm_spec if len(out) > 2 else vmem for out in outs],
        scratch_shapes=[
            pltpu.VMEM(shape, kind) if kind != "sem" else pltpu.SemaphoreType.DMA(shape)
            for shape, kind in scratch
        ],
        compiler_params=pltpu.CompilerParams(vmem_limit_bytes=limit * MIB),
        cost_estimate=pl.CostEstimate(flops=flops, bytes_accessed=2000000, transcendentals=0),
    )(*args)


def outside(value):
    return pltpu.with_memory_space_constraint(value, pltpu.HBM)


def factor_stages(space, traj):
    core = 2 if space % 2 == 0 else 1
    rest = space // core
    stride = traj * core
    stages = []
    first = [(1, traj)] if traj > 1 else []
    if rest % 2 == 0 and traj <= 2:
        first.append((stride, 2))
        stride, rest = stride * 2, rest // 2
    if first:
        stages.append(first)
    while rest > 1:
        size = next((f for f in (4, 3, 2) if rest % f == 0), rest)
        stages.append([(stride, size)])
        stride, rest = stride * size, rest // size
    return core, stages


def partners(total, digits):
    shifts = [()]
    for _, size in digits:
        shifts = [s + (k,) for s in shifts for k in range(size)]
    result = []
    order = shifts[1:]
    if len(digits) == 1 and len(order) == 3:
        order = [(k,) for k in [1,3,2]]
    for shift in order:
        pairs = []
        for index in range(total):
            to = index
            for (stride, size), k in zip(digits, shift):
                digit = index // stride % size
                other = digit ^ k if size & (size - 1) == 0 else (digit + k) % size
                to += (other - digit) * stride
            pairs.append((index, to))
        result.append(pairs)
    return result


def per_device(field, solid, cotangent, w_in, b_in, w_out, b_out):
    local, pops, depth, plane = field.shape
    hid = w_in.shape[1]
    space, traj = lax.axis_size("space"), lax.axis_size("traj")
    axes = ("space", "traj")
    chip = [(i, i + 1 - 2 * (i % 2)) for i in range(space)]
    next_chip = [(i, (i - 1 + 2 * (i % 2)) % space) for i in range(space)]
    place = lax.axis_index("space") % 2
    core_id = place.reshape(1).astype(jnp.int32)
    herm, herm_t = hermite_operands()
    edge = REACH + 1
    mid, ext = depth + 2 * edge, depth + 16
    near, far, some = depth, 2 * REACH, 8
    half = plane // 2
    field = field.reshape(pops * depth, plane)
    cot = cotangent.reshape(pops * depth, plane)
    solid = solid.reshape(depth, plane)

    def pops_buf(rows, count=QP):
        return ((2, count * rows, half), F32)

    raw = [w_in, b_in.reshape(1, hid), w_out.T, b_out.reshape(1, pops), herm, field, solid, cot]
    raw = [outside(value) for value in raw]
    send_on, send_off, post, mb0, w1, w2, b_col = call(
        first_kernel,
        [
            ((SEND_ONE, plane), F32),
            ((SEND_ONE, plane), F32),
            pops_buf(depth, Q),
            ((depth, MP, plane), BF, pltpu.HBM),
            ((hid, MP), BF),
            ((QP, hid), BF),
            ((QP, plane), F32),
        ],
        [pops_buf(depth), ((MP, hid), F32), ((QP, hid), F32)]
        + [(value.shape, value.dtype) for value in raw]
        + [((depth, hid, plane), BF), ((depth, MP, plane), BF), ((2, SEND_ONE, plane), F32)]
        + [((len(raw) + 1,), "sem")],
        [core_id] + raw,
        10**9,
        7,
        smem=(0,),
        hbm=range(1, len(raw) + 1),
    )
    on = lax.ppermute(send_on, "space", chip)
    off = lax.ppermute(send_off, "space", next_chip)
    h0, w_in_p, w_out_p = call(
        between_kernel,
        [((depth, hid, plane), BF, pltpu.HBM), ((MP, hid), BF), ((hid, QP), BF)],
        [
            (w_in.shape, BF), (w_out.T.shape, BF), ((depth, MP, plane), BF), ((depth, hid, plane), BF),
            ((MP, hid), F32), ((QP, hid), F32), ((depth + 3,), "sem"),
        ],
        [raw[0], raw[2], outside(mb0), w1],
        10**9,
        4,
        hbm=range(3),
    )
    p1, h_near, mb_near = call(
        near_kernel,
        [pops_buf(mid, Q), ((near, hid, plane), BF, pltpu.HBM), ((near, MP, plane), BF, pltpu.HBM)],
        [
            pops_buf(ext), pops_buf(mid), ((mid, plane), F32),
            ((near, hid, plane), BF), ((near, MP, plane), BF), ((near + 1,), "sem"),
        ],
        [core_id, post, on, solid, w1, w2, b_col, herm],
        10**9,
        6,
        smem=(0,),
    )
    send_on, send_off, g2, wall, h_far, mb_far, mb2, gb2 = call(
        second_kernel,
        [
            ((SEND_TWO, plane), F32),
            ((SEND_TWO, plane), F32),
            pops_buf(depth, Q),
            ((mid + QP, plane), F32),
            ((far, hid, plane), BF, pltpu.HBM),
            ((far, MP, plane), BF, pltpu.HBM),
            ((depth, MP, plane), BF, pltpu.HBM),
            ((depth, QP, plane), BF, pltpu.HBM),
        ],
        [
            pops_buf(ext), pops_buf(some), pops_buf(mid), pops_buf(depth), pops_buf(mid), pops_buf(depth),
            ((far, hid, plane), BF), ((far, MP, plane), BF), ((depth, MP, plane), BF),
            ((depth, QP, plane), BF), ((depth, hid, plane), BF), ((depth, hid, plane), BF),
            ((depth, 3 * MP, plane), BF), ((2, SEND_TWO, plane), F32), ((4,), "sem"),
        ],
        [core_id, post, on, off, cot, solid, p1, w1, w_in_p, w2, w_out_p, b_col, herm, herm_t],
        10**9,
        16,
        smem=(0,),
    )
    on = lax.ppermute(send_on, "space", chip)
    off = lax.ppermute(send_off, "space", next_chip)
    saved = [outside(value) for value in (mb2, gb2, mb_near, h_near, mb_far, h_far, mb0, h0)]
    raw_near, g_near, acc, total_g, mb_far, h_far, mb0, h0 = call(
        third_near_kernel,
        [pops_buf(mid, Q), pops_buf(mid, Q), ((MP + QP, hid), F32), ((QP, plane), F32)]
        + [(value.shape, BF) for value in saved[4:]],
        [
            pops_buf(ext), pops_buf(mid), pops_buf(mid), ((depth, QP, plane), BF),
            ((depth, hid, plane), BF), ((depth, 3 * MP, plane), BF), ((depth, hid, plane), BF),
        ]
        + [(value.shape, BF) for value in saved[:4]]
        + [((len(saved),), "sem")],
        [core_id, g2, on, wall, w1, w_in_p, w_out_p, herm_t] + saved,
        10**9,
        14,
        smem=(0,),
        hbm=range(8, 16),
    )
    sums, da0, gp0 = call(
        third_kernel,
        [((64, hid), F32), ((depth, hid, plane), BF, pltpu.HBM), pops_buf(depth) + (pltpu.HBM,)],
        [
            pops_buf(ext), pops_buf(mid), pops_buf(some), pops_buf(mid), pops_buf(mid), pops_buf(depth),
            ((depth, QP, plane), BF), ((depth, hid, plane), BF), ((depth, 3 * MP, plane), BF),
            ((MP + QP, hid), F32), ((QP, plane), F32), ((depth + 1,), "sem"),
        ],
        [
            core_id, g2, on, off, wall, h_far, mb_far, h0, mb0, raw_near, g_near, acc, total_g,
            w_in_p, w_out_p, herm_t,
        ],
        10**9,
        12,
        smem=(0,),
    )

    core, stages = factor_stages(space, traj)
    total = space * traj
    me = lax.axis_index("space") % core
    swap = partners(total, [(traj, core)])[0]
    rows = sums.shape[0] // 2
    mine = lax.dynamic_slice_in_dim(sums, me * rows, rows, 0)
    other = lax.dynamic_slice_in_dim(sums, (1 - me) * rows, rows, 0)
    mine = mine + lax.ppermute(other, axes, swap)
    for digits in stages:
        moved = [lax.ppermute(mine, axes, pairs) for pairs in partners(total, digits)]
        for value in moved:
            mine = mine + value
        if digits is stages[0]:
            (d_field,) = call(
                field_kernel,
                [((pops * depth, plane), F32)],
                [
                    ((depth, hid, plane), BF), pops_buf(depth), pops_buf(depth),
                    ((depth, 3 * MP, plane), BF), ((depth + 1,), "sem"),
                ],
                [mine, outside(da0), outside(gp0), w_in_p, herm_t],
                10**9,
                6,
                hbm=(1, 2),
            )
    mine, d_field = lax.optimization_barrier((mine, d_field))
    other = lax.ppermute(mine, axes, swap)

    cells = traj * local * space * depth * plane * STEPS
    scale = 1.0 / math.sqrt(float(cells))
    g_w_in, g_b_in, g_w_out, g_b_out = call(
        lambda *refs: last_kernel(scale, *refs),
        [((MOM, hid), F32), ((1, hid), F32), ((pops, hid), F32), ((1, pops), F32)],
        [],
        [core_id, mine, other],
        10**9,
        1,
        smem=(0,),
    )
    return (
        d_field.reshape(local, pops, depth, plane),
        g_w_in,
        g_b_in.reshape(hid),
        g_w_out.T,
        g_b_out.reshape(pops),
    )


def solution(mesh):
    return jax.shard_map(
        per_device,
        mesh=mesh,
        in_specs=(
            P("traj", None, "space", None),
            P("traj", "space", None),
            P("traj", None, "space", None),
            P(),
            P(),
            P(),
            P(),
        ),
        out_specs=(P("traj", None, "space", None), P(), P(), P(), P()),
        check_vma=False,
    )
```
